256 devices in a mesh: section: 2 (over core), tensor: 32 (over z, y), dp: 4 (over x).
Axes of the slice: x: 4, y: 4, z: 8, core: 2. Of those that a mesh axis runs over, the one named last changes fastest.
Arguments:
- hidden: bfloat16 [1024, 4096], P(('section', 'dp'), 'tensor'), may hold values from -500 to 500
- norm_gain: float32 [4096], P('tensor'), may hold values from 0.5 to 1.5
- head_weight: bfloat16 [131072, 4096], P(('section', 'tensor', 'dp')), may hold values from -1 to 1
- targets: int32 [1024], P(('section', 'dp')), may hold values from 0 to 131071
- span_starts: int32 [1024], P(('section', 'dp')), may hold values from 0 to 1
- live_rows: int32 [1024], P(('section', 'dp')), may hold values from 0 to 1, as said below
Outputs:
- hidden_grad: bfloat16 [1024, 4096], P(('section', 'dp'), 'tensor')
- gain_grad: float32 [4096], P('tensor')
- weight_grad: bfloat16 [131072, 4096], P(('section', 'tensor', 'dp'))
- mean_loss: float32 [], replicated
The draws below stay inside these ranges and needn't reach their ends.
Inputs may be any that keep to these rules, and one draw needn't show every extreme that they name: `live_rows`: in the rows of one device the live rows come first; each device has 1 to 112 of them, and some device exactly 112.
All inputs are finite; a program needn't handle non-finite values.
Results may differ from the reference program's by a relative error of at most 0.0077.
Values may be sent and summed in bfloat16 or wider, within the bound.
No kernel may reach another device: no remote copies, remote signals or barrier semaphores. Data moves between devices by JAX's collectives and lax.ppermute only.
A program may use at most 128 MiB of HBM per device.

```python
import math
import jax
import jax.numpy as jnp
import numpy as np
from jax import lax

D = 4096
VOCAB = 131072
NSENT = 100
ROWS_DEV = 128
LIVE_DEV = 112
ROWS = 1024


def fullest_block(key):
    block_key = jax.random.fold_in(key, 5)
    blocks = ROWS // ROWS_DEV
    return jax.random.randint(block_key, (), blocks // 2, blocks)


def draw_hidden(key, part):
    key = jax.random.fold_in(key, 11)
    key_base, key_cols, key_rows, key_spot = jax.random.split(key, 4)
    col_scale = jnp.exp(jax.random.uniform(key_cols, (D,), jnp.float32, 0.0, math.log(10.0)))
    row_scale = jnp.exp(jax.random.uniform(key_rows, (ROWS, 1), jnp.float32, 0.0, math.log(10.0)))
    base = jnp.clip(jax.random.normal(key_base, (ROWS, D), jnp.float32), -5.0, 5.0)
    values = base * col_scale[None, :] * row_scale
    values = jnp.clip(values, -500.0, 500.0)
    spot_keys = jax.random.split(key_spot, 4)
    spot_block = jax.random.randint(spot_keys[0], (), 0, ROWS // ROWS_DEV)
    spot_row = spot_block * ROWS_DEV + jax.random.randint(spot_keys[1], (), 1, ROWS_DEV)
    spot_col = jax.random.randint(spot_keys[2], (), 0, D)
    spot_value = jnp.where(jax.random.randint(spot_keys[3], (), 0, 2) == 0, -500.0, 500.0)
    row_index = jnp.arange(ROWS)
    col_index = jnp.arange(D)
    spot_mask = (row_index[:, None] == spot_row) & (col_index[None, :] == spot_col)
    return jnp.where(spot_mask, spot_value, values).astype(jnp.bfloat16)


def draw_head_weight(key, part):
    key = jax.random.fold_in(key, 23)
    key_base = jax.random.fold_in(key, 0)
    spread = 3.0 / math.sqrt(D)
    values = jnp.clip(jax.random.normal(key_base, (VOCAB, D), jnp.float32), -6.0, 6.0) * spread
    return values.astype(jnp.bfloat16)


def draw_live_rows(key, part):
    fullest = fullest_block(key)
    key = jax.random.fold_in(key, 37)
    key_counts = jax.random.fold_in(key, 0)
    blocks = ROWS // ROWS_DEV
    numbers = jnp.arange(blocks)
    lowest = LIVE_DEV // 3
    ceiling = lowest + numbers * (LIVE_DEV - lowest) // (blocks - 1)
    bottom = jnp.maximum(ceiling // 2, 1)
    counts = jax.random.randint(key_counts, (blocks,), bottom, ceiling + 1)
    counts = jnp.where(numbers == fullest, LIVE_DEV, counts)
    positions = jnp.arange(ROWS)
    return (positions % ROWS_DEV < counts[positions // ROWS_DEV]).astype(jnp.int32)


def draw_span_starts(key, part):
    dense_block = fullest_block(key)
    key = jax.random.fold_in(key, 41)
    key_sparse, key_dense = jax.random.split(key, 2)
    sparse_bits = jax.random.randint(key_sparse, (ROWS,), 0, 8) == 0
    dense_bits = jax.random.randint(key_dense, (ROWS,), 0, 16) != 0
    positions = jnp.arange(ROWS)
    offsets = positions % ROWS_DEV
    in_dense = positions // ROWS_DEV == dense_block
    forced = offsets < NSENT + 2
    bits = jnp.where(in_dense, forced | dense_bits, sparse_bits)
    return bits.astype(jnp.int32)


def with_ends(values, key, smallest, top_value):
    place = [jax.random.randint(jax.random.fold_in(key, axis), (), 0, length) for axis, length in enumerate(values.shape)]
    widest = values.shape.index(max(values.shape))
    beside = place[:widest] + [(place[widest] + 1) % values.shape[widest]] + place[widest + 1:]
    return values.at[tuple(place)].set(smallest).at[tuple(beside)].set(top_value)


def skewed_wide(key, extent, number_of, slope):
    loads = [min(1 << octave, number_of + 1 - (1 << octave)) * (1 << 20) // math.isqrt((1 << octave) ** slope) + 1 for octave in range((number_of + 1).bit_length()) if 1 << octave <= number_of]
    scale = 1 + sum(loads) // (1 << 30)
    listing = np.cumsum(np.array([max(1, weight // scale) for weight in loads]))
    ticket = jax.random.randint(jax.random.fold_in(key, 1), extent, 0, int(listing[len(loads) - 1]))
    start = jnp.left_shift(1, jnp.searchsorted(jnp.asarray(listing, jnp.int32), ticket, side="right").astype(jnp.int32))
    grade = start - 1 + jax.random.randint(jax.random.fold_in(key, 4), extent, 0, 1 << 30) % jnp.minimum(start, number_of + 1 - start)
    return jax.random.permutation(jax.random.fold_in(key, 2), number_of)[grade].astype(jnp.int32)


def setup_inputs(seed: int = 0) -> dict:
    key_list = jax.random.split(jax.random.key(seed), 7)
    return {
        "hidden": draw_hidden(jax.random.fold_in(key_list[6], 71), 0),
        "norm_gain": jnp.clip(1.0 + 0.1 * jax.random.normal(key_list[1], (D,), jnp.float32), 0.5, 1.5),
        "head_weight": draw_head_weight(jax.random.fold_in(key_list[6], 71), 0),
        "targets": with_ends(skewed_wide(key_list[3], (ROWS,), VOCAB, 1), jax.random.fold_in(key_list[3], 3), 0, VOCAB - 1).astype(jnp.int32),
        "span_starts": draw_span_starts(jax.random.fold_in(key_list[6], 71), 0),
        "live_rows": draw_live_rows(jax.random.fold_in(key_list[6], 71), 0),
    }


loss_scale = 8192.0
epsilon = 1e-06

def reference(hidden, norm_gain, head_weight, targets, span_starts, live_rows):
    activation = hidden.astype(jnp.float32)
    mean_square = lax.optimization_barrier(jnp.mean(activation * activation, axis=1))
    inv_rms = lax.rsqrt(mean_square + epsilon)
    normed = (activation * inv_rms[:, None] * norm_gain[None, :]).astype(jnp.bfloat16)
    sentinel_flags = span_starts.reshape(-1, ROWS_DEV)
    span_order = (jnp.cumsum(sentinel_flags, axis=1) - 1).astype(jnp.int32)
    sentinel_ids = (VOCAB - 1 - jnp.clip(span_order, 0, NSENT - 1)).astype(jnp.int32)
    labels = jnp.where(sentinel_flags > 0, sentinel_ids, targets.reshape(-1, ROWS_DEV)).reshape(-1).astype(jnp.int32)
    logits = jnp.einsum('rd,vd->rv', normed.astype(jnp.float32), head_weight.astype(jnp.float32))
    row_max = lax.optimization_barrier(jnp.max(logits, axis=1))
    log_total = row_max + jnp.log(lax.optimization_barrier(jnp.sum(jnp.exp(logits - row_max[:, None]), axis=1)))
    columns = lax.iota(jnp.int32, VOCAB)
    matches = labels[:, None] == columns[None, :]
    target_logit = lax.optimization_barrier(jnp.sum(jnp.where(matches, logits, 0.0), axis=1))
    live_float = live_rows.astype(jnp.float32)
    live_total = jnp.sum(live_float)
    mean_loss = jnp.sum(live_float * (log_total - target_logit)) / live_total
    probability = jnp.exp(logits - log_total[:, None])
    row_factor = live_float * (loss_scale / live_total)
    grad_logits = ((probability - matches.astype(jnp.float32)) * row_factor[:, None]).astype(jnp.bfloat16)
    weight_grad = jnp.dot(grad_logits.T, normed, preferred_element_type=jnp.float32).astype(jnp.bfloat16)
    normed_grad = jnp.dot(grad_logits, head_weight, preferred_element_type=jnp.float32)
    gain_grad = lax.optimization_barrier(jnp.sum(normed_grad * activation * inv_rms[:, None], axis=0))
    scaled = normed_grad * norm_gain[None, :]
    inner_mean = lax.optimization_barrier(jnp.mean(activation * scaled, axis=1))
    cube = inv_rms * inv_rms * inv_rms
    hidden_grad = (inv_rms[:, None] * scaled - activation * (cube * inner_mean)[:, None]).astype(jnp.bfloat16)
    return (hidden_grad, gain_grad, weight_grad, mean_loss)
```

```python
import functools
import jax
import jax.numpy as jnp
from jax import lax
from jax.experimental import pallas as pl
from jax.experimental.pallas import tpu as pltpu
from jax.sharding import Mesh, PartitionSpec as P

NSENT = 100
LIVE = 112
loss_scale = 8192.0
epsilon = 1e-06
f32, bf16 = jnp.float32, jnp.bfloat16


def shift(x, axis, k):
    n = lax.axis_size(axis)
    return lax.ppermute(x, axis, [(i, (i + k) % n) for i in range(n)])


def norm_kernel(y_ref, *refs):
    Y = len(refs) - 2
    blocks, out_ref, inv_ref = refs[:Y], refs[Y], refs[Y + 1]
    Z = blocks[0].shape[0]
    total = jnp.zeros((LIVE, 128), f32)
    for block in blocks:
        for z in range(Z):
            a = block[z, 0:LIVE, :].astype(f32)
            total = total + a * a
    mean_square = jnp.sum(total, axis=1, keepdims=True) / (Z * Y * 128)
    inv = lax.rsqrt(mean_square + epsilon)
    inv_ref[...] = inv
    for k, block in enumerate(blocks):
        y = lax.rem(y_ref[0] - k + Y, Y)
        for z in range(Z):
            a = block[z, 0:LIVE, :].astype(f32)
            pieces = block[z, LIVE:128, :].astype(f32)
            gain = pieces[0:1] + pieces[1:2] + pieces[2:3]
            at = pl.multiple_of((z * Y + y) * 128, 128)
            out_ref[:, pl.ds(at, 128)] = (a * inv * gain).astype(bf16)


def norm_rows(y, blocks):
    Y, Z = len(blocks), blocks[0].shape[0]
    vmem = pl.BlockSpec(memory_space=pltpu.VMEM)
    return pl.pallas_call(
        norm_kernel,
        out_shape=(
            jax.ShapeDtypeStruct((LIVE, Z * Y * 128), bf16),
            jax.ShapeDtypeStruct((LIVE, 1), f32),
        ),
        in_specs=[pl.BlockSpec(memory_space=pltpu.SMEM)] + [vmem] * Y,
        out_specs=(vmem, vmem),
        compiler_params=pltpu.CompilerParams(vmem_limit_bytes=32 << 20),
        name="norm_rows",
    )(y, *blocks)


def split_kernel(Y, y_ref, *refs):
    parts, outs = refs[:-Y], refs[-Y:]
    Z = outs[0].shape[0]
    for k, out in enumerate(outs):
        y = lax.rem(y_ref[0] + k, Y)
        for z in range(Z):
            at = pl.multiple_of((z * Y + y) * 128, 128)
            total = parts[0][:, pl.ds(at, 128)].astype(f32)
            for part in parts[1:]:
                total = total + part[:, pl.ds(at, 128)].astype(f32)
            out[z] = total.astype(out.dtype)


def split_rows(y, Y, parts):
    D = parts[0].shape[1]
    Z = D // (Y * 128)
    vmem = pl.BlockSpec(memory_space=pltpu.VMEM)
    return pl.pallas_call(
        functools.partial(split_kernel, Y),
        out_shape=tuple(
            jax.ShapeDtypeStruct((Z, LIVE, 128), f32 if k == 0 else bf16) for k in range(Y)
        ),
        in_specs=[pl.BlockSpec(memory_space=pltpu.SMEM)] + [vmem] * len(parts),
        out_specs=(vmem,) * Y,
        compiler_params=pltpu.CompilerParams(vmem_limit_bytes=32 << 20),
        name="split_rows",
    )(y, *parts)


def merge(stats, axis):
    top, total, weighted, target = (lax.index_in_dim(stats, i, axis + 1, False) for i in range(4))
    best = jnp.max(top, axis=axis, keepdims=True)
    scale = jnp.exp(top - best)
    return jnp.stack(
        [
            jnp.squeeze(best, axis),
            jnp.sum(total * scale, axis=axis),
            jnp.sum(weighted * scale, axis=axis),
            jnp.sum(target, axis=axis),
        ]
    )


def body(hidden, norm_gain, head_weight, targets, span_starts, live_rows):
    Z, Y, X = (lax.axis_size(a) for a in "zyx")
    V, D = head_weight.shape
    vocab = V * 2 * Z * Y * X
    c, z, y, x = (lax.axis_index(a) for a in "czyx")
    y_here = jnp.reshape(y, (1,))

    weight_other = shift(head_weight, "c", 1)
    weight = jnp.concatenate([head_weight, weight_other], axis=0)

    span_order = jnp.cumsum(span_starts) - 1
    sentinel_ids = vocab - 1 - jnp.clip(span_order, 0, NSENT - 1)
    labels = jnp.where(span_starts > 0, sentinel_ids, targets)
    meta = jnp.stack([labels, live_rows])
    meta = jnp.concatenate([meta, shift(meta, "c", 1)])
    metas = jnp.stack([meta] + [shift(meta, "x", k) for k in range(1, X)])[:, :, :LIVE]
    labels_all = metas[:, 0].reshape(-1)
    live_float = metas[:, 1].astype(f32).reshape(-1)
    live_total = jnp.sum(live_float) + jnp.sum(metas[:, 3].astype(f32))

    high = norm_gain.astype(bf16)
    rest = norm_gain - high.astype(f32)
    middle = rest.astype(bf16)
    low = (rest - middle.astype(f32)).astype(bf16)
    block = jnp.concatenate(
        [hidden[:LIVE], jnp.stack([high, middle, low]), jnp.zeros((128 - LIVE - 3, 128), bf16)]
    )
    block = lax.all_to_all(jnp.broadcast_to(block[None], (Z, 128, 128)), "z", 0, 0)
    blocks = [block] + [shift(block, "y", k) for k in range(1, Y)]
    normed, inv_rms = norm_rows(y_here, blocks)

    normed_all = jnp.concatenate([normed] + [shift(normed, "x", j) for j in range(1, X)])
    logits = jnp.einsum("rd,vd->rv", normed_all, weight, preferred_element_type=f32)
    place = (z * Y + y) * X + x
    columns = lax.iota(jnp.int32, V)
    columns = jnp.concatenate(
        [(c * (Z * Y * X) + place) * V + columns, ((1 - c) * (Z * Y * X) + place) * V + columns]
    )
    matches = labels_all[:, None] == columns[None, :]
    top = jnp.max(logits, axis=1)
    weights = jnp.exp(logits - top[:, None])
    stats = jnp.stack(
        [
            top,
            jnp.sum(weights, axis=1),
            jnp.sum(weights * logits, axis=1),
            jnp.sum(jnp.where(matches, logits, 0.0), axis=1),
        ]
    ).reshape(4, X, LIVE)
    stats = lax.all_to_all(jnp.broadcast_to(stats[None], (Z * Y, 4, X, LIVE)), ("z", "y"), 0, 0)
    stats = merge(stats, 0)
    stats = merge(
        jnp.stack([stats] + [jnp.roll(shift(stats, "x", k), k, axis=1) for k in range(1, X)]), 0
    )
    row_max, exp_total, weighted_total, target_logit = (s.reshape(-1) for s in stats)
    log_total = row_max + jnp.log(exp_total)
    loss = jnp.sum(live_float * (log_total - target_logit))
    mean_loss = (loss + shift(loss, "c", 1)) / live_total

    row_factor = live_float * (loss_scale / live_total)
    probability = jnp.exp(logits - log_total[:, None])
    grad_logits = ((probability - matches.astype(f32)) * row_factor[:, None]).astype(bf16)
    parts = [
        jnp.dot(grad_logits[j * LIVE : (j + 1) * LIVE], weight, preferred_element_type=f32).astype(bf16)
        for j in range(X)
    ]
    arrived = [shift(parts[j], "x", -j) for j in range(1, X)]
    outs = split_rows(y_here, Y, [parts[0]] + arrived)
    total = outs[0]
    for k in range(1, Y):
        total = total + shift(outs[k], "y", k).astype(f32)
    total = lax.all_to_all(total.astype(bf16), "z", 0, 0)
    normed_grad = jnp.sum(total.astype(f32), axis=0)

    grad_t = functools.partial(jnp.einsum, "rv,rd->vd", preferred_element_type=f32)
    weight_grad_other = grad_t(grad_logits[:, V:], normed_all).astype(bf16)
    weight_grad = grad_t(grad_logits[:, :V], normed_all)
    weight_grad = (weight_grad + shift(weight_grad_other, "c", 1).astype(f32)).astype(bf16)

    activation = hidden[:LIVE].astype(f32)
    inner = row_factor[:LIVE] * (weighted_total[:LIVE] / exp_total[:LIVE] - target_logit[:LIVE])
    scaled = normed_grad * norm_gain[None, :]
    hidden_grad = inv_rms * scaled - activation * (inv_rms * inv_rms * (inner[:, None] / D))
    hidden_grad = jnp.pad(hidden_grad.astype(bf16), ((0, 128 - LIVE), (0, 0)))

    gain_grad = jnp.sum(normed_grad * activation * inv_rms, axis=0)
    gain_grad = gain_grad + shift(gain_grad, "c", 1)
    gain_grad = gain_grad + sum(shift(gain_grad, "x", k) for k in range(1, X))
    return (hidden_grad, gain_grad, weight_grad, mean_loss)


def solution(mesh):
    S, T, X = mesh.devices.shape
    Y = 4 if T % 4 == 0 else 2
    split = Mesh(mesh.devices.reshape(S, T // Y, Y, X), ("c", "z", "y", "x"))
    return jax.shard_map(
        body,
        mesh=split,
        in_specs=(
            P(("c", "x"), ("z", "y")),
            P(("z", "y")),
            P(("c", "z", "y", "x"), None),
            P(("c", "x")),
            P(("c", "x")),
            P(("c", "x")),
        ),
        out_specs=(
            P(("c", "x"), ("z", "y")),
            P(("z", "y")),
            P(("c", "z", "y", "x"), None),
            P(),
        ),
        check_vma=False,
    )
```

```python
import functools
import jax
import jax.numpy as jnp
from jax import lax
from jax.experimental import pallas as pl
from jax.experimental.pallas import tpu as pltpu
from jax.sharding import Mesh, PartitionSpec as P

NSENT = 100
LIVE = 112
loss_scale = 8192.0
epsilon = 1e-06
f32, bf16 = jnp.float32, jnp.bfloat16
VMEM = pl.BlockSpec(memory_space=pltpu.VMEM)
SMEM = pl.BlockSpec(memory_space=pltpu.SMEM)
R = 4


def shift(x, axis, k):
    n = lax.axis_size(axis)
    return lax.ppermute(x, axis, [(i, (i + k) % n) for i in range(n)])


def ring_gather(block, axis):
    half = block.shape[0] // 2
    one, three = shift(block, axis, 1), shift(block, axis, -1)
    two = shift(one[:half], axis, 1), shift(three[half:], axis, -1)
    return block, one, three, *two


def ring_reduce(up, down, far, axis):
    half = far.shape[0] // 2
    low, high = shift(far[:half], axis, 1), shift(far[half:], axis, -1)
    add = lambda a, b: (a.astype(f32) + b.astype(f32)).astype(bf16)
    up = jnp.concatenate([add(up[:half], low), up[half:]])
    down = jnp.concatenate([down[:half], add(down[half:], high)])
    return shift(up, axis, 1), shift(down, axis, -1)


def pick(refs, outer, inner, z, Zh):
    if outer == 2:
        ref = refs[3 + inner // 2]
        inner = inner % 2
    else:
        ref = refs[(0, 1, None, 2)[outer]]
    at = (inner * Zh + z) * LIVE
    return ref[at : at + LIVE, :].astype(f32)


def norm_kernel(Zh, y_ref, *refs):
    gains, a_refs, b_refs = refs[:R], refs[R : R + 5], refs[R + 5 : R + 10]
    out_ref, inv_ref = refs[R + 10 :]
    Z = 2 * Zh
    for j in range(R):
        load = lambda k, z: (
            pick(a_refs, j, k, z, Zh) if z < Zh else pick(b_refs, k, j, z - Zh, Zh)
        )
        total = jnp.zeros((LIVE, 128), f32)
        for k in range(R):
            for z in range(Z):
                a = load(k, z)
                total = total + a * a
        mean_square = jnp.sum(total, axis=1, keepdims=True) / (Z * R * 128)
        inv = lax.rsqrt(mean_square + epsilon)
        if j == 0:
            inv_ref[...] = inv
        for k in range(R):
            y = lax.rem(y_ref[0] - k + R, R)
            for z in range(Z):
                at = Zh * LIVE + z * 16
                pieces = gains[k][at : at + 16, :].astype(f32)
                gain = pieces[0:1] + pieces[1:2] + pieces[2:3]
                column = pl.multiple_of((z * R + y) * 128, 128)
                out_ref[j * LIVE : (j + 1) * LIVE, pl.ds(column, 128)] = (
                    load(k, z) * inv * gain
                ).astype(bf16)


def norm_rows(y, Zh, gains, a, b):
    return pl.pallas_call(
        functools.partial(norm_kernel, Zh),
        out_shape=(
            jax.ShapeDtypeStruct((R * LIVE, 2 * Zh * R * 128), bf16),
            jax.ShapeDtypeStruct((LIVE, 1), f32),
        ),
        in_specs=[SMEM] + [VMEM] * (R + 10),
        out_specs=(VMEM, VMEM),
        compiler_params=pltpu.CompilerParams(vmem_limit_bytes=40 << 20),
        name="norm_rows",
    )(y, *gains, *a, *b)


def partial_kernel(by_x, y_ref, g0_ref, g1_ref, w0_ref, w1_ref, *refs):
    part = jnp.dot(g0_ref[...], w0_ref[...], preferred_element_type=f32)
    part = part + jnp.dot(g1_ref[...], w1_ref[...], preferred_element_type=f32)
    if by_x:
        for j in range(R):
            for y in range(R):
                refs[j][y * LIVE : (y + 1) * LIVE, :] = part[
                    j * LIVE : (j + 1) * LIVE, y * 128 : (y + 1) * 128
                ].astype(refs[j].dtype)
    else:
        scratch = refs[R]
        for y in range(R):
            scratch[y] = part[:, y * 128 : (y + 1) * 128]
        for k in range(R):
            refs[k][...] = scratch[lax.rem(y_ref[0] + k, R)].astype(refs[k].dtype)


def partial_rows(y, by_x, Zh, g0, g1, w0, w1):
    rows, V = g0.shape
    first = 0 if by_x else Zh
    grad = pl.BlockSpec((rows, V), lambda z: (0, 0))
    weight = pl.BlockSpec((V, R * 128), lambda z: (0, z + first))
    block = pl.BlockSpec((R * LIVE, 128), lambda z: (z, 0))
    return pl.pallas_call(
        functools.partial(partial_kernel, by_x),
        grid=(Zh,),
        out_shape=tuple(
            jax.ShapeDtypeStruct((Zh * R * LIVE, 128), f32 if k == 0 else bf16) for k in range(R)
        ),
        in_specs=[SMEM, grad, grad, weight, weight],
        out_specs=(block,) * R,
        scratch_shapes=[] if by_x else [pltpu.VMEM((R, rows, 128), f32)],
        compiler_params=pltpu.CompilerParams(vmem_limit_bytes=40 << 20),
        name="partial_x" if by_x else "partial_y",
    )(y, g0, g1, w0, w1)


def turn_kernel(Zh, y_ref, a0, a1, a2, b0, b1, b2, *outs):
    for z in range(Zh):
        at = z * LIVE
        for k in range(R):
            row = pl.multiple_of((z * R + lax.rem(y_ref[0] + k, R)) * LIVE, 16)
            rows = pl.ds(row, LIVE)
            total = a0[rows, :] + a1[rows, :].astype(f32) + a2[rows, :].astype(f32)
            outs[k][at : at + LIVE, :] = total.astype(outs[k].dtype)
        for j in range(R):
            rows = slice((z * R + j) * LIVE, (z * R + j + 1) * LIVE)
            total = b0[rows, :] + b1[rows, :].astype(f32) + b2[rows, :].astype(f32)
            outs[R + j][at : at + LIVE, :] = total.astype(outs[R + j].dtype)


def turn_rows(y, Zh, a, b):
    shape = lambda k: jax.ShapeDtypeStruct((Zh * LIVE, 128), f32 if k == 0 else bf16)
    return pl.pallas_call(
        functools.partial(turn_kernel, Zh),
        out_shape=tuple(shape(k) for k in range(R)) * 2,
        in_specs=[SMEM] + [VMEM] * 6,
        out_specs=(VMEM,) * (2 * R),
        compiler_params=pltpu.CompilerParams(vmem_limit_bytes=40 << 20),
        name="turn_rows",
    )(y, *a, *b)


def merge(stats, axis):
    top, total, weighted, target = (lax.index_in_dim(stats, i, axis + 1, False) for i in range(4))
    best = jnp.max(top, axis=axis, keepdims=True)
    scale = jnp.exp(top - best)
    return jnp.stack(
        [
            jnp.squeeze(best, axis),
            jnp.sum(total * scale, axis=axis),
            jnp.sum(weighted * scale, axis=axis),
            jnp.sum(target, axis=axis),
        ]
    )


def body(hidden, norm_gain, head_weight, targets, span_starts, live_rows):
    Z, Y, X = (lax.axis_size(a) for a in "zyx")
    Zh = Z // 2
    V, D = head_weight.shape
    vocab = V * 2 * Z * Y * X
    c, z, y, x = (lax.axis_index(a) for a in "czyx")
    y_here = jnp.reshape(y, (1,))

    weight_other = shift(head_weight, "c", 1)

    span_order = jnp.cumsum(span_starts) - 1
    sentinel_ids = vocab - 1 - jnp.clip(span_order, 0, NSENT - 1)
    labels = jnp.where(span_starts > 0, sentinel_ids, targets)
    live_other = shift(live_rows, "c", 1)
    meta = jnp.stack([labels // 65536, labels // 256 % 256, labels % 256, live_rows, live_other])
    meta = jnp.pad(meta.astype(bf16), ((0, 11), (0, 0)))

    high = norm_gain.astype(bf16)
    rest = norm_gain - high.astype(f32)
    middle = rest.astype(bf16)
    low = (rest - middle.astype(f32)).astype(bf16)
    block = jnp.concatenate(
        [hidden[:LIVE], jnp.stack([high, middle, low]), jnp.zeros((128 - LIVE - 3, 128), bf16)]
    )
    block = lax.all_to_all(jnp.broadcast_to(block[None], (Z, 128, 128)), "z", 0, 0)
    block, weight_other = lax.optimization_barrier((block, weight_other))

    a_block = jnp.concatenate(
        [block[:Zh, :LIVE].reshape(-1, 128), block[:, LIVE:].reshape(-1, 128)]
    )
    b_block = jnp.concatenate([block[Zh:, :LIVE].reshape(-1, 128), meta])
    a_blocks = [a_block] + [shift(a_block, "y", k) for k in range(1, R)]
    b_blocks = [b_block] + [shift(b_block, "x", k) for k in range(1, R)]
    a_all = ring_gather(jnp.concatenate([a[: Zh * LIVE] for a in a_blocks]), "x")
    b_all = ring_gather(jnp.concatenate([b[: Zh * LIVE] for b in b_blocks]), "y")
    normed_all, inv_rms = norm_rows(y_here, Zh, a_blocks, a_all, b_all)

    metas = jnp.stack([b[Zh * LIVE :, :LIVE] for b in b_blocks])
    numbers = metas[:, :3].astype(jnp.int32)
    labels_all = (numbers[:, 0] * 65536 + numbers[:, 1] * 256 + numbers[:, 2]).reshape(-1)
    live_float = metas[:, 3].astype(f32).reshape(-1)
    live_total = jnp.sum(metas[:, 3:5].astype(f32))

    place = (z * Y + y) * X + x
    shares = []
    for core, w in ((c, head_weight), (1 - c, weight_other)):
        logits = jnp.einsum("rd,vd->rv", normed_all, w, preferred_element_type=f32)
        columns = (core * (Z * Y * X) + place) * V + lax.iota(jnp.int32, V)
        shares.append((logits, labels_all[:, None] == columns[None, :]))
    top = functools.reduce(jnp.maximum, [jnp.max(l, axis=1) for l, _ in shares])
    weights = [jnp.exp(l - top[:, None]) for l, _ in shares]
    stats = jnp.stack(
        [
            top,
            sum(jnp.sum(w, axis=1) for w in weights),
            sum(jnp.sum(w * l, axis=1) for w, (l, _) in zip(weights, shares)),
            sum(jnp.sum(jnp.where(m, l, 0.0), axis=1) for l, m in shares),
        ]
    ).reshape(4 * X, LIVE)
    stats = jnp.broadcast_to(stats[None], (Z * Y, 4 * X, LIVE))
    stats = lax.all_to_all(stats, ("z", "y"), 0, 0).reshape(Z * Y, 4, X, LIVE)
    stats = merge(stats, 0)
    stats = merge(
        jnp.stack([stats] + [jnp.roll(shift(stats, "x", k), k, axis=1) for k in range(1, X)]), 0
    )
    row_max, exp_total, weighted_total, target_logit = (s.reshape(-1) for s in stats)
    log_total = row_max + jnp.log(exp_total)
    row_factor = live_float * (loss_scale / live_total)
    grads = [
        ((jnp.exp(l - log_total[:, None]) - m.astype(f32)) * row_factor[:, None]).astype(bf16)
        for l, m in shares
    ]

    pa = partial_rows(y_here, True, Zh, *grads, head_weight, weight_other)
    pb = partial_rows(y_here, False, Zh, *grads, head_weight, weight_other)
    (g0, g1), pa, pb = lax.optimization_barrier((tuple(grads), pa, pb))
    a_in = ring_reduce(pa[3], pa[1], pa[2], "x")
    b_in = ring_reduce(pb[1], pb[3], pb[2], "y")
    grad_t = functools.partial(jnp.einsum, "rv,rd->vd", preferred_element_type=f32)
    weight_grad_other = shift(grad_t(g1, normed_all).astype(bf16), "c", 1)
    weight_grad = grad_t(g0, normed_all)
    weight_grad = (weight_grad + weight_grad_other.astype(f32)).astype(bf16)
    a_in, b_in, weight_grad = lax.optimization_barrier((a_in, b_in, weight_grad))
    outs = turn_rows(y_here, Zh, (pa[0], *a_in), (pb[0], *b_in))
    a_sum, b_sum = outs[0], outs[R]
    for k in range(1, R):
        a_sum = a_sum + shift(outs[k], "y", k).astype(f32)
        b_sum = b_sum + shift(outs[R + k], "x", -k).astype(f32)
    total = jnp.concatenate([a_sum, b_sum]).astype(bf16).reshape(Z, LIVE, 128)
    total = lax.all_to_all(total, "z", 0, 0)
    normed_grad = jnp.sum(total.astype(f32), axis=0)

    activation = hidden[:LIVE].astype(f32)
    gain_grad = jnp.sum(normed_grad * activation * inv_rms, axis=0)
    gain_grad = gain_grad + shift(gain_grad, "c", 1)
    gain_grad = gain_grad + sum(shift(gain_grad, "x", k) for k in range(1, X))

    inner = row_factor[:LIVE] * (weighted_total[:LIVE] / exp_total[:LIVE] - target_logit[:LIVE])
    scaled = normed_grad * norm_gain[None, :]
    hidden_grad = inv_rms * scaled - activation * (inv_rms * inv_rms * (inner[:, None] / D))
    hidden_grad = jnp.pad(hidden_grad.astype(bf16), ((0, 128 - LIVE), (0, 0)))

    loss = jnp.sum(live_float * (log_total - target_logit))
    mean_loss = (loss + shift(loss, "c", 1)) / live_total
    return (hidden_grad, gain_grad, weight_grad, mean_loss)


def solution(mesh):
    S, T, X = mesh.devices.shape
    split = Mesh(mesh.devices.reshape(S, T // R, R, X), ("c", "z", "y", "x"))
    rows, features, entries = ("c", "x"), ("z", "y"), ("c", "z", "y", "x")
    return jax.shard_map(
        body,
        mesh=split,
        in_specs=(P(rows, features), P(features), P(entries, None), P(rows), P(rows), P(rows)),
        out_specs=(P(rows, features), P(features), P(entries, None), P()),
        check_vma=False,
    )
```

```python
import functools
import jax
import jax.numpy as jnp
from jax import lax
from jax.experimental import pallas as pl
from jax.experimental.pallas import tpu as pltpu
from jax.sharding import Mesh, PartitionSpec as P

NSENT = 100
LIVE = 112
loss_scale = 8192.0
epsilon = 1e-06
f32, bf16 = jnp.float32, jnp.bfloat16
VMEM = pl.BlockSpec(memory_space=pltpu.VMEM)
SMEM = pl.BlockSpec(memory_space=pltpu.SMEM)
R = 4
SCOPED = 16 << 20


def shift(x, axis, k):
    n = lax.axis_size(axis)
    return lax.ppermute(x, axis, [(i, (i + k) % n) for i in range(n)])


def ring_gather(block, axis):
    half = block.shape[0] // 2
    one, three = shift(block, axis, 1), shift(block, axis, -1)
    two = shift(one[:half], axis, 1), shift(three[half:], axis, -1)
    return block, one, three, *two


def ring_reduce(up, down, low, high, axis):
    half = low.shape[0]
    add = lambda a, b: (a.astype(f32) + b.astype(f32)).astype(bf16)
    up = jnp.concatenate([add(up[:half], low), up[half:]])
    down = jnp.concatenate([down[:half], add(down[half:], high)])
    return shift(up, axis, 1), shift(down, axis, -1)


def pick(refs, outer, inner, z, Zh):
    if outer == 2:
        ref = refs[3 + inner // 2]
        inner = inner % 2
    else:
        ref = refs[(0, 1, None, 2)[outer]]
    at = (inner * Zh + z) * LIVE
    return ref[at : at + LIVE, :].astype(f32)


def norm_kernel(Zh, y_ref, *refs):
    gains, a_refs, b_refs = refs[:R], refs[R : R + 5], refs[R + 5 : R + 10]
    out_ref, inv_ref = refs[R + 10 :]
    Z = 2 * Zh
    for j in range(R):
        load = lambda k, z: (
            pick(a_refs, j, k, z, Zh) if z < Zh else pick(b_refs, k, j, z - Zh, Zh)
        )
        total = jnp.zeros((LIVE, 128), f32)
        for k in range(R):
            for z in range(Z):
                a = load(k, z)
                total = total + a * a
        mean_square = jnp.sum(total, axis=1, keepdims=True) / (Z * R * 128)
        inv = lax.rsqrt(mean_square + epsilon)
        if j == 0:
            inv_ref[...] = inv
        for k in range(R):
            y = lax.rem(y_ref[0] - k + R, R)
            for z in range(Z):
                at = Zh * LIVE + z * 16
                pieces = gains[k][at : at + 16, :].astype(f32)
                gain = pieces[0:1] + pieces[1:2] + pieces[2:3]
                column = pl.multiple_of((z * R + y) * 128, 128)
                out_ref[j * LIVE : (j + 1) * LIVE, pl.ds(column, 128)] = (
                    load(k, z) * inv * gain
                ).astype(bf16)


def norm_rows(y, Zh, gains, a, b):
    return pl.pallas_call(
        functools.partial(norm_kernel, Zh),
        out_shape=(
            jax.ShapeDtypeStruct((R * LIVE, 2 * Zh * R * 128), bf16),
            jax.ShapeDtypeStruct((LIVE, 1), f32),
        ),
        in_specs=[SMEM] + [VMEM] * (R + 10),
        out_specs=(VMEM, VMEM),
        compiler_params=pltpu.CompilerParams(vmem_limit_bytes=SCOPED),
        name="norm_rows",
    )(y, *gains, *a, *b)


def far_kernel(Zh, y_ref, g0_ref, g1_ref, w0_ref, w1_ref, n_ref, *refs):
    a_refs, b_refs, gain_ref = refs[0:2], refs[2:4], refs[4]
    rows = slice(2 * LIVE, 3 * LIVE)
    gain_ref[...] = jnp.zeros_like(gain_ref)
    for z in range(Zh):
        columns = slice(z * R * 128, (z + 1) * R * 128)
        part = jnp.dot(g0_ref[rows, :], w0_ref[:, columns], preferred_element_type=f32)
        part = part + jnp.dot(g1_ref[rows, :], w1_ref[:, columns], preferred_element_type=f32)
        gain = jnp.sum(part * n_ref[rows, columns].astype(f32), axis=0, keepdims=True)
        for y in range(R):
            at = (z % (Zh // 2) * R + y) * LIVE
            lanes = slice(y * 128, (y + 1) * 128)
            a_refs[z // (Zh // 2)][at : at + LIVE, :] = part[:, lanes].astype(bf16)
            gain_ref[z * R + y] = gain[:, lanes]
    for z in range(Zh):
        place = (Zh + z) * R + lax.rem(y_ref[0] + 2, R)
        columns = pl.ds(pl.multiple_of(place * 128, 128), 128)
        part = jnp.dot(g0_ref[...], w0_ref[:, columns], preferred_element_type=f32)
        part = part + jnp.dot(g1_ref[...], w1_ref[:, columns], preferred_element_type=f32)
        gain = jnp.sum(part * n_ref[:, columns].astype(f32), axis=0, keepdims=True)
        at = z % (Zh // 2) * R * LIVE
        b_refs[z // (Zh // 2)][at : at + R * LIVE, :] = part.astype(bf16)
        gain_ref[place] = gain


def near_kernel(Zh, y_ref, g0_ref, g1_ref, w0_ref, w1_ref, n_ref, *refs):
    a_refs, b_refs, gain_ref, scratch, sums = refs[0:3], refs[3:6], refs[6], refs[7], refs[8]
    gain_ref[...] = jnp.zeros_like(gain_ref)
    for z in range(Zh):
        columns = slice(z * R * 128, (z + 1) * R * 128)
        gain = jnp.zeros((1, R * 128), f32)
        for first, last, js in ((0, 2, (0, 1)), (3, 4, (3,))):
            rows = slice(first * LIVE, last * LIVE)
            part = jnp.dot(g0_ref[rows, :], w0_ref[:, columns], preferred_element_type=f32)
            part = part + jnp.dot(g1_ref[rows, :], w1_ref[:, columns], preferred_element_type=f32)
            gain = gain + jnp.sum(part * n_ref[rows, columns].astype(f32), axis=0, keepdims=True)
            for j in js:
                ref = a_refs[(0, 1, None, 2)[j]]
                own = slice((j - first) * LIVE, (j - first + 1) * LIVE)
                for y in range(R):
                    at = (z * R + y) * LIVE
                    ref[at : at + LIVE, :] = part[own, y * 128 : (y + 1) * 128].astype(ref.dtype)
        for y in range(R):
            gain_ref[z * R + y] = gain[:, y * 128 : (y + 1) * 128]
    for z in range(Zh):
        columns = slice((Zh + z) * R * 128, (Zh + z + 1) * R * 128)
        part = jnp.dot(g0_ref[...], w0_ref[:, columns], preferred_element_type=f32)
        part = part + jnp.dot(g1_ref[...], w1_ref[:, columns], preferred_element_type=f32)
        gain = jnp.sum(part * n_ref[:, columns].astype(f32), axis=0, keepdims=True)
        for y in range(R):
            scratch[y] = part[:, y * 128 : (y + 1) * 128]
            sums[y] = gain[:, y * 128 : (y + 1) * 128]
        at = z * R * LIVE
        for k in (0, 1, 3):
            ref = b_refs[(0, 1, None, 2)[k]]
            y = lax.rem(y_ref[0] + k, R)
            ref[at : at + R * LIVE, :] = scratch[y].astype(ref.dtype)
            gain_ref[(Zh + z) * R + y] = sums[y]


def partial_rows(y, far, Zh, g0, g1, w0, w1, normed):
    rows, block = g0.shape[0], Zh * R * LIVE
    gain = jax.ShapeDtypeStruct((2 * Zh * R, 1, 128), f32)
    if far:
        shapes = (jax.ShapeDtypeStruct((block // 2, 128), bf16),) * 4
        scratch = []
    else:
        shapes = tuple(jax.ShapeDtypeStruct((block, 128), t) for t in (f32, bf16, bf16)) * 2
        scratch = [pltpu.VMEM((R, rows, 128), f32), pltpu.VMEM((R, 1, 128), f32)]
    share = 4 if far else 1
    return pl.pallas_call(
        functools.partial(far_kernel if far else near_kernel, Zh),
        out_shape=(*shapes, gain),
        in_specs=[SMEM] + [VMEM] * 5,
        out_specs=(VMEM,) * (len(shapes) + 1),
        scratch_shapes=scratch,
        compiler_params=pltpu.CompilerParams(vmem_limit_bytes=SCOPED),
        cost_estimate=pl.CostEstimate(
            flops=4 * rows * w0.size // share, bytes_accessed=8 * w0.size // share, transcendentals=0
        ),
        name="far_rows" if far else "near_rows",
    )(y, g0, g1, w0, w1, normed)


def turn_kernel(Zh, y_ref, a0, a1, a2, b0, b1, b2, *outs):
    for z in range(Zh):
        at = z * LIVE
        for k in range(R):
            row = pl.multiple_of((z * R + lax.rem(y_ref[0] + k, R)) * LIVE, 16)
            rows = pl.ds(row, LIVE)
            total = a0[rows, :] + a1[rows, :].astype(f32) + a2[rows, :].astype(f32)
            outs[k][at : at + LIVE, :] = total.astype(outs[k].dtype)
        for j in range(R):
            rows = slice((z * R + j) * LIVE, (z * R + j + 1) * LIVE)
            total = b0[rows, :] + b1[rows, :].astype(f32) + b2[rows, :].astype(f32)
            outs[R + j][at : at + LIVE, :] = total.astype(outs[R + j].dtype)


def turn_rows(y, Zh, a, b):
    shape = lambda k: jax.ShapeDtypeStruct((Zh * LIVE, 128), f32 if k == 0 else bf16)
    return pl.pallas_call(
        functools.partial(turn_kernel, Zh),
        out_shape=tuple(shape(k) for k in range(R)) * 2,
        in_specs=[SMEM] + [VMEM] * 6,
        out_specs=(VMEM,) * (2 * R),
        compiler_params=pltpu.CompilerParams(vmem_limit_bytes=SCOPED),
        name="turn_rows",
    )(y, *a, *b)


def prepare_kernel(vocab, hidden_ref, gain_ref, target_ref, start_ref, live_ref, out_ref, meta_ref):
    gain = gain_ref[...]
    high = gain.astype(bf16).astype(f32)
    middle = (gain - high).astype(bf16).astype(f32)
    low = gain - high - middle
    row = lax.broadcasted_iota(jnp.int32, (16, 128), 0)
    tile = jnp.where(row == 0, high, jnp.where(row == 1, middle, jnp.where(row == 2, low, 0.0)))
    for z in range(out_ref.shape[0]):
        out_ref[z, 0:LIVE, :] = hidden_ref[0:LIVE, :]
        out_ref[z, LIVE:128, :] = tile.astype(bf16)
    starts = start_ref[...]
    upto = lax.broadcasted_iota(jnp.int32, (128, 128), 0) <= lax.broadcasted_iota(
        jnp.int32, (128, 128), 1
    )
    flags = jnp.broadcast_to(starts.astype(f32), (16, 128)).astype(bf16)
    order = jnp.dot(flags, upto.astype(f32).astype(bf16), preferred_element_type=f32)
    order = order[0:1].astype(jnp.int32) - 1
    sentinel = vocab - 1 - jnp.clip(order, 0, NSENT - 1)
    label = jnp.where(starts > 0, sentinel, target_ref[...])
    pieces = (label >> 16, (label >> 8) & 255, label & 255, live_ref[...])
    tile = jnp.zeros((16, 128), f32)
    for i, piece in enumerate(pieces):
        tile = jnp.where(row == i, piece.astype(f32), tile)
    meta_ref[...] = tile.astype(bf16)


def prepare(Z, vocab, hidden, norm_gain, targets, span_starts, live_rows):
    line = lambda a: a.reshape(1, 128)
    return pl.pallas_call(
        functools.partial(prepare_kernel, vocab),
        out_shape=(
            jax.ShapeDtypeStruct((Z, 128, 128), bf16),
            jax.ShapeDtypeStruct((16, 128), bf16),
        ),
        in_specs=[VMEM] * 5,
        out_specs=(VMEM, VMEM),
        name="prepare",
    )(hidden, line(norm_gain), line(targets), line(span_starts), line(live_rows))


def finish_kernel(D, total_ref, hidden_ref, gain_ref, inv_ref, inner_ref, out_ref):
    total = total_ref[0].astype(f32)
    for z in range(1, total_ref.shape[0]):
        total = total + total_ref[z].astype(f32)
    inv = inv_ref[...]
    slope = inv * inv * (inner_ref[...] / D)
    grad = inv * (total * gain_ref[...]) - hidden_ref[0:LIVE, :].astype(f32) * slope
    out_ref[0:LIVE, :] = grad.astype(bf16)
    out_ref[LIVE:128, :] = jnp.zeros((128 - LIVE, 128), bf16)


def finish(D, total, hidden, norm_gain, inv_rms, inner):
    return pl.pallas_call(
        functools.partial(finish_kernel, D),
        out_shape=jax.ShapeDtypeStruct((128, 128), bf16),
        in_specs=[VMEM] * 5,
        out_specs=VMEM,
        name="finish",
    )(total, hidden, norm_gain.reshape(1, 128), inv_rms, inner)


def turn(x, values):
    places = (x - lax.iota(jnp.int32, R)) % R
    return sum(
        jnp.where((places == j)[:, None], values[j : j + 1], jnp.zeros_like(values)) for j in range(R)
    )


def body(hidden, norm_gain, head_weight, targets, span_starts, live_rows):
    Z, Y, X = (lax.axis_size(a) for a in "zyx")
    Zh = Z // 2
    V, D = head_weight.shape
    vocab = V * 2 * Z * Y * X
    c, z, y, x = (lax.axis_index(a) for a in "czyx")
    y_here = jnp.reshape(y, (1,))

    weight_other = shift(head_weight, "c", 1)

    block, meta = prepare(Z, vocab, hidden, norm_gain, targets, span_starts, live_rows)
    block = lax.all_to_all(block, "z", 0, 0)
    block, weight_other = lax.optimization_barrier((block, weight_other))

    a_block = jnp.concatenate(
        [block[:Zh, :LIVE].reshape(-1, 128), block[:, LIVE:].reshape(-1, 128)]
    )
    b_block = jnp.concatenate([block[Zh:, :LIVE].reshape(-1, 128), meta])
    a_blocks = [a_block] + [shift(a_block, "y", k) for k in range(1, R)]
    b_blocks = [b_block] + [shift(b_block, "x", k) for k in range(1, R)]
    a_all = ring_gather(jnp.concatenate([a[: Zh * LIVE] for a in a_blocks]), "x")
    b_all = ring_gather(jnp.concatenate([b[: Zh * LIVE] for b in b_blocks]), "y")
    normed_all, inv_rms = norm_rows(y_here, Zh, a_blocks, a_all, b_all)

    metas = jnp.stack([b[Zh * LIVE :, :LIVE] for b in b_blocks])
    numbers = metas[:, :3].astype(jnp.int32)
    labels_all = (numbers[:, 0] * 65536 + numbers[:, 1] * 256 + numbers[:, 2]).reshape(-1)
    live_float = metas[:, 3].astype(f32).reshape(-1)
    live_total = jnp.sum(live_float)
    live_total = live_total + shift(live_total, "c", 1)

    place = (z * Y + y) * X + x
    shares = []
    for core, w in ((c, head_weight), (1 - c, weight_other)):
        logits = jnp.einsum("rd,vd->rv", normed_all, w, preferred_element_type=f32)
        columns = (core * (Z * Y * X) + place) * V + lax.iota(jnp.int32, V)
        shares.append((logits, labels_all[:, None] == columns[None, :]))
    top = functools.reduce(jnp.maximum, [jnp.max(l, axis=1) for l, _ in shares])
    here = top + jnp.log(sum(jnp.sum(jnp.exp(l - top[:, None]), axis=1) for l, _ in shares))
    here = turn(x, jnp.pad(here.reshape(X, LIVE), ((0, 0), (0, 128 - LIVE))))
    every = lax.all_to_all(jnp.broadcast_to(here[None], (Z * Y * X, X, 128)), ("z", "y", "x"), 0, 0)
    best = jnp.max(every, axis=0)
    log_total = best + jnp.log(jnp.sum(jnp.exp(every - best[None]), axis=0))
    log_total = turn(x, log_total)[:, :LIVE].reshape(-1)

    row_factor = live_float * (loss_scale / live_total)
    grads = [
        (jnp.exp(l - log_total[:, None]) - m.astype(f32)) * row_factor[:, None] for l, m in shares
    ]
    g0, g1 = (g.astype(bf16) for g in grads)

    operands = (Zh, g0, g1, head_weight, weight_other, normed_all)
    a_low, a_high, b_low, b_high, gain_far = partial_rows(y_here, True, *operands)
    a_low, a_high = shift(a_low, "x", 1), shift(a_high, "x", -1)
    b_low, b_high = shift(b_low, "y", 1), shift(b_high, "y", -1)
    a0, a1, a3, b0, b1, b3, gain_near = partial_rows(y_here, False, *operands)
    (a_low, a_high, b_low, b_high), (g0, g1) = lax.optimization_barrier(
        ((a_low, a_high, b_low, b_high), (g0, g1))
    )
    a_in = ring_reduce(a3, a1, a_low, a_high, "x")
    b_in = ring_reduce(b1, b3, b_low, b_high, "y")

    inner = sum(jnp.sum(g * l, axis=1) for g, (l, _) in zip(grads, shares)).reshape(X, LIVE)
    inner = turn(x, jnp.pad(inner, ((0, 0), (0, 128 - LIVE))))
    target = sum(
        jnp.sum(jnp.where(m, l, 0.0) * live_float[:, None]) for l, m in shares
    )
    gain = (gain_far + gain_near).reshape(Z * Y, 1, 128)
    side = jnp.concatenate(
        [
            jnp.broadcast_to(gain[:, None], (Z * Y, X, 1, 128)),
            jnp.broadcast_to(inner[None, :, None], (Z * Y, X, 1, 128)),
            jnp.full((Z * Y, X, 1, 128), target),
            jnp.zeros((Z * Y, X, 1, 128), f32),
        ],
        axis=2,
    ).reshape(Z * Y * X, 4, 128)
    side = jnp.sum(lax.all_to_all(side, ("z", "y", "x"), 0, 0), axis=0)
    inner = side[1, :LIVE, None]
    loss = jnp.sum(live_float * log_total) - side[2]
    both = jnp.stack([side[0], loss])
    both = both + shift(both, "c", 1)
    gain_grad = both[0] / norm_gain
    mean_loss = both[1, 0] / live_total

    grad_t = functools.partial(jnp.einsum, "rv,rd->vd", preferred_element_type=f32)
    weight_grad_other = shift(grad_t(g1, normed_all).astype(bf16), "c", 1)
    weight_grad = grad_t(g0, normed_all)
    weight_grad = (weight_grad + weight_grad_other.astype(f32)).astype(bf16)
    a_in, b_in, weight_grad = lax.optimization_barrier((a_in, b_in, weight_grad))
    outs = turn_rows(y_here, Zh, (a0, *a_in), (b0, *b_in))
    a_sum, b_sum = outs[0], outs[R]
    for k in range(1, R):
        a_sum = a_sum + shift(outs[k], "y", k).astype(f32)
        b_sum = b_sum + shift(outs[R + k], "x", -k).astype(f32)
    total = jnp.concatenate([a_sum, b_sum]).astype(bf16).reshape(Z, LIVE, 128)
    total = lax.all_to_all(total, "z", 0, 0)
    hidden_grad = finish(D, total, hidden, norm_gain, inv_rms, inner)
    return (hidden_grad, gain_grad, weight_grad, mean_loss)


def solution(mesh):
    S, T, X = mesh.devices.shape
    split = Mesh(mesh.devices.reshape(S, T // R, R, X), ("c", "z", "y", "x"))
    rows, features, entries = ("c", "x"), ("z", "y"), ("c", "z", "y", "x")
    return jax.shard_map(
        body,
        mesh=split,
        in_specs=(P(rows, features), P(features), P(entries, None), P(rows), P(rows), P(rows)),
        out_specs=(P(rows, features), P(features), P(entries, None), P()),
        check_vma=False,
    )
```

```python
import functools
import jax
import jax.numpy as jnp
from jax import lax
from jax.experimental import pallas as pl
from jax.experimental.pallas import tpu as pltpu
from jax.sharding import Mesh, PartitionSpec as P

NSENT = 100
LIVE = 112
loss_scale = 8192.0
epsilon = 1e-06
f32, bf16 = jnp.float32, jnp.bfloat16
VMEM = pl.BlockSpec(memory_space=pltpu.VMEM)
SMEM = pl.BlockSpec(memory_space=pltpu.SMEM)
ANY = pl.BlockSpec(memory_space=pl.ANY)
R = 4
ORDER = (0, 1, 3, 2)
SCOPED = 16 << 20


def shift(x, axis, k):
    n = lax.axis_size(axis)
    return lax.ppermute(x, axis, [(i, (i + k) % n) for i in range(n)])


def ring_gather(block, axis):
    half = block.shape[0] // 2
    one, three = shift(block, axis, 1), shift(block, axis, -1)
    two = shift(one[:half], axis, 1), shift(three[half:], axis, -1)
    return block, one, three, *two


def pick(refs, outer, inner, z, Zh):
    if outer == 2:
        ref = refs[3 + inner // 2]
        inner = inner % 2
    else:
        ref = refs[(0, 1, None, 2)[outer]]
    at = (inner * Zh + z) * LIVE
    return ref[at : at + LIVE, :].astype(f32)


def same():
    return lax.broadcasted_iota(jnp.int32, (LIVE, 128), 0) == lax.broadcasted_iota(
        jnp.int32, (LIVE, 128), 1
    )


def to_row(column):
    return jnp.sum(jnp.where(same(), column, 0.0), axis=0, keepdims=True)


def to_column(row):
    return jnp.sum(jnp.where(same(), row, 0.0), axis=1, keepdims=True)


def place_of(x, p):
    return lax.rem(x - ORDER[p] + R, R)


def forward_kernel(Zh, place_ref, w0_ref, w1_ref, *refs):
    gains, a_refs, b_refs = refs[:R], refs[R : R + 5], refs[R + 5 : R + 10]
    n_out, inv_ref, l_ref, share_ref, n_ref, w_ref, w_sems, n_sem = refs[R + 10 :]
    Z = 2 * Zh
    V = w0_ref.shape[0]
    tile = V // 2
    copies = [
        pltpu.make_async_copy(w.at[pl.ds(h * tile, tile)], w_ref.at[2 * i + h], w_sems.at[2 * i + h])
        for i, w in enumerate((w0_ref, w1_ref))
        for h in range(2)
    ]
    for copy in copies:
        copy.start()
    for p, j in enumerate(ORDER):
        load = lambda k, z: (
            pick(a_refs, j, k, z, Zh) if z < Zh else pick(b_refs, k, j, z - Zh, Zh)
        )
        total = jnp.zeros((LIVE, 128), f32)
        for k in range(R):
            for z in range(Z):
                a = load(k, z)
                total = total + a * a
        mean_square = jnp.sum(total, axis=1, keepdims=True) / (Z * R * 128)
        inv = lax.rsqrt(mean_square + epsilon)
        if j == 0:
            inv_ref[...] = inv
        for k in range(R):
            y = lax.rem(place_ref[0] - k + R, R)
            for z in range(Z):
                at = Zh * LIVE + z * 16
                pieces = gains[k][at : at + 16, :].astype(f32)
                gain = pieces[0:1] + pieces[1:2] + pieces[2:3]
                column = pl.multiple_of((z * R + y) * 128, 128)
                n_ref[p * LIVE : (p + 1) * LIVE, pl.ds(column, 128)] = (
                    load(k, z) * inv * gain
                ).astype(bf16)
    n_copy = pltpu.make_async_copy(n_ref, n_out, n_sem)
    n_copy.start()
    for q in range(4):
        copies[q].wait()
        l_ref[:, q * tile : (q + 1) * tile] = lax.dot_general(
            n_ref[...], w_ref[q], (((1,), (1,)), ((), ())), preferred_element_type=f32
        )
    place = lax.broadcasted_iota(jnp.int32, (R, 128), 0)
    share = jnp.zeros((R, 128), f32)
    for p in range(R):
        logits = l_ref[p * LIVE : (p + 1) * LIVE, :]
        top = jnp.max(logits, axis=1, keepdims=True)
        here = top + jnp.log(jnp.sum(jnp.exp(logits - top), axis=1, keepdims=True))
        share = jnp.where(place == place_of(place_ref[1], p), to_row(here), share)
    share_ref[...] = jnp.broadcast_to(share[None], share_ref.shape)
    n_copy.wait()


def forward(place, Zh, w0, w1, gains, a, b):
    V, D = w0.shape
    rows = R * LIVE
    return pl.pallas_call(
        functools.partial(forward_kernel, Zh),
        out_shape=(
            jax.ShapeDtypeStruct((rows, D), bf16),
            jax.ShapeDtypeStruct((LIVE, 1), f32),
            jax.ShapeDtypeStruct((rows, 2 * V), f32),
            jax.ShapeDtypeStruct((2 * Zh * R * R, R, 128), f32),
        ),
        in_specs=[SMEM, ANY, ANY] + [VMEM] * (R + 10),
        out_specs=(ANY, VMEM, VMEM, VMEM),
        scratch_shapes=[
            pltpu.VMEM((rows, D), bf16),
            pltpu.VMEM((4, V // 2, D), bf16),
            pltpu.SemaphoreType.DMA((4,)),
            pltpu.SemaphoreType.DMA,
        ],
        compiler_params=pltpu.CompilerParams(vmem_limit_bytes=28 << 20),
        cost_estimate=pl.CostEstimate(
            flops=4 * rows * V * D, bytes_accessed=4 * V * D, transcendentals=2 * rows * V
        ),
        name="forward",
    )(place, w0, w1, *gains, *a, *b)


def split_tile(rows):
    place = lax.broadcasted_iota(jnp.int32, (16, 128), 0)
    tile = jnp.zeros((16, 128), f32)
    for i, row in enumerate(rows):
        for n in range(3):
            piece = row.astype(bf16).astype(f32)
            tile = jnp.where(place == 3 * i + n, piece, tile)
            row = row - piece
    return tile.astype(bf16)


def read_tile(tile, n):
    tile = tile.astype(f32)
    return [tile[3 * i : 3 * i + 1] + tile[3 * i + 1 : 3 * i + 2] + tile[3 * i + 2 : 3 * i + 3] for i in range(n)]


def soft_kernel(Zh, place_ref, w0_ref, w1_ref, every_ref, l_ref, label_ref, live_ref, factor_ref, *refs):
    g_ref, g1_ref, side_ref, loss_ref, a_low, a_high, b_low, b_high, wa_ref, wb_ref, sems = refs
    V = w0_ref.shape[0]
    far = lax.rem(place_ref[0] + 2, R)
    copies = []
    for z in range(Zh):
        for i, w in enumerate((w0_ref, w1_ref)):
            column = pl.multiple_of(((Zh + z) * R + far) * 128, 128)
            rows = pl.ds(i * V, V)
            copies.append(
                (
                    pltpu.make_async_copy(
                        w.at[:, pl.ds(z * R * 128, R * 128)], wa_ref.at[z, rows], sems.at[z, 2 * i]
                    ),
                    pltpu.make_async_copy(
                        w.at[:, pl.ds(column, 128)], wb_ref.at[z, rows], sems.at[z, 2 * i + 1]
                    ),
                )
            )
    for pair in copies:
        for copy in pair:
            copy.start()
    every = every_ref[...]
    best = jnp.max(every, axis=0)
    log_total = best + jnp.log(jnp.sum(jnp.exp(every - best[None]), axis=0))
    place = lax.broadcasted_iota(jnp.int32, (R, 128), 0)
    lane = lax.broadcasted_iota(jnp.int32, (1, 2 * V), 1)
    entry = jnp.where(lane < V, place_ref[2] + lane, place_ref[3] + lane - V).astype(f32)
    target = jnp.zeros((1, 1), f32)
    loss = jnp.zeros((1, 1), f32)
    inner = []
    for p in range(R):
        rows = slice(p * LIVE, (p + 1) * LIVE)
        total = jnp.sum(
            jnp.where(place == place_of(place_ref[1], p), log_total, 0.0), axis=0, keepdims=True
        )
        live = live_ref[p : p + 1, :]
        logits = l_ref[rows, :]
        match = to_column(label_ref[p : p + 1, :]) == entry
        grad = jnp.exp(logits - to_column(total)) - jnp.where(match, 1.0, 0.0)
        grad = grad * to_column(factor_ref[p : p + 1, :])
        g_ref[rows, :] = grad.astype(bf16)
        g1_ref[rows, :] = grad[:, V:].astype(bf16)
        inner.append(to_row(jnp.sum(grad * logits, axis=1, keepdims=True)))
        own = jnp.sum(jnp.where(match, logits, 0.0), axis=1, keepdims=True) * to_column(live)
        target = target + jnp.sum(own, axis=0, keepdims=True)
        loss = loss + jnp.sum(live * total, axis=1, keepdims=True)
    for p in range(R):
        side_ref[p] = split_tile([inner[p], jnp.broadcast_to(target, (1, 128))])
    loss_ref[...] = jnp.broadcast_to(loss, (1, 128))
    rows = slice((R - 1) * LIVE, R * LIVE)
    for z in range(Zh):
        for pair in copies[2 * z : 2 * z + 2]:
            for copy in pair:
                copy.wait()
        part = jnp.dot(g_ref[rows, :], wa_ref[z], preferred_element_type=f32)
        other = jnp.dot(g_ref[...], wb_ref[z], preferred_element_type=f32)
        a_ref, b_ref = (a_low, b_low) if z < Zh // 2 else (a_high, b_high)
        at = z % (Zh // 2) * R * LIVE
        for y in range(R):
            a_ref[at + y * LIVE : at + (y + 1) * LIVE, :] = part[:, y * 128 : (y + 1) * 128].astype(
                bf16
            )
        b_ref[at : at + R * LIVE, :] = other.astype(bf16)
    a_low[Zh // 2 * R * LIVE :, :] = side_ref[R - 1]


def soft_rows(place, Zh, w0, w1, every, logits, labels, live, factor):
    V = w0.shape[0]
    rows = logits.shape[0]
    half = Zh // 2 * R * LIVE
    shapes = [((rows, 2 * V), bf16), ((rows, V), bf16), ((R, 16, 128), bf16), ((1, 128), f32)]
    shapes += [((half + 16, 128), bf16)] + [((half, 128), bf16)] * 3
    return pl.pallas_call(
        functools.partial(soft_kernel, Zh),
        out_shape=tuple(jax.ShapeDtypeStruct(*shape) for shape in shapes),
        in_specs=[SMEM, ANY, ANY] + [VMEM] * 5,
        out_specs=(VMEM,) * len(shapes),
        scratch_shapes=[
            pltpu.VMEM((Zh, 2 * V, R * 128), bf16),
            pltpu.VMEM((Zh, 2 * V, 128), bf16),
            pltpu.SemaphoreType.DMA((Zh, 4)),
        ],
        compiler_params=pltpu.CompilerParams(vmem_limit_bytes=20 << 20),
        name="soft_rows",
    )(place, w0, w1, every, logits, labels, live, factor)


def near_kernel(Zh, place_ref, w0_ref, w1_ref, side_ref, g_ref, a0, a1, a3, b0, b1, b3, w_ref, scratch, sems):
    V = w0_ref.shape[0]
    copies = []
    for z in range(2 * Zh):
        for i, w in enumerate((w0_ref, w1_ref)):
            copies.append(
                pltpu.make_async_copy(
                    w.at[:, pl.ds(z * R * 128, R * 128)], w_ref.at[z, pl.ds(i * V, V)], sems.at[z, i]
                )
            )
    for copy in copies:
        copy.start()
    for z in range(2 * Zh):
        for copy in copies[2 * z : 2 * z + 2]:
            copy.wait()
        at = z % Zh * R * LIVE
        if z < Zh:
            part = jnp.dot(g_ref[0 : 3 * LIVE, :], w_ref[z], preferred_element_type=f32)
            for p, ref in enumerate((a0, a1, a3)):
                for y in range(R):
                    ref[at + y * LIVE : at + (y + 1) * LIVE, :] = part[
                        p * LIVE : (p + 1) * LIVE, y * 128 : (y + 1) * 128
                    ].astype(ref.dtype)
        else:
            scratch[...] = jnp.dot(g_ref[...], w_ref[z], preferred_element_type=f32)
            for k, ref in ((0, b0), (1, b1), (3, b3)):
                column = pl.multiple_of(lax.rem(place_ref[0] + k, R) * 128, 128)
                ref[at : at + R * LIVE, :] = scratch[:, pl.ds(column, 128)].astype(ref.dtype)
    a1[Zh * R * LIVE :, :] = side_ref[1]
    a3[Zh * R * LIVE :, :] = side_ref[2]


def near_rows(place, Zh, w0, w1, side, g):
    V = w0.shape[0]
    rows, block = g.shape[0], Zh * R * LIVE
    shapes = [(block, 128), (block + 16, 128), (block + 16, 128)] + [(block, 128)] * 3
    return pl.pallas_call(
        functools.partial(near_kernel, Zh),
        out_shape=tuple(
            jax.ShapeDtypeStruct(shape, f32 if i % 3 == 0 else bf16) for i, shape in enumerate(shapes)
        ),
        in_specs=[SMEM, ANY, ANY, VMEM, VMEM],
        out_specs=(VMEM,) * 6,
        scratch_shapes=[
            pltpu.VMEM((2 * Zh, 2 * V, R * 128), bf16),
            pltpu.VMEM((rows, R * 128), f32),
            pltpu.SemaphoreType.DMA((2 * Zh, 2)),
        ],
        compiler_params=pltpu.CompilerParams(vmem_limit_bytes=28 << 20),
        name="near_rows",
    )(place, w0, w1, side, g)


def relay_kernel(up, down, low, high, up_out, down_out):
    half, block = high.shape[0], 2 * high.shape[0]
    add = lambda a, b: (a.astype(f32) + b.astype(f32)).astype(bf16)
    up_out[0:half, :] = add(up[0:half, :], low[0:half, :])
    up_out[half:block, :] = up[half:block, :]
    down_out[0:half, :] = down[0:half, :]
    down_out[half:block, :] = add(down[half:block, :], high[...])
    if up.shape[0] > block:
        mine, came = read_tile(up[block:, :], 2), read_tile(low[half:, :], 2)
        up_out[block:, :] = split_tile([a + b for a, b in zip(mine, came)])
        down_out[block:, :] = down[block:, :]


def relay(up, down, low, high):
    return pl.pallas_call(
        relay_kernel,
        out_shape=(jax.ShapeDtypeStruct(up.shape, bf16), jax.ShapeDtypeStruct(down.shape, bf16)),
        in_specs=[VMEM] * 4,
        out_specs=(VMEM, VMEM),
        compiler_params=pltpu.CompilerParams(vmem_limit_bytes=SCOPED),
        name="relay",
    )(up, down, low, high)


def turn_kernel(Zh, y_ref, side_ref, a0, a1, a2, b0, b1, b2, *outs):
    block, part = Zh * R * LIVE, Zh * LIVE
    for z in range(Zh):
        at = z * LIVE
        for k in range(R):
            row = pl.multiple_of((z * R + lax.rem(y_ref[0] + k, R)) * LIVE, 16)
            rows = pl.ds(row, LIVE)
            total = a0[rows, :] + a1[rows, :].astype(f32) + a2[rows, :].astype(f32)
            outs[k][at : at + LIVE, :] = total.astype(outs[k].dtype)
        for j in range(R):
            p = ORDER.index(j)
            rows = slice((z * R + p) * LIVE, (z * R + p + 1) * LIVE)
            total = b0[rows, :] + b1[rows, :].astype(f32) + b2[rows, :].astype(f32)
            outs[R + j][at : at + LIVE, :] = total.astype(outs[R + j].dtype)
    tiles = [read_tile(t, 2) for t in (side_ref[0], a1[block:, :], a2[block:, :])]
    tile = split_tile([sum(rows) for rows in zip(*tiles)])
    outs[2 * R][...] = tile
    for k in range(1, R):
        outs[k][part:, :] = tile


def turn_rows(y, Zh, side, a, b):
    part = Zh * LIVE
    shapes = [((part, 128), f32)] + [((part + 16, 128), bf16)] * (R - 1)
    shapes += [((part, 128), f32)] + [((part, 128), bf16)] * (R - 1) + [((16, 128), bf16)]
    return pl.pallas_call(
        functools.partial(turn_kernel, Zh),
        out_shape=tuple(jax.ShapeDtypeStruct(*shape) for shape in shapes),
        in_specs=[SMEM] + [VMEM] * 7,
        out_specs=(VMEM,) * (2 * R + 1),
        compiler_params=pltpu.CompilerParams(vmem_limit_bytes=SCOPED),
        name="turn_rows",
    )(y, side, *a, *b)


def gather_kernel(Zh, side_ref, *refs):
    a, b, out = refs[:R], refs[R : 2 * R], refs[2 * R]
    tiles = [read_tile(side_ref[...], 2)] + [read_tile(ref[Zh * LIVE :, :], 2) for ref in a[1:]]
    tile = split_tile([sum(rows) for rows in zip(*tiles)])
    for half, refs in enumerate((a, b)):
        for z in range(Zh):
            rows = slice(z * LIVE, (z + 1) * LIVE)
            total = refs[0][rows, :]
            for ref in refs[1:]:
                total = total + ref[rows, :].astype(f32)
            out[half * Zh + z, 0:LIVE, :] = total.astype(bf16)
            out[half * Zh + z, LIVE:128, :] = tile


def gather_rows(Zh, side, a, b):
    return pl.pallas_call(
        functools.partial(gather_kernel, Zh),
        out_shape=jax.ShapeDtypeStruct((2 * Zh, 128, 128), bf16),
        in_specs=[VMEM] * (2 * R + 1),
        out_specs=VMEM,
        compiler_params=pltpu.CompilerParams(vmem_limit_bytes=SCOPED),
        name="gather_rows",
    )(side, *a, *b)


def prepare_kernel(vocab, hidden_ref, gain_ref, target_ref, start_ref, live_ref, out_ref, meta_ref):
    gain = gain_ref[...]
    high = gain.astype(bf16).astype(f32)
    middle = (gain - high).astype(bf16).astype(f32)
    low = gain - high - middle
    row = lax.broadcasted_iota(jnp.int32, (16, 128), 0)
    tile = jnp.where(row == 0, high, jnp.where(row == 1, middle, jnp.where(row == 2, low, 0.0)))
    for z in range(out_ref.shape[0]):
        out_ref[z, 0:LIVE, :] = hidden_ref[0:LIVE, :]
        out_ref[z, LIVE:128, :] = tile.astype(bf16)
    starts = start_ref[...]
    upto = lax.broadcasted_iota(jnp.int32, (128, 128), 0) <= lax.broadcasted_iota(
        jnp.int32, (128, 128), 1
    )
    flags = jnp.broadcast_to(starts.astype(f32), (16, 128)).astype(bf16)
    order = jnp.dot(flags, upto.astype(f32).astype(bf16), preferred_element_type=f32)
    order = order[0:1].astype(jnp.int32) - 1
    sentinel = vocab - 1 - jnp.clip(order, 0, NSENT - 1)
    label = jnp.where(starts > 0, sentinel, target_ref[...])
    pieces = (label >> 16, (label >> 8) & 255, label & 255, live_ref[...])
    tile = jnp.zeros((16, 128), f32)
    for i, piece in enumerate(pieces):
        tile = jnp.where(row == i, piece.astype(f32), tile)
    meta_ref[...] = tile.astype(bf16)


def prepare(Z, vocab, hidden, norm_gain, targets, span_starts, live_rows):
    line = lambda a: a.reshape(1, 128)
    return pl.pallas_call(
        functools.partial(prepare_kernel, vocab),
        out_shape=(
            jax.ShapeDtypeStruct((Z, 128, 128), bf16),
            jax.ShapeDtypeStruct((16, 128), bf16),
        ),
        in_specs=[VMEM] * 5,
        out_specs=(VMEM, VMEM),
        name="prepare",
    )(hidden, line(norm_gain), line(targets), line(span_starts), line(live_rows))


def finish_kernel(D, loss_ref, total_ref, hidden_ref, gain_ref, inv_ref, out_ref, sums_ref):
    total = total_ref[0].astype(f32)
    for z in range(1, total_ref.shape[0]):
        total = total + total_ref[z].astype(f32)
    inner, target = read_tile(total[LIVE:128], 2)
    total = total[0:LIVE]
    inner = to_column(inner)
    inv = inv_ref[...]
    activation = hidden_ref[0:LIVE, :].astype(f32)
    grad = inv * (total * gain_ref[...]) - activation * (inv * inv * (inner / D))
    out_ref[0:LIVE, :] = grad.astype(bf16)
    out_ref[LIVE:128, :] = jnp.zeros((128 - LIVE, 128), bf16)
    sums_ref[0:1, :] = jnp.sum(total * activation * inv, axis=0, keepdims=True)
    sums_ref[1:2, :] = loss_ref[...] - target


def finish(D, loss, total, hidden, norm_gain, inv_rms):
    return pl.pallas_call(
        functools.partial(finish_kernel, D),
        out_shape=(jax.ShapeDtypeStruct((128, 128), bf16), jax.ShapeDtypeStruct((2, 128), f32)),
        in_specs=[VMEM] * 5,
        out_specs=(VMEM, VMEM),
        name="finish",
    )(loss, total, hidden, norm_gain.reshape(1, 128), inv_rms)


def body(hidden, norm_gain, head_weight, targets, span_starts, live_rows):
    Z, Y, X = (lax.axis_size(a) for a in "zyx")
    Zh = Z // 2
    V, D = head_weight.shape
    vocab = V * 2 * Z * Y * X
    c, z, y, x = (lax.axis_index(a) for a in "czyx")
    spot = (z * Y + y) * X + x
    first, second = (c * (Z * Y * X) + spot) * V, ((1 - c) * (Z * Y * X) + spot) * V
    place = jnp.stack([y, x, first, second]).astype(jnp.int32)

    live_other = shift(live_rows, "c", 1)
    weight_other = shift(head_weight, "c", 1)

    block, meta = prepare(Z, vocab, hidden, norm_gain, targets, span_starts, live_rows)
    block = lax.all_to_all(block, "z", 0, 0)
    meta = meta + jnp.pad(live_other[None].astype(bf16), ((4, 11), (0, 0)))
    block, weight_other, meta = lax.optimization_barrier((block, weight_other, meta))

    a_block = jnp.concatenate(
        [block[:Zh, :LIVE].reshape(-1, 128), block[:, LIVE:].reshape(-1, 128)]
    )
    b_block = jnp.concatenate([block[Zh:, :LIVE].reshape(-1, 128), meta])
    a_blocks = [a_block] + [shift(a_block, "y", k) for k in range(1, R)]
    b_blocks = [b_block] + [shift(b_block, "x", k) for k in range(1, R)]
    a_all = ring_gather(jnp.concatenate([a[: Zh * LIVE] for a in a_blocks]), "x")
    b_all = ring_gather(jnp.concatenate([b[: Zh * LIVE] for b in b_blocks]), "y")
    metas = jnp.stack([b_blocks[j][Zh * LIVE :] for j in ORDER]).astype(f32)
    labels = metas[:, 0] * 65536 + metas[:, 1] * 256 + metas[:, 2]
    live = metas[:, 3]
    live_total = jnp.sum(metas[:, 3:5])
    factor = live * (loss_scale / live_total)
    a_all, b_all, labels, live, factor = lax.optimization_barrier(
        (a_all, b_all, labels, live, factor)
    )

    weights = (head_weight, weight_other)
    normed_all, inv_rms, logits, share = forward(place, Zh, *weights, a_blocks, a_all, b_all)
    normed_other = shift(normed_all, "c", 1)
    every = lax.all_to_all(share, ("z", "y", "x"), 0, 0)
    every, normed_other = lax.optimization_barrier((every, normed_other))
    g, g1, side, loss, a_low, a_high, b_low, b_high = soft_rows(
        place, Zh, *weights, every, logits, labels, live, factor
    )

    a_low, a_high = shift(a_low, "x", 1), shift(a_high, "x", -1)
    b_low, b_high = shift(b_low, "y", 1), shift(b_high, "y", -1)
    near = near_rows(place, Zh, *weights, side, g)
    g_other = shift(g1, "c", 1)
    near, a_low, a_high, b_low, b_high, g, g_other = lax.optimization_barrier(
        (near, a_low, a_high, b_low, b_high, g, g_other)
    )
    a0, a1, a3, b0, b1, b3 = near
    a_up, a_down = relay(a3, a1, a_low, a_high)
    b_up, b_down = relay(b1, b3, b_low, b_high)
    a_in = shift(a_up, "x", 1), shift(a_down, "x", -1)
    b_in = shift(b_up, "y", 1), shift(b_down, "y", -1)
    grad_t = functools.partial(jnp.einsum, "rv,rd->vd", preferred_element_type=f32)
    weight_grad = (grad_t(g[:, :V], normed_all) + grad_t(g_other, normed_other)).astype(bf16)
    a_in, b_in, weight_grad = lax.optimization_barrier((a_in, b_in, weight_grad))
    outs = turn_rows(place, Zh, side, (a0, *a_in), (b0, *b_in))
    a_sums = [outs[0]] + [shift(outs[k], "y", k) for k in range(1, R)]
    b_sums = [outs[R]] + [shift(outs[R + k], "x", -k) for k in range(1, R)]
    total = gather_rows(Zh, outs[2 * R], a_sums, b_sums)
    total = lax.all_to_all(total, "z", 0, 0)
    hidden_grad, sums = finish(D, loss, total, hidden, norm_gain, inv_rms)

    sums = sums + shift(sums, "c", 1)
    gain_grad = sums[0]
    gain_grad = gain_grad + sum(shift(gain_grad, "x", k) for k in range(1, X))
    mean_loss = sums[1, 0] / live_total
    return (hidden_grad, gain_grad, weight_grad, mean_loss)


def solution(mesh):
    S, T, X = mesh.devices.shape
    split = Mesh(mesh.devices.reshape(S, T // R, R, X), ("c", "z", "y", "x"))
    rows, features, entries = ("c", "x"), ("z", "y"), ("c", "z", "y", "x")
    return jax.shard_map(
        body,
        mesh=split,
        in_specs=(P(rows, features), P(features), P(entries, None), P(rows), P(rows), P(rows)),
        out_specs=(P(rows, features), P(features), P(entries, None), P()),
        check_vma=False,
    )
```

```python
import functools
import jax
import jax.numpy as jnp
from jax import lax
from jax.experimental import pallas as pl
from jax.experimental.pallas import tpu as pltpu
from jax.sharding import Mesh, PartitionSpec as P

NSENT = 100
LIVE = 112
loss_scale = 8192.0
epsilon = 1e-06
f32, bf16 = jnp.float32, jnp.bfloat16
VMEM = pl.BlockSpec(memory_space=pltpu.VMEM)
SMEM = pl.BlockSpec(memory_space=pltpu.SMEM)
HBM = pl.BlockSpec(memory_space=pltpu.HBM)
R = 4
ORDER = (0, 1, 3, 2)
SCOPED = 16 << 20


def shift(x, axis, k):
    n = lax.axis_size(axis)
    return lax.ppermute(x, axis, [(i, (i + k) % n) for i in range(n)])


def ring_gather(block, axis):
    half = block.shape[0] // 2
    one, three = shift(block, axis, 1), shift(block, axis, -1)
    two = shift(one[:half], axis, 1), shift(three[half:], axis, -1)
    return block, one, three, *two


def pick(refs, outer, inner, z, Zh):
    if outer == 2:
        ref = refs[3 + inner // 2]
        inner = inner % 2
    else:
        ref = refs[(0, 1, None, 2)[outer]]
    at = pl.multiple_of((inner * Zh + z) * LIVE, 16)
    return ref[pl.ds(at, LIVE), :].astype(f32)


def same():
    return lax.broadcasted_iota(jnp.int32, (LIVE, 128), 0) == lax.broadcasted_iota(
        jnp.int32, (LIVE, 128), 1
    )


def to_row(column):
    return jnp.sum(jnp.where(same(), column, 0.0), axis=0, keepdims=True)


def to_column(row):
    return jnp.sum(jnp.where(same(), row, 0.0), axis=1, keepdims=True)


def place_of(x, p):
    return lax.rem(x - ORDER[p] + R, R)


def forward_kernel(Zh, place_ref, w0_ref, w1_ref, *refs):
    gains, a_refs, b_refs = refs[:R], refs[R : R + 5], refs[R + 5 : R + 10]
    n_ref, inv_ref, l_ref, share_ref, w_ref, w_sems = refs[R + 10 :]
    Z = 2 * Zh
    V = w0_ref.shape[0]
    tile = 2 * V // 2
    copies = [
        pltpu.make_async_copy(w, w_ref.at[i], w_sems.at[i]) for i, w in enumerate((w0_ref, w1_ref))
    ]
    for copy in copies:
        copy.start()
    for p, j in enumerate(ORDER):
        rows = slice(p * LIVE, (p + 1) * LIVE)

        def square(z, total):
            for k in range(R):
                for refs, outer, at in ((a_refs, j, k), (b_refs, k, j)):
                    block = pick(refs, outer, at, z, Zh)
                    total = total + block * block
            return total

        total = lax.fori_loop(0, Zh, square, jnp.zeros((LIVE, 128), f32))
        mean_square = jnp.sum(total, axis=1, keepdims=True) / (Z * R * 128)
        inv = lax.rsqrt(mean_square + epsilon)
        if j == 0:
            inv_ref[...] = inv
        wide = jnp.broadcast_to(inv, (LIVE, 128))

        def scale(z, _):
            for k in range(R):
                y = lax.rem(place_ref[0] - k + R, R)
                for half, refs, outer, at in ((0, a_refs, j, k), (1, b_refs, k, j)):
                    t = half * Zh + z
                    line = pl.multiple_of(Zh * LIVE + t * 16, 16)
                    pieces = gains[k][pl.ds(line, 16), :].astype(f32)
                    gain = pieces[0:1] + pieces[1:2] + pieces[2:3]
                    column = pl.multiple_of((t * R + y) * 128, 128)
                    n_ref[rows, pl.ds(column, 128)] = (
                        pick(refs, outer, at, z, Zh) * wide * gain
                    ).astype(bf16)
            return 0

        lax.fori_loop(0, Zh, scale, 0)

    def logits_of(q, _):
        pltpu.make_async_copy(w0_ref, w_ref.at[q], w_sems.at[q]).wait()
        l_ref[:, pl.ds(pl.multiple_of(q * tile, tile), tile)] = lax.dot_general(
            n_ref[...], w_ref[q], (((1,), (1,)), ((), ())), preferred_element_type=f32
        )
        return 0

    lax.fori_loop(0, 2, logits_of, 0)
    place = lax.broadcasted_iota(jnp.int32, (R, 128), 0)
    share = jnp.zeros((R, 128), f32)
    for p in range(R):
        logits = l_ref[p * LIVE : (p + 1) * LIVE, :]
        top = jnp.max(logits, axis=1, keepdims=True)
        here = top + jnp.log(jnp.sum(jnp.exp(logits - top), axis=1, keepdims=True))
        share = jnp.where(place == place_of(place_ref[1], p), to_row(here), share)
    share_ref[...] = jnp.broadcast_to(share[None], share_ref.shape)


def forward(place, Zh, w0, w1, gains, a, b):
    V, D = w0.shape
    rows = R * LIVE
    return pl.pallas_call(
        functools.partial(forward_kernel, Zh),
        out_shape=(
            jax.ShapeDtypeStruct((rows, D), bf16),
            jax.ShapeDtypeStruct((LIVE, 1), f32),
            jax.ShapeDtypeStruct((rows, 2 * V), f32),
            jax.ShapeDtypeStruct((2 * Zh * R * R, R, 128), f32),
        ),
        in_specs=[SMEM, HBM, HBM] + [VMEM] * (R + 10),
        out_specs=(VMEM,) * 4,
        scratch_shapes=[
            pltpu.VMEM((2, V, D), bf16),
            pltpu.SemaphoreType.DMA((2,)),
        ],
        compiler_params=pltpu.CompilerParams(vmem_limit_bytes=28 << 20),
        cost_estimate=pl.CostEstimate(
            flops=4 * rows * V * D, bytes_accessed=4 * V * D, transcendentals=2 * rows * V
        ),
        name="forward",
    )(place, w0, w1, *gains, *a, *b)


def split_tile(rows):
    place = lax.broadcasted_iota(jnp.int32, (16, 128), 0)
    tile = jnp.zeros((16, 128), f32)
    for i, row in enumerate(rows):
        for n in range(3):
            piece = row.astype(bf16).astype(f32)
            tile = jnp.where(place == 3 * i + n, piece, tile)
            row = row - piece
    return tile.astype(bf16)


def read_tile(tile, n):
    tile = tile.astype(f32)
    return [tile[3 * i : 3 * i + 1] + tile[3 * i + 1 : 3 * i + 2] + tile[3 * i + 2 : 3 * i + 3] for i in range(n)]


def soft_kernel(Zh, place_ref, w0_ref, w1_ref, every_ref, l_ref, n_ref, label_ref, live_ref, factor_ref, *refs):
    g_ref, g1_ref, side_ref, loss_ref, gain_ref, a_low, a_high, b_low, b_high = refs[:9]
    wa_ref, wb_ref, sems = refs[9:]
    V = w0_ref.shape[0]
    far = lax.rem(place_ref[0] + 2, R)
    copies = []
    for i, w in enumerate((w0_ref, w1_ref)):
        rows = pl.ds(i * V, V)
        copies.append(
            [pltpu.make_async_copy(w.at[:, pl.ds(0, Zh * R * 128)], wa_ref.at[rows], sems.at[0, i])]
        )
        for z in range(Zh):
            column = pl.multiple_of(((Zh + z) * R + far) * 128, 128)
            copies[-1].append(
                pltpu.make_async_copy(
                    w.at[:, pl.ds(column, 128)],
                    wb_ref.at[rows, pl.ds(z * 128, 128)],
                    sems.at[1 + z, i],
                )
            )
    for pair in copies:
        for copy in pair:
            copy.start()
    every = every_ref[...]
    best = jnp.max(every, axis=0)
    log_total = best + jnp.log(jnp.sum(jnp.exp(every - best[None]), axis=0))
    place = lax.broadcasted_iota(jnp.int32, (R, 128), 0)
    lane = lax.broadcasted_iota(jnp.int32, (1, 2 * V), 1)
    entry = jnp.where(lane < V, place_ref[2] + lane, place_ref[3] + lane - V).astype(f32)

    def block(p, sums):
        inner, target, loss = sums
        rows = pl.ds(pl.multiple_of(p * LIVE, 16), LIVE)
        distance = jnp.where(p < 2, p, 5 - p)
        here = lax.rem(place_ref[1] - distance + R, R)
        total = jnp.sum(jnp.where(place == here, log_total, 0.0), axis=0, keepdims=True)
        pick_row = lambda ref: jnp.sum(jnp.where(place == p, ref[...], 0.0), axis=0, keepdims=True)
        live = pick_row(live_ref)
        logits = l_ref[rows, :]
        match = to_column(pick_row(label_ref)) == entry
        grad = jnp.exp(logits - to_column(total)) - jnp.where(match, 1.0, 0.0)
        grad = grad * to_column(pick_row(factor_ref))
        g_ref[rows, :] = grad.astype(bf16)
        g1_ref[rows, :] = grad[:, V:].astype(bf16)
        line = to_row(jnp.sum(grad * logits, axis=1, keepdims=True))
        inner = jnp.where(place == p, line, inner)
        own = jnp.sum(jnp.where(match, logits, 0.0), axis=1, keepdims=True) * to_column(live)
        target = target + jnp.sum(own, axis=0, keepdims=True)
        loss = loss + jnp.sum(live * total, axis=1, keepdims=True)
        return inner, target, loss

    zero = jnp.zeros((1, 1), f32)
    inner, target, loss = lax.fori_loop(0, R, block, (jnp.zeros((R, 128), f32), zero, zero))
    for p in range(R):
        side_ref[p] = split_tile([inner[p : p + 1], jnp.broadcast_to(target, (1, 128))])
    loss_ref[...] = jnp.broadcast_to(loss, (1, 128))
    for pair in copies:
        for copy in pair:
            copy.wait()
    half = Zh // 2
    gain_ref[...] = jnp.zeros_like(gain_ref)
    part = jnp.dot(g_ref[(R - 1) * LIVE :, :], wa_ref[...], preferred_element_type=f32)
    gain = part * n_ref[(R - 1) * LIVE :, 0 : Zh * R * 128].astype(f32)
    gain = jnp.sum(gain, axis=0, keepdims=True)
    for t in range(Zh * R):
        at = t % (half * R) * LIVE
        gain_ref[t : t + 1, :] = gain[:, t * 128 : (t + 1) * 128]
        (a_low if t < half * R else a_high)[at : at + LIVE, :] = part[
            :, t * 128 : (t + 1) * 128
        ].astype(bf16)
    part = jnp.dot(g_ref[...], wb_ref[...], preferred_element_type=f32)
    for z in range(Zh):
        at = z % half * R * LIVE
        t = (Zh + z) * R + far
        block = part[:, z * 128 : (z + 1) * 128]
        (b_low if z < half else b_high)[at : at + R * LIVE, :] = block.astype(bf16)
        gain = block * n_ref[:, pl.ds(pl.multiple_of(t * 128, 128), 128)].astype(f32)
        gain_ref[pl.ds(t, 1), :] = jnp.sum(gain, axis=0, keepdims=True)
    a_low[Zh // 2 * R * LIVE :, :] = side_ref[R - 1]


def soft_rows(place, Zh, w0, w1, every, logits, normed, labels, live, factor):
    V = w0.shape[0]
    rows = logits.shape[0]
    half = Zh // 2 * R * LIVE
    shapes = [((rows, 2 * V), bf16), ((rows, V), bf16), ((R, 16, 128), bf16), ((1, 128), f32)]
    shapes += [((2 * Zh * R, 128), f32)]
    shapes += [((half + 16, 128), bf16)] + [((half, 128), bf16)] * 3
    return pl.pallas_call(
        functools.partial(soft_kernel, Zh),
        out_shape=tuple(jax.ShapeDtypeStruct(*shape) for shape in shapes),
        in_specs=[SMEM, HBM, HBM] + [VMEM] * 6,
        out_specs=(VMEM,) * len(shapes),
        scratch_shapes=[
            pltpu.VMEM((2 * V, Zh * R * 128), bf16),
            pltpu.VMEM((2 * V, Zh * 128), bf16),
            pltpu.SemaphoreType.DMA((1 + Zh, 2)),
        ],
        compiler_params=pltpu.CompilerParams(vmem_limit_bytes=20 << 20),
        name="soft_rows",
    )(place, w0, w1, every, logits, normed, labels, live, factor)


def near_kernel(Zh, place_ref, w0_ref, w1_ref, side_ref, g_ref, n_ref, *refs):
    a0, a1, a3, b0, b1, b3, gain_ref, w_ref, scratch, sems = refs
    V = w0_ref.shape[0]
    copies = []
    wide = 2 * R * 128
    for q in range(4):
        for i, w in enumerate((w0_ref, w1_ref)):
            copies.append(
                pltpu.make_async_copy(
                    w.at[:, pl.ds(q * wide, wide)], w_ref.at[q, pl.ds(i * V, V)], sems.at[q, i]
                )
            )
    for copy in copies:
        copy.start()

    def arrived(q):
        for i in range(2):
            pltpu.make_async_copy(
                w0_ref.at[:, pl.ds(0, wide)], w_ref.at[q, pl.ds(i * V, V)], sems.at[q, i]
            ).wait()
        return w_ref[q]

    gain_ref[...] = jnp.zeros_like(gain_ref)

    def first(q, _):
        part = jnp.dot(g_ref[0 : 3 * LIVE, :], arrived(q), preferred_element_type=f32)
        gain = n_ref[0 : 3 * LIVE, pl.ds(pl.multiple_of(q * wide, 128), wide)].astype(f32)
        gain = jnp.sum(part * gain, axis=0, keepdims=True)
        for t in range(2 * R):
            at = pl.multiple_of((q * 2 * R + t) * LIVE, 16)
            gain_ref[pl.ds(q * 2 * R + t, 1), :] = gain[:, t * 128 : (t + 1) * 128]
            for p, ref in enumerate((a0, a1, a3)):
                ref[pl.ds(at, LIVE), :] = part[
                    p * LIVE : (p + 1) * LIVE, t * 128 : (t + 1) * 128
                ].astype(ref.dtype)
        return 0

    def second(q, _):
        scratch[...] = jnp.dot(g_ref[...], arrived(2 + q), preferred_element_type=f32)
        for z in range(2):
            at = pl.multiple_of((q * 2 + z) * (R * LIVE), 16)
            for k, ref in ((0, b0), (1, b1), (3, b3)):
                t = z * R + lax.rem(place_ref[0] + k, R)
                part = scratch[:, pl.ds(pl.multiple_of(t * 128, 128), 128)]
                ref[pl.ds(at, R * LIVE), :] = part.astype(ref.dtype)
                t = (Zh + q * 2) * R + t
                gain = n_ref[:, pl.ds(pl.multiple_of(t * 128, 128), 128)].astype(f32)
                gain_ref[pl.ds(t, 1), :] = jnp.sum(part * gain, axis=0, keepdims=True)
        return 0

    lax.fori_loop(0, 2, first, 0)
    lax.fori_loop(0, 2, second, 0)
    a1[Zh * R * LIVE :, :] = side_ref[1]
    a3[Zh * R * LIVE :, :] = side_ref[2]


def near_rows(place, Zh, w0, w1, side, g, normed):
    V = w0.shape[0]
    rows, block = g.shape[0], Zh * R * LIVE
    shapes = [(block, 128), (block + 16, 128), (block + 16, 128)] + [(block, 128)] * 3
    return pl.pallas_call(
        functools.partial(near_kernel, Zh),
        out_shape=(
            *(jax.ShapeDtypeStruct(shape, bf16) for shape in shapes),
            jax.ShapeDtypeStruct((2 * Zh * R, 128), f32),
        ),
        in_specs=[SMEM, HBM, HBM, VMEM, VMEM, VMEM],
        out_specs=(VMEM,) * 7,
        scratch_shapes=[
            pltpu.VMEM((4, 2 * V, 2 * R * 128), bf16),
            pltpu.VMEM((rows, 2 * R * 128), f32),
            pltpu.SemaphoreType.DMA((4, 2)),
        ],
        compiler_params=pltpu.CompilerParams(vmem_limit_bytes=28 << 20),
        name="near_rows",
    )(place, w0, w1, side, g, normed)


def two(value):
    high = value.astype(bf16)
    return high, (value - high.astype(f32)).astype(bf16)


def relay_kernel(up, down, low, high, *refs):
    half, block = high.shape[0], 2 * high.shape[0]
    up_out, down_out = refs[-2:] if len(refs) == 2 else refs[2:4]
    add = lambda a, b: (a.astype(f32) + b.astype(f32)).astype(bf16)
    up_out[0:half, :] = add(up[0:half, :], low[0:half, :])
    up_out[half:block, :] = up[half:block, :]
    down_out[0:half, :] = down[0:half, :]
    down_out[half:block, :] = add(down[half:block, :], high[...])
    if len(refs) > 2:
        mine, came = read_tile(up[block:, :], 2), read_tile(low[half:, :], 2)
        up_out[block : block + 16, :] = split_tile([a + b for a, b in zip(mine, came)])
        down_out[block : block + 16, :] = down[block:, :]
        gain = refs[0][...] + refs[1][...]
        refs[4][...] = gain
        lines = gain.shape[0]
        for i, piece in enumerate(two(gain)):
            for out in (up_out, down_out):
                at = block + 16 + i * lines
                out[at : at + lines, :] = piece


def relay(up, down, low, high, *gains):
    lines = gains[0].shape[0] if gains else 0
    shape = jax.ShapeDtypeStruct((up.shape[0] + 2 * lines, 128), bf16)
    shapes = (shape, shape) + ((jax.ShapeDtypeStruct((lines, 128), f32),) if gains else ())
    return pl.pallas_call(
        relay_kernel,
        out_shape=shapes,
        in_specs=[VMEM] * (4 + len(gains)),
        out_specs=(VMEM,) * len(shapes),
        compiler_params=pltpu.CompilerParams(vmem_limit_bytes=SCOPED),
        name="relay",
    )(up, down, low, high, *gains)


def turn_kernel(Zh, y_ref, side_ref, mine, far, a0, a1, a2, b0, b1, b2, *outs):
    block, part = Zh * R * LIVE, Zh * LIVE

    def one(z, _):
        to = pl.ds(pl.multiple_of(z * LIVE, 16), LIVE)
        for k in range(R):
            row = pl.multiple_of((z * R + lax.rem(y_ref[0] + k, R)) * LIVE, 16)
            rows = pl.ds(row, LIVE)
            total = a0[rows, :].astype(f32) + a1[rows, :].astype(f32) + a2[rows, :].astype(f32)
            outs[k][to, :] = total.astype(outs[k].dtype)
        for j in range(R):
            rows = pl.ds(pl.multiple_of((z * R + ORDER.index(j)) * LIVE, 16), LIVE)
            total = b0[rows, :].astype(f32) + b1[rows, :].astype(f32) + b2[rows, :].astype(f32)
            outs[R + j][to, :] = total.astype(outs[R + j].dtype)
        return 0

    lax.fori_loop(0, Zh, one, 0)
    tiles = [read_tile(t, 2) for t in (side_ref[0], a1[block : block + 16, :], a2[block : block + 16, :])]
    tile = split_tile([sum(rows) for rows in zip(*tiles)])
    outs[2 * R][...] = tile
    lines, gain_ref = mine.shape[0], outs[2 * R + 2]
    gain = mine[...] + far[...]
    for ref in (a1, a2):
        for i in range(2):
            at = block + 16 + i * lines
            gain = gain + ref[at : at + lines, :].astype(f32)
    gain_ref[...] = gain
    Z = 2 * Zh
    place = lax.broadcasted_iota(jnp.int32, (Z, 128), 0)
    for k in range(R):
        gain = jnp.zeros((Z, 128), f32)
        for z in range(Z):
            line = gain_ref[pl.ds(z * R + lax.rem(y_ref[0] + k, R), 1), :]
            gain = jnp.where(place == z, line, gain)
        if k == 0:
            outs[2 * R + 1][...] = gain
        else:
            outs[k][part : part + 16, :] = tile
            outs[k][part + 16 : part + 32, :] = jnp.concatenate(
                [piece.astype(f32) for piece in two(gain)]
            ).astype(bf16)


def turn_rows(y, Zh, side, mine, far, a, b):
    part = Zh * LIVE
    shapes = [((part, 128), f32)] + [((part + 32, 128), bf16)] * (R - 1)
    shapes += [((part, 128), f32)] + [((part, 128), bf16)] * (R - 1) + [((16, 128), bf16)]
    shapes += [((2 * Zh, 128), f32)]
    return pl.pallas_call(
        functools.partial(turn_kernel, Zh),
        out_shape=tuple(jax.ShapeDtypeStruct(*shape) for shape in shapes),
        in_specs=[SMEM] + [VMEM] * 9,
        out_specs=(VMEM,) * (2 * R + 2),
        scratch_shapes=[pltpu.VMEM(mine.shape, f32)],
        compiler_params=pltpu.CompilerParams(vmem_limit_bytes=SCOPED),
        name="turn_rows",
    )(y, side, mine, far, *a, *b)


def gather_kernel(Zh, side_ref, gain_ref, *refs):
    a, b, out = refs[:R], refs[R : 2 * R], refs[2 * R]
    at, Z = Zh * LIVE, 2 * Zh
    tiles = [read_tile(side_ref[...], 2)] + [read_tile(ref[at : at + 16, :], 2) for ref in a[1:]]
    lines = [sum(rows) for rows in zip(*tiles)]
    gain = gain_ref[...]
    for ref in a[1:]:
        pieces = ref[at + 16 : at + 32, :].astype(f32)
        gain = gain + pieces[0:Z] + pieces[Z : 2 * Z]
    for z in range(Z):
        out[z, LIVE:128, :] = split_tile(lines + [gain[z : z + 1]])
    for half, refs in enumerate((a, b)):

        def one(z, _):
            rows = pl.ds(pl.multiple_of(z * LIVE, 16), LIVE)
            total = refs[0][rows, :]
            for ref in refs[1:]:
                total = total + ref[rows, :].astype(f32)
            out[half * Zh + z, 0:LIVE, :] = total.astype(bf16)
            return 0

        lax.fori_loop(0, Zh, one, 0)


def gather_rows(Zh, side, gain, a, b):
    return pl.pallas_call(
        functools.partial(gather_kernel, Zh),
        out_shape=jax.ShapeDtypeStruct((2 * Zh, 128, 128), bf16),
        in_specs=[VMEM] * (2 * R + 2),
        out_specs=VMEM,
        compiler_params=pltpu.CompilerParams(vmem_limit_bytes=SCOPED),
        name="gather_rows",
    )(side, gain, *a, *b)


def prepare_kernel(vocab, hidden_ref, gain_ref, target_ref, start_ref, live_ref, out_ref, meta_ref):
    gain = gain_ref[...]
    high = gain.astype(bf16).astype(f32)
    middle = (gain - high).astype(bf16).astype(f32)
    low = gain - high - middle
    row = lax.broadcasted_iota(jnp.int32, (16, 128), 0)
    tile = jnp.where(row == 0, high, jnp.where(row == 1, middle, jnp.where(row == 2, low, 0.0)))
    for z in range(out_ref.shape[0]):
        out_ref[z, 0:LIVE, :] = hidden_ref[0:LIVE, :]
        out_ref[z, LIVE:128, :] = tile.astype(bf16)
    starts = start_ref[...]
    upto = lax.broadcasted_iota(jnp.int32, (128, 128), 0) <= lax.broadcasted_iota(
        jnp.int32, (128, 128), 1
    )
    flags = jnp.broadcast_to(starts.astype(f32), (16, 128)).astype(bf16)
    order = jnp.dot(flags, upto.astype(f32).astype(bf16), preferred_element_type=f32)
    order = order[0:1].astype(jnp.int32) - 1
    sentinel = vocab - 1 - jnp.clip(order, 0, NSENT - 1)
    label = jnp.where(starts > 0, sentinel, target_ref[...])
    pieces = (label >> 16, (label >> 8) & 255, label & 255, live_ref[...])
    tile = jnp.zeros((16, 128), f32)
    for i, piece in enumerate(pieces):
        tile = jnp.where(row == i, piece.astype(f32), tile)
    meta_ref[...] = tile.astype(bf16)


def prepare(Z, vocab, hidden, norm_gain, targets, span_starts, live_rows):
    line = lambda a: a.reshape(1, 128)
    return pl.pallas_call(
        functools.partial(prepare_kernel, vocab),
        out_shape=(
            jax.ShapeDtypeStruct((Z, 128, 128), bf16),
            jax.ShapeDtypeStruct((16, 128), bf16),
        ),
        in_specs=[VMEM] * 5,
        out_specs=(VMEM, VMEM),
        name="prepare",
    )(hidden, line(norm_gain), line(targets), line(span_starts), line(live_rows))


def meta_kernel(at, w_ref, *refs):
    label_ref, live_ref, factor_ref, total_ref = refs[R:]
    place = lax.broadcasted_iota(jnp.int32, (R, 128), 0)
    labels, live, total = jnp.zeros((R, 128), f32), jnp.zeros((R, 128), f32), jnp.zeros((1, 1), f32)
    for p, j in enumerate(ORDER):
        tile = refs[j][at : at + 16, :].astype(f32)
        label = tile[0:1] * 65536 + tile[1:2] * 256 + tile[2:3]
        labels = jnp.where(place == p, label, labels)
        live = jnp.where(place == p, tile[3:4], live)
        total = total + jnp.sum(tile[3:4] + tile[4:5], axis=1, keepdims=True)
    label_ref[...] = labels
    live_ref[...] = live
    factor_ref[...] = live * (loss_scale / total)
    total_ref[...] = jnp.broadcast_to(total, (1, 128))


def read_meta(at, weight, blocks):
    line = jax.ShapeDtypeStruct((R, 128), f32)
    return pl.pallas_call(
        functools.partial(meta_kernel, at),
        out_shape=(line, line, line, jax.ShapeDtypeStruct((1, 128), f32)),
        in_specs=[VMEM] * (1 + R),
        out_specs=(VMEM,) * 4,
        compiler_params=pltpu.CompilerParams(vmem_limit_bytes=SCOPED),
        name="read_meta",
    )(weight, *blocks)


def outer_kernel(g_ref, h_ref, n_ref, m_ref, out_ref, g_turned, h_turned):
    V = h_ref.shape[1]

    @pl.when(pl.program_id(0) == 0)
    def _():
        g_turned[...] = g_ref[:, 0:V].astype(f32).T.astype(bf16)
        h_turned[...] = h_ref[...].astype(f32).T.astype(bf16)

    total = jnp.dot(g_turned[...], n_ref[...], preferred_element_type=f32)
    total = total + jnp.dot(h_turned[...], m_ref[...], preferred_element_type=f32)
    out_ref[...] = total.astype(bf16)


def outer(g, h, n, m):
    rows, V = h.shape
    D, wide = n.shape[1], 512
    whole = lambda a: pl.BlockSpec(a.shape, lambda i: (0, 0))
    part = pl.BlockSpec((rows, wide), lambda i: (0, i))
    return pl.pallas_call(
        outer_kernel,
        grid=(D // wide,),
        out_shape=jax.ShapeDtypeStruct((V, D), bf16),
        in_specs=[whole(g), whole(h), part, part],
        out_specs=pl.BlockSpec((V, wide), lambda i: (0, i)),
        scratch_shapes=[pltpu.VMEM((V, rows), bf16)] * 2,
        compiler_params=pltpu.CompilerParams(vmem_limit_bytes=SCOPED),
        cost_estimate=pl.CostEstimate(
            flops=4 * rows * V * D, bytes_accessed=8 * V * D, transcendentals=0
        ),
        name="outer",
    )(g, h, n, m)


def finish_kernel(D, loss_ref, total_ref, hidden_ref, gain_ref, inv_ref, out_ref, sums_ref):
    total = total_ref[0].astype(f32)
    for z in range(1, total_ref.shape[0]):
        total = total + total_ref[z].astype(f32)
    inner, target, gain = read_tile(total[LIVE:128], 3)
    total = total[0:LIVE]
    inner = to_column(inner)
    inv = inv_ref[...]
    activation = hidden_ref[0:LIVE, :].astype(f32)
    grad = inv * (total * gain_ref[...]) - activation * (inv * inv * (inner / D))
    out_ref[0:LIVE, :] = grad.astype(bf16)
    out_ref[LIVE:128, :] = jnp.zeros((128 - LIVE, 128), bf16)
    sums_ref[0:1, :] = gain / gain_ref[...]
    sums_ref[1:2, :] = loss_ref[...] - target


def finish(D, loss, total, hidden, norm_gain, inv_rms):
    return pl.pallas_call(
        functools.partial(finish_kernel, D),
        out_shape=(jax.ShapeDtypeStruct((128, 128), bf16), jax.ShapeDtypeStruct((2, 128), f32)),
        in_specs=[VMEM] * 5,
        out_specs=(VMEM, VMEM),
        name="finish",
    )(loss, total, hidden, norm_gain.reshape(1, 128), inv_rms)


def body(hidden, norm_gain, head_weight, targets, span_starts, live_rows):
    Z, Y, X = (lax.axis_size(a) for a in "zyx")
    Zh = Z // 2
    V, D = head_weight.shape
    vocab = V * 2 * Z * Y * X
    c, z, y, x = (lax.axis_index(a) for a in "czyx")
    spot = (z * Y + y) * X + x
    first, second = (c * (Z * Y * X) + spot) * V, ((1 - c) * (Z * Y * X) + spot) * V
    place = jnp.stack([y, x, first, second]).astype(jnp.int32)

    live_other = shift(live_rows, "c", 1)
    weight_other = shift(head_weight, "c", 1)

    block, meta = prepare(Z, vocab, hidden, norm_gain, targets, span_starts, live_rows)
    block = lax.all_to_all(block, "z", 0, 0)
    meta = meta + jnp.pad(live_other[None].astype(bf16), ((4, 11), (0, 0)))
    block, weight_other, meta = lax.optimization_barrier((block, weight_other, meta))

    a_block = jnp.concatenate(
        [block[:Zh, :LIVE].reshape(-1, 128), block[:, LIVE:].reshape(-1, 128)]
    )
    b_block = jnp.concatenate([block[Zh:, :LIVE].reshape(-1, 128), meta])
    a_blocks = [a_block] + [shift(a_block, "y", k) for k in range(1, R)]
    b_blocks = [b_block] + [shift(b_block, "x", k) for k in range(1, R)]
    a_all = ring_gather(jnp.concatenate([a[: Zh * LIVE] for a in a_blocks]), "x")
    b_all = ring_gather(jnp.concatenate([b[: Zh * LIVE] for b in b_blocks]), "y")
    labels, live, factor, live_total = read_meta(Zh * LIVE, head_weight, b_blocks)
    a_all, b_all, labels, live, factor = lax.optimization_barrier(
        (a_all, b_all, labels, live, factor)
    )

    weights = (head_weight, weight_other)
    normed_all, inv_rms, logits, share = forward(place, Zh, *weights, a_blocks, a_all, b_all)
    normed_other = shift(normed_all, "c", 1)
    every = lax.all_to_all(share, ("z", "y", "x"), 0, 0)
    every, normed_other = lax.optimization_barrier((every, normed_other))
    g, g1, side, loss, gain_far, a_low, a_high, b_low, b_high = soft_rows(
        place, Zh, *weights, every, logits, normed_all, labels, live, factor
    )

    a_low, a_high = shift(a_low, "x", 1), shift(a_high, "x", -1)
    b_low, b_high = shift(b_low, "y", 1), shift(b_high, "y", -1)
    near = near_rows(place, Zh, *weights, side, g, normed_all)
    g_other = shift(g1, "c", 1)
    near, a_low, a_high, b_low, b_high, g, g_other = lax.optimization_barrier(
        (near, a_low, a_high, b_low, b_high, g, g_other)
    )
    a0, a1, a3, b0, b1, b3, gain_near = near
    a_up, a_down, gain = relay(a3, a1, a_low, a_high, gain_far, gain_near)
    b_up, b_down = relay(b1, b3, b_low, b_high)
    a_in = shift(a_up, "x", 1), shift(a_down, "x", -1)
    b_in = shift(b_up, "y", 1), shift(b_down, "y", -1)
    gain_in = shift(gain, "x", 2)
    weight_grad = outer(g, g_other, normed_all, normed_other)
    a_in, b_in, weight_grad = lax.optimization_barrier((a_in, b_in, weight_grad))
    outs = turn_rows(place, Zh, side, gain, gain_in, (a0, *a_in), (b0, *b_in))
    a_sums = [outs[0]] + [shift(outs[k], "y", k) for k in range(1, R)]
    b_sums = [outs[R]] + [shift(outs[R + k], "x", -k) for k in range(1, R)]
    total = gather_rows(Zh, outs[2 * R], outs[2 * R + 1], a_sums, b_sums)
    total = lax.all_to_all(total, "z", 0, 0)
    hidden_grad, sums = finish(D, loss, total, hidden, norm_gain, inv_rms)

    sums = sums + shift(sums, "c", 1)
    gain_grad = sums[0]
    mean_loss = sums[1, 0] / live_total[0, 0]
    return (hidden_grad, gain_grad, weight_grad, mean_loss)


def solution(mesh):
    S, T, X = mesh.devices.shape
    split = Mesh(mesh.devices.reshape(S, T // R, R, X), ("c", "z", "y", "x"))
    rows, features, entries = ("c", "x"), ("z", "y"), ("c", "z", "y", "x")
    return jax.shard_map(
        body,
        mesh=split,
        in_specs=(P(rows, features), P(features), P(entries, None), P(rows), P(rows), P(rows)),
        out_specs=(P(rows, features), P(features), P(entries, None), P()),
        check_vma=False,
    )
```

```python
import functools
import jax
import jax.numpy as jnp
from jax import lax
from jax.experimental import pallas as pl
from jax.experimental.pallas import tpu as pltpu
from jax.sharding import Mesh, PartitionSpec as P

NSENT = 100
LIVE = 112
loss_scale = 8192.0
epsilon = 1e-06
f32, bf16 = jnp.float32, jnp.bfloat16
VMEM = pl.BlockSpec(memory_space=pltpu.VMEM)
SMEM = pl.BlockSpec(memory_space=pltpu.SMEM)
HBM = pl.BlockSpec(memory_space=pltpu.HBM)
R = 4
ORDER = (0, 1, 3, 2)
SCOPED = 16 << 20


def shift(x, axis, k):
    n = lax.axis_size(axis)
    return lax.ppermute(x, axis, [(i, (i + k) % n) for i in range(n)])


def ring_gather(block, axis):
    half = block.shape[0] // 2
    one, three = shift(block, axis, 1), shift(block, axis, -1)
    two = shift(one[:half], axis, 1), shift(three[half:], axis, -1)
    return block, one, three, *two


PARTS = ((0, 0, 4), (1, 0, 4), (3, 0, 4), (2, 0, 2), (2, 2, 4))


def spot_of(j):
    return jnp.where(j < 2, j, 5 - j)


def same():
    return lax.broadcasted_iota(jnp.int32, (LIVE, 128), 0) == lax.broadcasted_iota(
        jnp.int32, (LIVE, 128), 1
    )


def to_row(column):
    return jnp.sum(jnp.where(same(), column, 0.0), axis=0, keepdims=True)


def to_column(row):
    return jnp.sum(jnp.where(same(), row, 0.0), axis=1, keepdims=True)


def place_of(x, p):
    return lax.rem(x - ORDER[p] + R, R)


def forward_kernel(Zh, place_ref, w0_ref, w1_ref, gain_ref, *refs):
    a_refs, b_refs = refs[:5], refs[5:10]
    n_ref, inv_ref, l_ref, share_ref, w_ref, total_ref, w_sems = refs[10:]
    Z = 2 * Zh
    V = w0_ref.shape[0]
    copies = [
        pltpu.make_async_copy(w, w_ref.at[i], w_sems.at[i]) for i, w in enumerate((w0_ref, w1_ref))
    ]
    for copy in copies:
        copy.start()

    def load(ref, i, z):
        at = pl.multiple_of((i * Zh + z) * LIVE, 16)
        return ref[pl.ds(at, LIVE), :].astype(f32)

    def squares(ref, i):
        def add(z, total):
            block = load(ref, i, z)
            return total + block * block

        return lax.fori_loop(0, Zh, add, jnp.zeros((LIVE, 128), f32), unroll=True)

    total_ref[...] = jnp.zeros_like(total_ref)
    for ref, (j, first, last) in zip(a_refs, PARTS):
        add = lambda i, total, ref=ref: total + squares(ref, i)
        p = ORDER.index(j)
        total_ref[p] = lax.fori_loop(0, last - first, add, total_ref[p])
    for ref, (_, first, last) in zip(b_refs, PARTS):

        def add(i, _, ref=ref, first=first):
            p = spot_of(first + i)
            total_ref[p] = total_ref[p] + squares(ref, i)
            return 0

        lax.fori_loop(0, last - first, add, 0)
    for p in range(R):
        mean_square = jnp.sum(total_ref[p], axis=1, keepdims=True) / (Z * R * 128)
        inv = lax.rsqrt(mean_square + epsilon)
        if p == 0:
            inv_ref[...] = inv
        total_ref[p] = jnp.broadcast_to(inv, (LIVE, 128))

    def scale(ref, i, k, p, half):
        inv = total_ref[p]
        y = lax.rem(place_ref[0] - k + R, R)
        rows = pl.ds(pl.multiple_of(p * LIVE, 16), LIVE)

        def one(z, _):
            t = half * Zh + z
            column = pl.multiple_of((t * R + y) * 128, 128)
            n_ref[rows, pl.ds(column, 128)] = (
                load(ref, i, z) * inv * gain_ref[pl.ds(k * Z + t, 1), :]
            ).astype(bf16)
            return 0

        lax.fori_loop(0, Zh, one, 0, unroll=True)

    for ref, (j, first, last) in zip(a_refs, PARTS):

        def one(i, _, ref=ref, j=j, first=first):
            scale(ref, i, first + i, ORDER.index(j), 0)
            return 0

        lax.fori_loop(0, last - first, one, 0)
    for ref, (k, first, last) in zip(b_refs, PARTS):

        def one(i, _, ref=ref, k=k, first=first):
            scale(ref, i, k, spot_of(first + i), 1)
            return 0

        lax.fori_loop(0, last - first, one, 0)

    def logits_of(q, _):
        pltpu.make_async_copy(w0_ref, w_ref.at[q], w_sems.at[q]).wait()
        l_ref[:, pl.ds(pl.multiple_of(q * V, V), V)] = lax.dot_general(
            n_ref[:, 0 : w_ref.shape[2]], w_ref[q], (((1,), (1,)), ((), ())), preferred_element_type=f32
        )
        return 0

    lax.fori_loop(0, 2, logits_of, 0)
    place = lax.broadcasted_iota(jnp.int32, (R, 128), 0)
    share = jnp.zeros((R, 128), f32)
    for p in range(R):
        logits = l_ref[p * LIVE : (p + 1) * LIVE, :]
        top = jnp.max(logits, axis=1, keepdims=True)
        here = top + jnp.log(jnp.sum(jnp.exp(logits - top), axis=1, keepdims=True))
        share = jnp.where(place == place_of(place_ref[1], p), to_row(here), share)
    share_ref[...] = jnp.broadcast_to(share[None], share_ref.shape)


def forward(place, Zh, w0, w1, gain, a, b):
    V, D = w0.shape
    rows = R * LIVE
    return pl.pallas_call(
        functools.partial(forward_kernel, Zh),
        out_shape=(
            jax.ShapeDtypeStruct((rows, D + V), bf16),
            jax.ShapeDtypeStruct((LIVE, 1), f32),
            jax.ShapeDtypeStruct((rows, 2 * V), f32),
            jax.ShapeDtypeStruct((2 * Zh * R * R, R, 128), f32),
        ),
        in_specs=[SMEM, HBM, HBM] + [VMEM] * 11,
        out_specs=(VMEM,) * 4,
        scratch_shapes=[
            pltpu.VMEM((2, V, D), bf16),
            pltpu.VMEM((R, LIVE, 128), f32),
            pltpu.SemaphoreType.DMA((2,)),
        ],
        compiler_params=pltpu.CompilerParams(vmem_limit_bytes=28 << 20),
        cost_estimate=pl.CostEstimate(
            flops=4 * rows * V * D, bytes_accessed=4 * V * D, transcendentals=2 * rows * V
        ),
        name="forward",
    )(place, w0, w1, gain, *a, *b)


def split_tile(rows):
    place = lax.broadcasted_iota(jnp.int32, (16, 128), 0)
    tile = jnp.zeros((16, 128), f32)
    for i, row in enumerate(rows):
        for n in range(3):
            piece = row.astype(bf16).astype(f32)
            tile = jnp.where(place == 3 * i + n, piece, tile)
            row = row - piece
    return tile.astype(bf16)


def read_tile(tile, n):
    tile = tile.astype(f32)
    return [tile[3 * i : 3 * i + 1] + tile[3 * i + 1 : 3 * i + 2] + tile[3 * i + 2 : 3 * i + 3] for i in range(n)]


def soft_kernel(Zh, place_ref, w0_ref, w1_ref, every_ref, l_ref, n_ref, label_ref, live_ref, factor_ref, *refs):
    g_ref, ng_ref, side_ref, loss_ref, gain_ref, a_low, a_high, b_low, b_high = refs[:9]
    wa_ref, wb_ref, sems = refs[9:]
    V = w0_ref.shape[0]
    far = lax.rem(place_ref[0] + 2, R)
    copies = []
    for i, w in enumerate((w0_ref, w1_ref)):
        rows = pl.ds(i * V, V)
        copies.append(
            [pltpu.make_async_copy(w.at[:, pl.ds(0, Zh * R * 128)], wa_ref.at[rows], sems.at[0, i])]
        )
        for z in range(Zh):
            column = pl.multiple_of(((Zh + z) * R + far) * 128, 128)
            copies[-1].append(
                pltpu.make_async_copy(
                    w.at[:, pl.ds(column, 128)],
                    wb_ref.at[rows, pl.ds(z * 128, 128)],
                    sems.at[1 + z, i],
                )
            )
    for pair in copies:
        for copy in pair:
            copy.start()
    every = every_ref[...]
    best = jnp.max(every, axis=0)
    log_total = best + jnp.log(jnp.sum(jnp.exp(every - best[None]), axis=0))
    place = lax.broadcasted_iota(jnp.int32, (R, 128), 0)
    lane = lax.broadcasted_iota(jnp.int32, (1, 2 * V), 1)
    entry = jnp.where(lane < V, place_ref[2] + lane, place_ref[3] + lane - V).astype(f32)

    def block(p, sums):
        inner, target, loss = sums
        rows = pl.ds(pl.multiple_of(p * LIVE, 16), LIVE)
        distance = jnp.where(p < 2, p, 5 - p)
        here = lax.rem(place_ref[1] - distance + R, R)
        total = jnp.sum(jnp.where(place == here, log_total, 0.0), axis=0, keepdims=True)
        pick_row = lambda ref: jnp.sum(jnp.where(place == p, ref[...], 0.0), axis=0, keepdims=True)
        live = pick_row(live_ref)
        logits = l_ref[rows, :]
        match = to_column(pick_row(label_ref)) == entry
        grad = jnp.exp(logits - to_column(total)) - jnp.where(match, 1.0, 0.0)
        grad = grad * to_column(pick_row(factor_ref))
        g_ref[rows, :] = grad.astype(bf16)
        ng_ref[rows, pl.ds(w0_ref.shape[1], V)] = grad[:, V:].astype(bf16)
        line = to_row(jnp.sum(grad * logits, axis=1, keepdims=True))
        inner = jnp.where(place == p, line, inner)
        own = jnp.sum(jnp.where(match, logits, 0.0), axis=1, keepdims=True) * to_column(live)
        target = target + jnp.sum(own, axis=0, keepdims=True)
        loss = loss + jnp.sum(live * total, axis=1, keepdims=True)
        return inner, target, loss

    zero = jnp.zeros((1, 1), f32)
    inner, target, loss = lax.fori_loop(0, R, block, (jnp.zeros((R, 128), f32), zero, zero))
    for p in range(R):
        side_ref[p] = split_tile([inner[p : p + 1], jnp.broadcast_to(target, (1, 128))])
    loss_ref[...] = jnp.broadcast_to(loss, (1, 128))
    for pair in copies:
        for copy in pair:
            copy.wait()
    half = Zh // 2
    gain_ref[...] = jnp.zeros_like(gain_ref)
    part = jnp.dot(g_ref[(R - 1) * LIVE :, :], wa_ref[...], preferred_element_type=f32)
    gain = part * n_ref[(R - 1) * LIVE :, 0 : Zh * R * 128].astype(f32)
    gain = jnp.sum(gain, axis=0, keepdims=True)
    for t in range(Zh * R):
        at = t % (half * R) * LIVE
        gain_ref[t : t + 1, :] = gain[:, t * 128 : (t + 1) * 128]
        (a_low if t < half * R else a_high)[at : at + LIVE, :] = part[
            :, t * 128 : (t + 1) * 128
        ].astype(bf16)
    part = jnp.dot(g_ref[...], wb_ref[...], preferred_element_type=f32)
    for z in range(Zh):
        at = z % half * R * LIVE
        t = (Zh + z) * R + far
        block = part[:, z * 128 : (z + 1) * 128]
        (b_low if z < half else b_high)[at : at + R * LIVE, :] = block.astype(bf16)
        gain = block * n_ref[:, pl.ds(pl.multiple_of(t * 128, 128), 128)].astype(f32)
        gain_ref[pl.ds(t, 1), :] = jnp.sum(gain, axis=0, keepdims=True)
    a_low[Zh // 2 * R * LIVE :, :] = side_ref[R - 1]


def soft_rows(place, Zh, w0, w1, every, logits, normed, labels, live, factor):
    V = w0.shape[0]
    rows = logits.shape[0]
    half = Zh // 2 * R * LIVE
    shapes = [((rows, 2 * V), bf16), (normed.shape, bf16), ((R, 16, 128), bf16), ((1, 128), f32)]
    shapes += [((2 * Zh * R, 128), f32)]
    shapes += [((half + 16, 128), bf16)] + [((half, 128), bf16)] * 3
    return pl.pallas_call(
        functools.partial(soft_kernel, Zh),
        out_shape=tuple(jax.ShapeDtypeStruct(*shape) for shape in shapes),
        in_specs=[SMEM, HBM, HBM] + [VMEM] * 6,
        out_specs=(VMEM,) * len(shapes),
        scratch_shapes=[
            pltpu.VMEM((2 * V, Zh * R * 128), bf16),
            pltpu.VMEM((2 * V, Zh * 128), bf16),
            pltpu.SemaphoreType.DMA((1 + Zh, 2)),
        ],
        input_output_aliases={5: 1},
        compiler_params=pltpu.CompilerParams(vmem_limit_bytes=20 << 20),
        name="soft_rows",
    )(place, w0, w1, every, logits, normed, labels, live, factor)


def near_kernel(Zh, place_ref, w0_ref, w1_ref, side_ref, g_ref, n_ref, *refs):
    a0, a1, a3, b0, b1, b3, gain_ref, w_ref, scratch, sems = refs
    V = w0_ref.shape[0]
    copies = []
    wide = 2 * R * 128
    for q in range(4):
        for i, w in enumerate((w0_ref, w1_ref)):
            copies.append(
                pltpu.make_async_copy(
                    w.at[:, pl.ds(q * wide, wide)], w_ref.at[q, pl.ds(i * V, V)], sems.at[q, i]
                )
            )
    for copy in copies:
        copy.start()

    def arrived(q):
        for i in range(2):
            pltpu.make_async_copy(
                w0_ref.at[:, pl.ds(0, wide)], w_ref.at[q, pl.ds(i * V, V)], sems.at[q, i]
            ).wait()
        return w_ref[q]

    gain_ref[...] = jnp.zeros_like(gain_ref)

    def first(q, _):
        part = jnp.dot(g_ref[0 : 3 * LIVE, :], arrived(q), preferred_element_type=f32)
        gain = n_ref[0 : 3 * LIVE, pl.ds(pl.multiple_of(q * wide, 128), wide)].astype(f32)
        gain = jnp.sum(part * gain, axis=0, keepdims=True)
        for t in range(2 * R):
            at = pl.multiple_of((q * 2 * R + t) * LIVE, 16)
            gain_ref[pl.ds(q * 2 * R + t, 1), :] = gain[:, t * 128 : (t + 1) * 128]
            for p, ref in enumerate((a0, a1, a3)):
                ref[pl.ds(at, LIVE), :] = part[
                    p * LIVE : (p + 1) * LIVE, t * 128 : (t + 1) * 128
                ].astype(ref.dtype)
        return 0

    def second(q, _):
        scratch[...] = jnp.dot(g_ref[...], arrived(2 + q), preferred_element_type=f32)
        for z in range(2):
            at = pl.multiple_of((q * 2 + z) * (R * LIVE), 16)
            for k, ref in ((0, b0), (1, b1), (3, b3)):
                t = z * R + lax.rem(place_ref[0] + k, R)
                part = scratch[:, pl.ds(pl.multiple_of(t * 128, 128), 128)]
                ref[pl.ds(at, R * LIVE), :] = part.astype(ref.dtype)
                t = (Zh + q * 2) * R + t
                gain = n_ref[:, pl.ds(pl.multiple_of(t * 128, 128), 128)].astype(f32)
                gain_ref[pl.ds(t, 1), :] = jnp.sum(part * gain, axis=0, keepdims=True)
        return 0

    lax.fori_loop(0, 2, first, 0)
    lax.fori_loop(0, 2, second, 0)
    a1[Zh * R * LIVE :, :] = side_ref[1]
    a3[Zh * R * LIVE :, :] = side_ref[2]


def near_rows(place, Zh, w0, w1, side, g, normed):
    V = w0.shape[0]
    rows, block = g.shape[0], Zh * R * LIVE
    shapes = [(block, 128), (block + 16, 128), (block + 16, 128)] + [(block, 128)] * 3
    return pl.pallas_call(
        functools.partial(near_kernel, Zh),
        out_shape=(
            *(jax.ShapeDtypeStruct(shape, bf16) for shape in shapes),
            jax.ShapeDtypeStruct((2 * Zh * R, 128), f32),
        ),
        in_specs=[SMEM, HBM, HBM, VMEM, VMEM, VMEM],
        out_specs=(VMEM,) * 7,
        scratch_shapes=[
            pltpu.VMEM((4, 2 * V, 2 * R * 128), bf16),
            pltpu.VMEM((rows, 2 * R * 128), f32),
            pltpu.SemaphoreType.DMA((4, 2)),
        ],
        compiler_params=pltpu.CompilerParams(vmem_limit_bytes=28 << 20),
        name="near_rows",
    )(place, w0, w1, side, g, normed)


def two(value):
    high = value.astype(bf16)
    return high, (value - high.astype(f32)).astype(bf16)


def relay_kernel(up, down, low, high, *refs):
    half, block = high.shape[0], 2 * high.shape[0]
    up_out, down_out = refs[-2:] if len(refs) == 2 else refs[2:4]
    add = lambda a, b: (a.astype(f32) + b.astype(f32)).astype(bf16)
    up_out[0:half, :] = add(up[0:half, :], low[0:half, :])
    up_out[half:block, :] = up[half:block, :]
    down_out[0:half, :] = down[0:half, :]
    down_out[half:block, :] = add(down[half:block, :], high[...])
    if len(refs) > 2:
        mine, came = read_tile(up[block:, :], 2), read_tile(low[half:, :], 2)
        up_out[block : block + 16, :] = split_tile([a + b for a, b in zip(mine, came)])
        down_out[block : block + 16, :] = down[block:, :]
        gain = refs[0][...] + refs[1][...]
        refs[4][...] = gain
        lines = gain.shape[0]
        for i, piece in enumerate(two(gain)):
            for out in (up_out, down_out):
                at = block + 16 + i * lines
                out[at : at + lines, :] = piece


def relay(up, down, low, high, *gains):
    lines = gains[0].shape[0] if gains else 0
    shape = jax.ShapeDtypeStruct((up.shape[0] + 2 * lines, 128), bf16)
    shapes = (shape, shape) + ((jax.ShapeDtypeStruct((lines, 128), f32),) if gains else ())
    return pl.pallas_call(
        relay_kernel,
        out_shape=shapes,
        in_specs=[VMEM] * (4 + len(gains)),
        out_specs=(VMEM,) * len(shapes),
        compiler_params=pltpu.CompilerParams(vmem_limit_bytes=SCOPED),
        name="relay",
    )(up, down, low, high, *gains)


def turn_kernel(Zh, y_ref, side_ref, mine, far, a0, a1, a2, b0, b1, b2, *outs):
    block, part = Zh * R * LIVE, Zh * LIVE

    def one(z, _):
        to = pl.ds(pl.multiple_of(z * LIVE, 16), LIVE)
        for k in range(R):
            row = pl.multiple_of((z * R + lax.rem(y_ref[0] + k, R)) * LIVE, 16)
            rows = pl.ds(row, LIVE)
            total = a0[rows, :].astype(f32) + a1[rows, :].astype(f32) + a2[rows, :].astype(f32)
            outs[k][to, :] = total.astype(outs[k].dtype)
        for j in range(R):
            rows = pl.ds(pl.multiple_of((z * R + ORDER.index(j)) * LIVE, 16), LIVE)
            total = b0[rows, :].astype(f32) + b1[rows, :].astype(f32) + b2[rows, :].astype(f32)
            outs[R + j][to, :] = total.astype(outs[R + j].dtype)
        return 0

    lax.fori_loop(0, Zh, one, 0)
    tiles = [read_tile(t, 2) for t in (side_ref[0], a1[block : block + 16, :], a2[block : block + 16, :])]
    tile = split_tile([sum(rows) for rows in zip(*tiles)])
    outs[2 * R][...] = tile
    lines, gain_ref = mine.shape[0], outs[2 * R + 2]
    gain = mine[...] + far[...]
    for ref in (a1, a2):
        for i in range(2):
            at = block + 16 + i * lines
            gain = gain + ref[at : at + lines, :].astype(f32)
    gain_ref[...] = gain
    Z = 2 * Zh
    place = lax.broadcasted_iota(jnp.int32, (Z, 128), 0)
    for k in range(R):
        gain = jnp.zeros((Z, 128), f32)
        for z in range(Z):
            line = gain_ref[pl.ds(z * R + lax.rem(y_ref[0] + k, R), 1), :]
            gain = jnp.where(place == z, line, gain)
        if k == 0:
            outs[2 * R + 1][...] = gain
        else:
            outs[k][part : part + 16, :] = tile
            outs[k][part + 16 : part + 32, :] = jnp.concatenate(
                [piece.astype(f32) for piece in two(gain)]
            ).astype(bf16)


def turn_rows(y, Zh, side, mine, far, a, b):
    part = Zh * LIVE
    shapes = [((part, 128), f32)] + [((part + 32, 128), bf16)] * (R - 1)
    shapes += [((part, 128), f32)] + [((part, 128), bf16)] * (R - 1) + [((16, 128), bf16)]
    shapes += [((2 * Zh, 128), f32)]
    return pl.pallas_call(
        functools.partial(turn_kernel, Zh),
        out_shape=tuple(jax.ShapeDtypeStruct(*shape) for shape in shapes),
        in_specs=[SMEM] + [VMEM] * 9,
        out_specs=(VMEM,) * (2 * R + 2),
        scratch_shapes=[pltpu.VMEM(mine.shape, f32)],
        compiler_params=pltpu.CompilerParams(vmem_limit_bytes=SCOPED),
        name="turn_rows",
    )(y, side, mine, far, *a, *b)


def gather_kernel(Zh, side_ref, gain_ref, *refs):
    a, b, out = refs[:R], refs[R : 2 * R], refs[2 * R]
    at, Z = Zh * LIVE, 2 * Zh
    tiles = [read_tile(side_ref[...], 2)] + [read_tile(ref[at : at + 16, :], 2) for ref in a[1:]]
    lines = [sum(rows) for rows in zip(*tiles)]
    gain = gain_ref[...]
    for ref in a[1:]:
        pieces = ref[at + 16 : at + 32, :].astype(f32)
        gain = gain + pieces[0:Z] + pieces[Z : 2 * Z]
    for z in range(Z):
        out[z, LIVE:128, :] = split_tile(lines + [gain[z : z + 1]])
    for half, refs in enumerate((a, b)):

        def one(z, _):
            rows = pl.ds(pl.multiple_of(z * LIVE, 16), LIVE)
            total = refs[0][rows, :]
            for ref in refs[1:]:
                total = total + ref[rows, :].astype(f32)
            out[half * Zh + z, 0:LIVE, :] = total.astype(bf16)
            return 0

        lax.fori_loop(0, Zh, one, 0)


def gather_rows(Zh, side, gain, a, b):
    return pl.pallas_call(
        functools.partial(gather_kernel, Zh),
        out_shape=jax.ShapeDtypeStruct((2 * Zh, 128, 128), bf16),
        in_specs=[VMEM] * (2 * R + 2),
        out_specs=VMEM,
        compiler_params=pltpu.CompilerParams(vmem_limit_bytes=SCOPED),
        name="gather_rows",
    )(side, gain, *a, *b)


def prepare_kernel(vocab, hidden_ref, gain_ref, target_ref, start_ref, live_ref, out_ref, meta_ref):
    gain = gain_ref[...]
    high = gain.astype(bf16).astype(f32)
    middle = (gain - high).astype(bf16).astype(f32)
    low = gain - high - middle
    row = lax.broadcasted_iota(jnp.int32, (16, 128), 0)
    tile = jnp.where(row == 0, high, jnp.where(row == 1, middle, jnp.where(row == 2, low, 0.0)))
    for z in range(out_ref.shape[0]):
        out_ref[z, 0:LIVE, :] = hidden_ref[0:LIVE, :]
        out_ref[z, LIVE:128, :] = tile.astype(bf16)
    starts = start_ref[...]
    upto = lax.broadcasted_iota(jnp.int32, (128, 128), 0) <= lax.broadcasted_iota(
        jnp.int32, (128, 128), 1
    )
    flags = jnp.broadcast_to(starts.astype(f32), (16, 128)).astype(bf16)
    order = jnp.dot(flags, upto.astype(f32).astype(bf16), preferred_element_type=f32)
    order = order[0:1].astype(jnp.int32) - 1
    sentinel = vocab - 1 - jnp.clip(order, 0, NSENT - 1)
    label = jnp.where(starts > 0, sentinel, target_ref[...])
    pieces = (label >> 16, (label >> 8) & 255, label & 255, live_ref[...])
    tile = jnp.zeros((16, 128), f32)
    for i, piece in enumerate(pieces):
        tile = jnp.where(row == i, piece.astype(f32), tile)
    meta_ref[...] = tile.astype(bf16)


def prepare(Z, vocab, hidden, norm_gain, targets, span_starts, live_rows):
    line = lambda a: a.reshape(1, 128)
    return pl.pallas_call(
        functools.partial(prepare_kernel, vocab),
        out_shape=(
            jax.ShapeDtypeStruct((Z, 128, 128), bf16),
            jax.ShapeDtypeStruct((16, 128), bf16),
        ),
        in_specs=[VMEM] * 5,
        out_specs=(VMEM, VMEM),
        name="prepare",
    )(hidden, line(norm_gain), line(targets), line(span_starts), line(live_rows))


def meta_kernel(at, w_ref, *refs):
    tiles, a_refs = refs[:R], refs[R : 2 * R]
    label_ref, live_ref, factor_ref, total_ref, gain_ref = refs[2 * R :]
    Z = gain_ref.shape[0] // R
    for k, ref in enumerate(a_refs):
        for z in range(Z):
            pieces = ref[at + z * 16 : at + (z + 1) * 16, :].astype(f32)
            gain_ref[k * Z + z : k * Z + z + 1, :] = pieces[0:1] + pieces[1:2] + pieces[2:3]
    place = lax.broadcasted_iota(jnp.int32, (R, 128), 0)
    labels, live, total = jnp.zeros((R, 128), f32), jnp.zeros((R, 128), f32), jnp.zeros((1, 1), f32)
    for p, j in enumerate(ORDER):
        tile = tiles[j][at : at + 16, :].astype(f32)
        label = tile[0:1] * 65536 + tile[1:2] * 256 + tile[2:3]
        labels = jnp.where(place == p, label, labels)
        live = jnp.where(place == p, tile[3:4], live)
        total = total + jnp.sum(tile[3:4] + tile[4:5], axis=1, keepdims=True)
    label_ref[...] = labels
    live_ref[...] = live
    factor_ref[...] = live * (loss_scale / total)
    total_ref[...] = jnp.broadcast_to(total, (1, 128))


def read_meta(at, weight, Z, blocks, a_blocks):
    line = jax.ShapeDtypeStruct((R, 128), f32)
    return pl.pallas_call(
        functools.partial(meta_kernel, at),
        out_shape=(
            line,
            line,
            line,
            jax.ShapeDtypeStruct((1, 128), f32),
            jax.ShapeDtypeStruct((R * Z, 128), f32),
        ),
        in_specs=[VMEM] * (1 + 2 * R),
        out_specs=(VMEM,) * 5,
        compiler_params=pltpu.CompilerParams(vmem_limit_bytes=SCOPED),
        name="read_meta",
    )(weight, *blocks, *a_blocks)


def outer_kernel(g_ref, h_ref, n_ref, m_ref, out_ref, g_turned, h_turned):
    V = h_ref.shape[1]

    @pl.when(pl.program_id(0) == 0)
    def _():
        g_turned[...] = g_ref[:, 0:V].astype(f32).T.astype(bf16)
        h_turned[...] = h_ref[...].astype(f32).T.astype(bf16)

    total = jnp.dot(g_turned[...], n_ref[...], preferred_element_type=f32)
    total = total + jnp.dot(h_turned[...], m_ref[...], preferred_element_type=f32)
    out_ref[...] = total.astype(bf16)


def outer(g, ours, theirs, D):
    rows, V = g.shape[0], g.shape[1] // 2
    part = pl.BlockSpec((rows, V), lambda i: (0, i))
    return pl.pallas_call(
        outer_kernel,
        grid=(D // V,),
        out_shape=jax.ShapeDtypeStruct((V, D), bf16),
        in_specs=[
            pl.BlockSpec(g.shape, lambda i: (0, 0)),
            pl.BlockSpec((rows, V), lambda i: (0, D // V)),
            part,
            part,
        ],
        out_specs=pl.BlockSpec((V, V), lambda i: (0, i)),
        scratch_shapes=[pltpu.VMEM((V, rows), bf16)] * 2,
        compiler_params=pltpu.CompilerParams(vmem_limit_bytes=SCOPED),
        cost_estimate=pl.CostEstimate(
            flops=4 * rows * V * D, bytes_accessed=8 * V * D, transcendentals=0
        ),
        name="outer",
    )(g, theirs, ours, theirs)


def last_kernel(sums_ref, came_ref, total_ref, gain_ref, loss_ref):
    sums = sums_ref[...] + came_ref[...]
    gain_ref[...] = sums[0:1]
    loss_ref[...] = sums[1:2, 0:1] / total_ref[:, 0:1]


def last(sums, came, total):
    return pl.pallas_call(
        last_kernel,
        out_shape=(jax.ShapeDtypeStruct((1, 128), f32), jax.ShapeDtypeStruct((1, 1), f32)),
        in_specs=[VMEM] * 3,
        out_specs=(VMEM, VMEM),
        name="last",
    )(sums, came, total)


def finish_kernel(D, loss_ref, total_ref, hidden_ref, gain_ref, inv_ref, out_ref, sums_ref):
    total = total_ref[0].astype(f32)
    for z in range(1, total_ref.shape[0]):
        total = total + total_ref[z].astype(f32)
    inner, target, gain = read_tile(total[LIVE:128], 3)
    total = total[0:LIVE]
    inner = to_column(inner)
    inv = inv_ref[...]
    activation = hidden_ref[0:LIVE, :].astype(f32)
    grad = inv * (total * gain_ref[...]) - activation * (inv * inv * (inner / D))
    out_ref[0:LIVE, :] = grad.astype(bf16)
    out_ref[LIVE:128, :] = jnp.zeros((128 - LIVE, 128), bf16)
    sums_ref[0:1, :] = gain / gain_ref[...]
    sums_ref[1:2, :] = loss_ref[...] - target


def finish(D, loss, total, hidden, norm_gain, inv_rms):
    return pl.pallas_call(
        functools.partial(finish_kernel, D),
        out_shape=(jax.ShapeDtypeStruct((128, 128), bf16), jax.ShapeDtypeStruct((2, 128), f32)),
        in_specs=[VMEM] * 5,
        out_specs=(VMEM, VMEM),
        name="finish",
    )(loss, total, hidden, norm_gain.reshape(1, 128), inv_rms)


def body(hidden, norm_gain, head_weight, targets, span_starts, live_rows):
    Z, Y, X = (lax.axis_size(a) for a in "zyx")
    Zh = Z // 2
    V, D = head_weight.shape
    vocab = V * 2 * Z * Y * X
    c, z, y, x = (lax.axis_index(a) for a in "czyx")
    spot = (z * Y + y) * X + x
    first, second = (c * (Z * Y * X) + spot) * V, ((1 - c) * (Z * Y * X) + spot) * V
    place = jnp.stack([y, x, first, second]).astype(jnp.int32)

    live_other = shift(live_rows, "c", 1)
    weight_other = shift(head_weight, "c", 1)

    block, meta = prepare(Z, vocab, hidden, norm_gain, targets, span_starts, live_rows)
    block = lax.all_to_all(block, "z", 0, 0)
    meta = meta + jnp.pad(live_other[None].astype(bf16), ((4, 11), (0, 0)))
    block, weight_other, meta = lax.optimization_barrier((block, weight_other, meta))

    a_block = jnp.concatenate(
        [block[:Zh, :LIVE].reshape(-1, 128), block[:, LIVE:].reshape(-1, 128)]
    )
    b_block = jnp.concatenate([block[Zh:, :LIVE].reshape(-1, 128), meta])
    a_blocks = [a_block] + [shift(a_block, "y", k) for k in range(1, R)]
    b_blocks = [b_block] + [shift(b_block, "x", k) for k in range(1, R)]
    a_all = ring_gather(jnp.concatenate([a[: Zh * LIVE] for a in a_blocks]), "x")
    b_all = ring_gather(jnp.concatenate([b[: Zh * LIVE] for b in b_blocks]), "y")
    labels, live, factor, live_total, gain = read_meta(
        Zh * LIVE, head_weight, Z, b_blocks, a_blocks
    )
    a_all, b_all, labels, live, factor, gain = lax.optimization_barrier(
        (a_all, b_all, labels, live, factor, gain)
    )

    weights = (head_weight, weight_other)
    normed, inv_rms, logits, share = forward(place, Zh, *weights, gain, a_all, b_all)
    every = lax.all_to_all(share, ("z", "y", "x"), 0, 0)
    g, normed, side, loss, gain_far, a_low, a_high, b_low, b_high = soft_rows(
        place, Zh, *weights, every, logits, normed, labels, live, factor
    )

    a_low, a_high = shift(a_low, "x", 1), shift(a_high, "x", -1)
    b_low, b_high = shift(b_low, "y", 1), shift(b_high, "y", -1)
    near = near_rows(place, Zh, *weights, side, g, normed)
    near, a_low, a_high, b_low, b_high, g, normed = lax.optimization_barrier(
        (near, a_low, a_high, b_low, b_high, g, normed)
    )
    theirs = shift(normed, "c", 1)
    a0, a1, a3, b0, b1, b3, gain_near = near
    a_up, a_down, gain = relay(a3, a1, a_low, a_high, gain_far, gain_near)
    b_up, b_down = relay(b1, b3, b_low, b_high)
    a_in = shift(a_up, "x", 1), shift(a_down, "x", -1)
    b_in = shift(b_up, "y", 1), shift(b_down, "y", -1)
    gain_in = shift(gain, "x", 2)
    weight_grad = outer(g, normed, theirs, D)
    a_in, b_in, weight_grad = lax.optimization_barrier((a_in, b_in, weight_grad))
    outs = turn_rows(place, Zh, side, gain, gain_in, (a0, *a_in), (b0, *b_in))
    a_sums = [outs[0]] + [shift(outs[k], "y", k) for k in range(1, R)]
    b_sums = [outs[R]] + [shift(outs[R + k], "x", -k) for k in range(1, R)]
    total = gather_rows(Zh, outs[2 * R], outs[2 * R + 1], a_sums, b_sums)
    total = lax.all_to_all(total, "z", 0, 0)
    hidden_grad, sums = finish(D, loss, total, hidden, norm_gain, inv_rms)

    gain_grad, mean_loss = last(sums, shift(sums, "c", 1), live_total)
    gain_grad, mean_loss = gain_grad.reshape(128), mean_loss.reshape(())
    return (hidden_grad, gain_grad, weight_grad, mean_loss)


def solution(mesh):
    S, T, X = mesh.devices.shape
    split = Mesh(mesh.devices.reshape(S, T // R, R, X), ("c", "z", "y", "x"))
    rows, features, entries = ("c", "x"), ("z", "y"), ("c", "z", "y", "x")
    return jax.shard_map(
        body,
        mesh=split,
        in_specs=(P(rows, features), P(features), P(entries, None), P(rows), P(rows), P(rows)),
        out_specs=(P(rows, features), P(features), P(entries, None), P()),
        check_vma=False,
    )
```

```python
import functools
import jax
import jax.numpy as jnp
from jax import lax
from jax.experimental import pallas as pl
from jax.experimental.pallas import tpu as pltpu
from jax.sharding import Mesh, PartitionSpec as P

NSENT = 100
LIVE = 112
loss_scale = 8192.0
epsilon = 1e-06
f32, bf16 = jnp.float32, jnp.bfloat16
VMEM = pl.BlockSpec(memory_space=pltpu.VMEM)
SMEM = pl.BlockSpec(memory_space=pltpu.SMEM)
HBM = pl.BlockSpec(memory_space=pltpu.HBM)
R = 4
ORDER = (0, 1, 3, 2)
SCOPED = 16 << 20


def shift(x, axis, k):
    n = lax.axis_size(axis)
    return lax.ppermute(x, axis, [(i, (i + k) % n) for i in range(n)])


def ring_gather(block, axis):
    one = shift(block, axis, 1)
    return block, one, shift(block, axis, -1), shift(one, axis, 1)


PARTS = ((0, 0, 4), (1, 0, 4), (3, 0, 4), (2, 0, 4))


def spot_of(j):
    return jnp.where(j < 2, j, 5 - j)


def same():
    return lax.broadcasted_iota(jnp.int32, (LIVE, 128), 0) == lax.broadcasted_iota(
        jnp.int32, (LIVE, 128), 1
    )


def to_row(column):
    return jnp.sum(jnp.where(same(), column, 0.0), axis=0, keepdims=True)


def to_column(row):
    return jnp.sum(jnp.where(same(), row, 0.0), axis=1, keepdims=True)


def place_of(x, p):
    return lax.rem(x - ORDER[p] + R, R)


def forward_kernel(Zh, place_ref, w0_ref, w1_ref, gain_ref, *refs):
    a_refs, b_refs = refs[:R], refs[R : 2 * R]
    n_ref, inv_ref, l_ref, share_ref, w_ref, total_ref, w_sems = refs[2 * R :]
    Z = 2 * Zh
    V = w0_ref.shape[0]
    copies = [
        pltpu.make_async_copy(w, w_ref.at[i], w_sems.at[i]) for i, w in enumerate((w0_ref, w1_ref))
    ]
    for copy in copies:
        copy.start()

    def load(ref, i, z):
        at = pl.multiple_of((i * Zh + z) * LIVE, 16)
        return ref[pl.ds(at, LIVE), :].astype(f32)

    def squares(ref, i):
        def add(z, total):
            block = load(ref, i, z)
            return total + block * block

        return lax.fori_loop(0, Zh, add, jnp.zeros((LIVE, 128), f32), unroll=True)

    total_ref[...] = jnp.zeros_like(total_ref)
    for ref, (j, first, last) in zip(a_refs, PARTS):
        add = lambda i, total, ref=ref: total + squares(ref, i)
        p = ORDER.index(j)
        total_ref[p] = lax.fori_loop(0, last - first, add, total_ref[p])
    for ref, (_, first, last) in zip(b_refs, PARTS):

        def add(i, _, ref=ref, first=first):
            p = spot_of(first + i)
            total_ref[p] = total_ref[p] + squares(ref, i)
            return 0

        lax.fori_loop(0, last - first, add, 0)
    for p in range(R):
        mean_square = jnp.sum(total_ref[p], axis=1, keepdims=True) / (Z * R * 128)
        inv = lax.rsqrt(mean_square + epsilon)
        if p == 0:
            inv_ref[...] = inv
        total_ref[p] = jnp.broadcast_to(inv, (LIVE, 128))

    def scale(ref, i, k, p, half):
        inv = total_ref[p]
        y = lax.rem(place_ref[0] - k + R, R)
        rows = pl.ds(pl.multiple_of(p * LIVE, 16), LIVE)

        def one(z, _):
            t = half * Zh + z
            column = pl.multiple_of((t * R + y) * 128, 128)
            n_ref[rows, pl.ds(column, 128)] = (
                load(ref, i, z) * inv * gain_ref[pl.ds(k * Z + t, 1), :]
            ).astype(bf16)
            return 0

        lax.fori_loop(0, Zh, one, 0, unroll=True)

    for ref, (j, first, last) in zip(a_refs, PARTS):

        def one(i, _, ref=ref, j=j, first=first):
            scale(ref, i, first + i, ORDER.index(j), 0)
            return 0

        lax.fori_loop(0, last - first, one, 0)
    for ref, (k, first, last) in zip(b_refs, PARTS):

        def one(i, _, ref=ref, k=k, first=first):
            scale(ref, i, k, spot_of(first + i), 1)
            return 0

        lax.fori_loop(0, last - first, one, 0)

    def logits_of(q, _):
        pltpu.make_async_copy(w0_ref, w_ref.at[q], w_sems.at[q]).wait()
        l_ref[:, pl.ds(pl.multiple_of(q * V, V), V)] = lax.dot_general(
            n_ref[:, 0 : w_ref.shape[2]], w_ref[q], (((1,), (1,)), ((), ())), preferred_element_type=f32
        )
        return 0

    lax.fori_loop(0, 2, logits_of, 0)
    place = lax.broadcasted_iota(jnp.int32, (R, 128), 0)
    share = jnp.zeros((R, 128), f32)
    for p in range(R):
        logits = l_ref[p * LIVE : (p + 1) * LIVE, :]
        top = jnp.max(logits, axis=1, keepdims=True)
        here = top + jnp.log(jnp.sum(jnp.exp(logits - top), axis=1, keepdims=True))
        share = jnp.where(place == place_of(place_ref[1], p), to_row(here), share)
    share_ref[...] = jnp.broadcast_to(share[None], share_ref.shape)


def forward(place, Zh, w0, w1, gain, a, b):
    V, D = w0.shape
    rows = R * LIVE
    return pl.pallas_call(
        functools.partial(forward_kernel, Zh),
        out_shape=(
            jax.ShapeDtypeStruct((rows, D + V), bf16),
            jax.ShapeDtypeStruct((LIVE, 1), f32),
            jax.ShapeDtypeStruct((rows, 2 * V), f32),
            jax.ShapeDtypeStruct((2 * Zh * R * R, R, 128), f32),
        ),
        in_specs=[SMEM, HBM, HBM] + [VMEM] * (1 + 2 * R),
        out_specs=(VMEM,) * 4,
        scratch_shapes=[
            pltpu.VMEM((2, V, D), bf16),
            pltpu.VMEM((R, LIVE, 128), f32),
            pltpu.SemaphoreType.DMA((2,)),
        ],
        compiler_params=pltpu.CompilerParams(vmem_limit_bytes=28 << 20),
        cost_estimate=pl.CostEstimate(
            flops=4 * rows * V * D, bytes_accessed=4 * V * D, transcendentals=2 * rows * V
        ),
        name="forward",
    )(place, w0, w1, gain, *a, *b)


def split_tile(rows):
    place = lax.broadcasted_iota(jnp.int32, (16, 128), 0)
    tile = jnp.zeros((16, 128), f32)
    for i, row in enumerate(rows):
        for n in range(3):
            piece = row.astype(bf16).astype(f32)
            tile = jnp.where(place == 3 * i + n, piece, tile)
            row = row - piece
    return tile.astype(bf16)


def read_tile(tile, n):
    tile = tile.astype(f32)
    return [tile[3 * i : 3 * i + 1] + tile[3 * i + 1 : 3 * i + 2] + tile[3 * i + 2 : 3 * i + 3] for i in range(n)]


def soft_kernel(Zh, place_ref, w0_ref, w1_ref, every_ref, l_ref, n_ref, label_ref, live_ref, factor_ref, *refs):
    g_ref, ng_ref, side_ref, loss_ref, gain_ref, a_low, a_high, b_low, b_high = refs[:9]
    wa_ref, wb_ref, sems = refs[9:]
    V = w0_ref.shape[0]
    far = lax.rem(place_ref[0] + 2, R)
    copies = []
    for i, w in enumerate((w0_ref, w1_ref)):
        rows = pl.ds(i * V, V)
        copies.append(
            [pltpu.make_async_copy(w.at[:, pl.ds(0, Zh * R * 128)], wa_ref.at[rows], sems.at[0, i])]
        )
        for z in range(Zh):
            column = pl.multiple_of(((Zh + z) * R + far) * 128, 128)
            copies[-1].append(
                pltpu.make_async_copy(
                    w.at[:, pl.ds(column, 128)],
                    wb_ref.at[rows, pl.ds(z * 128, 128)],
                    sems.at[1 + z, i],
                )
            )
    for pair in copies:
        for copy in pair:
            copy.start()
    every = every_ref[...]
    best = jnp.max(every, axis=0)
    log_total = best + jnp.log(jnp.sum(jnp.exp(every - best[None]), axis=0))
    place = lax.broadcasted_iota(jnp.int32, (R, 128), 0)
    lane = lax.broadcasted_iota(jnp.int32, (1, 2 * V), 1)
    entry = jnp.where(lane < V, place_ref[2] + lane, place_ref[3] + lane - V).astype(f32)

    def block(p, sums):
        inner, target, loss = sums
        rows = pl.ds(pl.multiple_of(p * LIVE, 16), LIVE)
        distance = jnp.where(p < 2, p, 5 - p)
        here = lax.rem(place_ref[1] - distance + R, R)
        total = jnp.sum(jnp.where(place == here, log_total, 0.0), axis=0, keepdims=True)
        pick_row = lambda ref: jnp.sum(jnp.where(place == p, ref[...], 0.0), axis=0, keepdims=True)
        live = pick_row(live_ref)
        logits = l_ref[rows, :]
        match = to_column(pick_row(label_ref)) == entry
        grad = jnp.exp(logits - to_column(total)) - jnp.where(match, 1.0, 0.0)
        grad = grad * to_column(pick_row(factor_ref))
        g_ref[rows, :] = grad.astype(bf16)
        ng_ref[rows, pl.ds(w0_ref.shape[1], V)] = grad[:, V:].astype(bf16)
        line = to_row(jnp.sum(grad * logits, axis=1, keepdims=True))
        inner = jnp.where(place == p, line, inner)
        own = jnp.sum(jnp.where(match, logits, 0.0), axis=1, keepdims=True) * to_column(live)
        target = target + jnp.sum(own, axis=0, keepdims=True)
        loss = loss + jnp.sum(live * total, axis=1, keepdims=True)
        return inner, target, loss

    zero = jnp.zeros((1, 1), f32)
    inner, target, loss = lax.fori_loop(0, R, block, (jnp.zeros((R, 128), f32), zero, zero))
    for p in range(R):
        side_ref[p] = split_tile([inner[p : p + 1], jnp.broadcast_to(target, (1, 128))])
    loss_ref[...] = jnp.broadcast_to(loss, (1, 128))
    for pair in copies:
        for copy in pair:
            copy.wait()
    half = Zh // 2
    gain_ref[...] = jnp.zeros_like(gain_ref)
    part = jnp.dot(g_ref[(R - 1) * LIVE :, :], wa_ref[...], preferred_element_type=f32)
    gain = part * n_ref[(R - 1) * LIVE :, 0 : Zh * R * 128].astype(f32)
    gain = jnp.sum(gain, axis=0, keepdims=True)
    for t in range(Zh * R):
        at = t % (half * R) * LIVE
        gain_ref[t : t + 1, :] = gain[:, t * 128 : (t + 1) * 128]
        (a_low if t < half * R else a_high)[at : at + LIVE, :] = part[
            :, t * 128 : (t + 1) * 128
        ].astype(bf16)
    part = jnp.dot(g_ref[...], wb_ref[...], preferred_element_type=f32)
    for z in range(Zh):
        at = z % half * R * LIVE
        t = (Zh + z) * R + far
        block = part[:, z * 128 : (z + 1) * 128]
        (b_low if z < half else b_high)[at : at + R * LIVE, :] = block.astype(bf16)
        gain = block * n_ref[:, pl.ds(pl.multiple_of(t * 128, 128), 128)].astype(f32)
        gain_ref[pl.ds(t, 1), :] = jnp.sum(gain, axis=0, keepdims=True)
    a_low[Zh // 2 * R * LIVE :, :] = side_ref[R - 1]


def soft_rows(place, Zh, w0, w1, every, logits, normed, labels, live, factor):
    V = w0.shape[0]
    rows = logits.shape[0]
    half = Zh // 2 * R * LIVE
    shapes = [((rows, 2 * V), bf16), (normed.shape, bf16), ((R, 16, 128), bf16), ((1, 128), f32)]
    shapes += [((2 * Zh * R, 128), f32)]
    shapes += [((half + 16, 128), bf16)] + [((half, 128), bf16)] * 3
    return pl.pallas_call(
        functools.partial(soft_kernel, Zh),
        out_shape=tuple(jax.ShapeDtypeStruct(*shape) for shape in shapes),
        in_specs=[SMEM, HBM, HBM] + [VMEM] * 6,
        out_specs=(VMEM,) * len(shapes),
        scratch_shapes=[
            pltpu.VMEM((2 * V, Zh * R * 128), bf16),
            pltpu.VMEM((2 * V, Zh * 128), bf16),
            pltpu.SemaphoreType.DMA((1 + Zh, 2)),
        ],
        input_output_aliases={5: 1},
        compiler_params=pltpu.CompilerParams(vmem_limit_bytes=20 << 20),
        name="soft_rows",
    )(place, w0, w1, every, logits, normed, labels, live, factor)


def near_kernel(Zh, place_ref, w0_ref, w1_ref, side_ref, g_ref, n_ref, *refs):
    a_refs, b_refs, (gain_ref, wa_ref, wb_ref, sems) = refs[:3], refs[3:6], refs[6:]
    V = w0_ref.shape[0]
    wide = Zh * R * 128
    towards = [lax.rem(place_ref[0] + k, R) for k in (0, 1, 3)]
    first, second = [], []
    for i, w in enumerate((w0_ref, w1_ref)):
        rows = pl.ds(i * V, V)
        first.append(pltpu.make_async_copy(w.at[:, pl.ds(0, wide)], wa_ref.at[rows], sems.at[0, i]))
        for n in range(3 * Zh):
            column = pl.multiple_of(((Zh + n // 3) * R + towards[n % 3]) * 128, 128)
            second.append(
                pltpu.make_async_copy(
                    w.at[:, pl.ds(column, 128)],
                    wb_ref.at[rows, pl.ds(n * 128, 128)],
                    sems.at[1 + n, i],
                )
            )
    for copy in first + second:
        copy.start()
    gain_ref[...] = jnp.zeros_like(gain_ref)
    for copy in first:
        copy.wait()
    part = jnp.dot(g_ref[0 : 3 * LIVE, :], wa_ref[...], preferred_element_type=f32)
    gain = part * n_ref[0 : 3 * LIVE, 0:wide].astype(f32)
    gain = jnp.sum(gain, axis=0, keepdims=True)
    for t in range(Zh * R):
        lanes = slice(t * 128, (t + 1) * 128)
        gain_ref[t : t + 1, :] = gain[:, lanes]
        for p, ref in enumerate(a_refs):
            ref[t * LIVE : (t + 1) * LIVE, :] = part[p * LIVE : (p + 1) * LIVE, lanes].astype(bf16)
    for p, ref in enumerate(a_refs[1:]):
        ref[Zh * R * LIVE :, :] = side_ref[p + 1]
    for copy in second:
        copy.wait()
    part = jnp.dot(g_ref[...], wb_ref[...], preferred_element_type=f32)
    for n in range(3 * Zh):
        z = n // 3
        t = (Zh + z) * R + towards[n % 3]
        block = part[:, n * 128 : (n + 1) * 128]
        b_refs[n % 3][z * R * LIVE : (z + 1) * R * LIVE, :] = block.astype(bf16)
        gain = block * n_ref[:, pl.ds(pl.multiple_of(t * 128, 128), 128)].astype(f32)
        gain_ref[pl.ds(t, 1), :] = jnp.sum(gain, axis=0, keepdims=True)


def near_rows(place, Zh, w0, w1, side, g, normed):
    V = w0.shape[0]
    rows, block = g.shape[0], Zh * R * LIVE
    shapes = [(block, 128), (block + 16, 128), (block + 16, 128)] + [(block, 128)] * 3
    return pl.pallas_call(
        functools.partial(near_kernel, Zh),
        out_shape=(
            *(jax.ShapeDtypeStruct(shape, bf16) for shape in shapes),
            jax.ShapeDtypeStruct((2 * Zh * R, 128), f32),
        ),
        in_specs=[SMEM, HBM, HBM, VMEM, VMEM, VMEM],
        out_specs=(VMEM,) * 7,
        scratch_shapes=[
            pltpu.VMEM((2 * V, Zh * R * 128), bf16),
            pltpu.VMEM((2 * V, 3 * Zh * 128), bf16),
            pltpu.SemaphoreType.DMA((1 + 3 * Zh, 2)),
        ],
        compiler_params=pltpu.CompilerParams(vmem_limit_bytes=24 << 20),
        name="near_rows",
    )(place, w0, w1, side, g, normed)


def two(value):
    high = value.astype(bf16)
    return high, (value - high.astype(f32)).astype(bf16)


def relay_kernel(up, down, low, high, *refs):
    half, block = high.shape[0], 2 * high.shape[0]
    up_out, down_out = refs[-2:] if len(refs) == 2 else refs[2:4]
    add = lambda a, b: (a.astype(f32) + b.astype(f32)).astype(bf16)
    up_out[0:half, :] = add(up[0:half, :], low[0:half, :])
    up_out[half:block, :] = up[half:block, :]
    down_out[0:half, :] = down[0:half, :]
    down_out[half:block, :] = add(down[half:block, :], high[...])
    if len(refs) > 2:
        mine, came = read_tile(up[block:, :], 2), read_tile(low[half:, :], 2)
        up_out[block : block + 16, :] = split_tile([a + b for a, b in zip(mine, came)])
        down_out[block : block + 16, :] = down[block:, :]
        gain = refs[0][...] + refs[1][...]
        refs[4][...] = gain
        lines = gain.shape[0]
        for i, piece in enumerate(two(gain)):
            for out in (up_out, down_out):
                at = block + 16 + i * lines
                out[at : at + lines, :] = piece


def relay(up, down, low, high, *gains):
    lines = gains[0].shape[0] if gains else 0
    shape = jax.ShapeDtypeStruct((up.shape[0] + 2 * lines, 128), bf16)
    shapes = (shape, shape) + ((jax.ShapeDtypeStruct((lines, 128), f32),) if gains else ())
    return pl.pallas_call(
        relay_kernel,
        out_shape=shapes,
        in_specs=[VMEM] * (4 + len(gains)),
        out_specs=(VMEM,) * len(shapes),
        compiler_params=pltpu.CompilerParams(vmem_limit_bytes=SCOPED),
        name="relay",
    )(up, down, low, high, *gains)


def turn_kernel(Zh, y_ref, side_ref, mine, far, a0, a1, a2, b0, b1, b2, *outs):
    block, part = Zh * R * LIVE, Zh * LIVE

    def one(z, _):
        to = pl.ds(pl.multiple_of(z * LIVE, 16), LIVE)
        for k in range(R):
            row = pl.multiple_of((z * R + lax.rem(y_ref[0] + k, R)) * LIVE, 16)
            rows = pl.ds(row, LIVE)
            total = a0[rows, :].astype(f32) + a1[rows, :].astype(f32) + a2[rows, :].astype(f32)
            outs[k][to, :] = total.astype(outs[k].dtype)
        for j in range(R):
            rows = pl.ds(pl.multiple_of((z * R + ORDER.index(j)) * LIVE, 16), LIVE)
            total = b0[rows, :].astype(f32) + b1[rows, :].astype(f32) + b2[rows, :].astype(f32)
            outs[R + j][to, :] = total.astype(outs[R + j].dtype)
        return 0

    lax.fori_loop(0, Zh, one, 0)
    tiles = [read_tile(t, 2) for t in (side_ref[0], a1[block : block + 16, :], a2[block : block + 16, :])]
    tile = split_tile([sum(rows) for rows in zip(*tiles)])
    outs[2 * R][...] = tile
    lines, gain_ref = mine.shape[0], outs[2 * R + 2]
    gain = mine[...] + far[...]
    for ref in (a1, a2):
        for i in range(2):
            at = block + 16 + i * lines
            gain = gain + ref[at : at + lines, :].astype(f32)
    gain_ref[...] = gain
    Z = 2 * Zh
    place = lax.broadcasted_iota(jnp.int32, (Z, 128), 0)
    for k in range(R):
        gain = jnp.zeros((Z, 128), f32)
        for z in range(Z):
            line = gain_ref[pl.ds(z * R + lax.rem(y_ref[0] + k, R), 1), :]
            gain = jnp.where(place == z, line, gain)
        if k == 0:
            outs[2 * R + 1][...] = gain
        else:
            outs[k][part : part + 16, :] = tile
            outs[k][part + 16 : part + 32, :] = jnp.concatenate(
                [piece.astype(f32) for piece in two(gain)]
            ).astype(bf16)


def turn_rows(y, Zh, side, mine, far, a, b):
    part = Zh * LIVE
    shapes = [((part, 128), f32)] + [((part + 32, 128), bf16)] * (R - 1)
    shapes += [((part, 128), f32)] + [((part, 128), bf16)] * (R - 1) + [((16, 128), bf16)]
    shapes += [((2 * Zh, 128), f32)]
    return pl.pallas_call(
        functools.partial(turn_kernel, Zh),
        out_shape=tuple(jax.ShapeDtypeStruct(*shape) for shape in shapes),
        in_specs=[SMEM] + [VMEM] * 9,
        out_specs=(VMEM,) * (2 * R + 2),
        scratch_shapes=[pltpu.VMEM(mine.shape, f32)],
        compiler_params=pltpu.CompilerParams(vmem_limit_bytes=SCOPED),
        name="turn_rows",
    )(y, side, mine, far, *a, *b)


def gather_kernel(Zh, side_ref, gain_ref, *refs):
    a, b, out = refs[:R], refs[R : 2 * R], refs[2 * R]
    at, Z = Zh * LIVE, 2 * Zh
    tiles = [read_tile(side_ref[...], 2)] + [read_tile(ref[at : at + 16, :], 2) for ref in a[1:]]
    lines = [sum(rows) for rows in zip(*tiles)]
    gain = gain_ref[...]
    for ref in a[1:]:
        pieces = ref[at + 16 : at + 32, :].astype(f32)
        gain = gain + pieces[0:Z] + pieces[Z : 2 * Z]
    for z in range(Z):
        out[z, LIVE:128, :] = split_tile(lines + [gain[z : z + 1]])
    for half, refs in enumerate((a, b)):

        def one(z, _):
            rows = pl.ds(pl.multiple_of(z * LIVE, 16), LIVE)
            total = refs[0][rows, :]
            for ref in refs[1:]:
                total = total + ref[rows, :].astype(f32)
            out[half * Zh + z, 0:LIVE, :] = total.astype(bf16)
            return 0

        lax.fori_loop(0, Zh, one, 0)


def gather_rows(Zh, side, gain, a, b):
    return pl.pallas_call(
        functools.partial(gather_kernel, Zh),
        out_shape=jax.ShapeDtypeStruct((2 * Zh, 128, 128), bf16),
        in_specs=[VMEM] * (2 * R + 2),
        out_specs=VMEM,
        compiler_params=pltpu.CompilerParams(vmem_limit_bytes=SCOPED),
        name="gather_rows",
    )(side, gain, *a, *b)


def prepare_kernel(vocab, hidden_ref, gain_ref, target_ref, start_ref, live_ref, out_ref, meta_ref):
    gain = gain_ref[...]
    high = gain.astype(bf16).astype(f32)
    middle = (gain - high).astype(bf16).astype(f32)
    low = gain - high - middle
    row = lax.broadcasted_iota(jnp.int32, (16, 128), 0)
    tile = jnp.where(row == 0, high, jnp.where(row == 1, middle, jnp.where(row == 2, low, 0.0)))
    for z in range(out_ref.shape[0]):
        out_ref[z, 0:LIVE, :] = hidden_ref[0:LIVE, :]
        out_ref[z, LIVE:128, :] = tile.astype(bf16)
    starts = start_ref[...]
    upto = lax.broadcasted_iota(jnp.int32, (128, 128), 0) <= lax.broadcasted_iota(
        jnp.int32, (128, 128), 1
    )
    flags = jnp.broadcast_to(starts.astype(f32), (16, 128)).astype(bf16)
    order = jnp.dot(flags, upto.astype(f32).astype(bf16), preferred_element_type=f32)
    order = order[0:1].astype(jnp.int32) - 1
    sentinel = vocab - 1 - jnp.clip(order, 0, NSENT - 1)
    label = jnp.where(starts > 0, sentinel, target_ref[...])
    pieces = (label >> 16, (label >> 8) & 255, label & 255, live_ref[...])
    tile = jnp.zeros((16, 128), f32)
    for i, piece in enumerate(pieces):
        tile = jnp.where(row == i, piece.astype(f32), tile)
    meta_ref[...] = tile.astype(bf16)


def prepare(Z, vocab, hidden, norm_gain, targets, span_starts, live_rows):
    line = lambda a: a.reshape(1, 128)
    return pl.pallas_call(
        functools.partial(prepare_kernel, vocab),
        out_shape=(
            jax.ShapeDtypeStruct((Z, 128, 128), bf16),
            jax.ShapeDtypeStruct((16, 128), bf16),
        ),
        in_specs=[VMEM] * 5,
        out_specs=(VMEM, VMEM),
        name="prepare",
    )(hidden, line(norm_gain), line(targets), line(span_starts), line(live_rows))


def meta_kernel(at, w_ref, *refs):
    tiles, a_refs = refs[:R], refs[R : 2 * R]
    label_ref, live_ref, factor_ref, total_ref, gain_ref = refs[2 * R :]
    Z = gain_ref.shape[0] // R
    for k, ref in enumerate(a_refs):
        for z in range(Z):
            pieces = ref[at + z * 16 : at + (z + 1) * 16, :].astype(f32)
            gain_ref[k * Z + z : k * Z + z + 1, :] = pieces[0:1] + pieces[1:2] + pieces[2:3]
    place = lax.broadcasted_iota(jnp.int32, (R, 128), 0)
    labels, live, total = jnp.zeros((R, 128), f32), jnp.zeros((R, 128), f32), jnp.zeros((1, 1), f32)
    for p, j in enumerate(ORDER):
        tile = tiles[j][at : at + 16, :].astype(f32)
        label = tile[0:1] * 65536 + tile[1:2] * 256 + tile[2:3]
        labels = jnp.where(place == p, label, labels)
        live = jnp.where(place == p, tile[3:4], live)
        total = total + jnp.sum(tile[3:4] + tile[4:5], axis=1, keepdims=True)
    label_ref[...] = labels
    live_ref[...] = live
    factor_ref[...] = live * (loss_scale / total)
    total_ref[...] = jnp.broadcast_to(total, (1, 128))


def read_meta(at, weight, Z, blocks, a_blocks):
    line = jax.ShapeDtypeStruct((R, 128), f32)
    return pl.pallas_call(
        functools.partial(meta_kernel, at),
        out_shape=(
            line,
            line,
            line,
            jax.ShapeDtypeStruct((1, 128), f32),
            jax.ShapeDtypeStruct((R * Z, 128), f32),
        ),
        in_specs=[VMEM] * (1 + 2 * R),
        out_specs=(VMEM,) * 5,
        compiler_params=pltpu.CompilerParams(vmem_limit_bytes=SCOPED),
        name="read_meta",
    )(weight, *blocks, *a_blocks)


def outer_kernel(g_ref, h_ref, n_ref, m_ref, out_ref, g_turned, h_turned):
    V = h_ref.shape[1]

    @pl.when(pl.program_id(0) == 0)
    def _():
        g_turned[...] = g_ref[:, 0:V].astype(f32).T.astype(bf16)
        h_turned[...] = h_ref[...].astype(f32).T.astype(bf16)

    total = jnp.dot(g_turned[...], n_ref[...], preferred_element_type=f32)
    total = total + jnp.dot(h_turned[...], m_ref[...], preferred_element_type=f32)
    out_ref[...] = total.astype(bf16)


def outer(g, ours, theirs, D):
    rows, V = g.shape[0], g.shape[1] // 2
    part = pl.BlockSpec((rows, V), lambda i: (0, i))
    return pl.pallas_call(
        outer_kernel,
        grid=(D // V,),
        out_shape=jax.ShapeDtypeStruct((V, D), bf16),
        in_specs=[
            pl.BlockSpec(g.shape, lambda i: (0, 0)),
            pl.BlockSpec((rows, V), lambda i: (0, D // V)),
            part,
            part,
        ],
        out_specs=pl.BlockSpec((V, V), lambda i: (0, i)),
        scratch_shapes=[pltpu.VMEM((V, rows), bf16)] * 2,
        compiler_params=pltpu.CompilerParams(vmem_limit_bytes=SCOPED),
        cost_estimate=pl.CostEstimate(
            flops=4 * rows * V * D, bytes_accessed=8 * V * D, transcendentals=0
        ),
        name="outer",
    )(g, theirs, ours, theirs)


def last_kernel(sums_ref, came_ref, total_ref, gain_ref, loss_ref):
    sums = sums_ref[...] + came_ref[...]
    gain_ref[...] = sums[0:1]
    loss_ref[...] = sums[1:2, 0:1] / total_ref[:, 0:1]


def last(sums, came, total):
    return pl.pallas_call(
        last_kernel,
        out_shape=(jax.ShapeDtypeStruct((1, 128), f32), jax.ShapeDtypeStruct((1, 1), f32)),
        in_specs=[VMEM] * 3,
        out_specs=(VMEM, VMEM),
        name="last",
    )(sums, came, total)


def sums_kernel(loss_ref, total_ref, gain_ref, sums_ref):
    tile = total_ref[0, LIVE:128, :].astype(f32)
    for z in range(1, total_ref.shape[0]):
        tile = tile + total_ref[z, LIVE:128, :].astype(f32)
    _, target, gain = read_tile(tile, 3)
    sums_ref[0:1, :] = gain / gain_ref[...]
    sums_ref[1:2, :] = loss_ref[...] - target


def last_sums(loss, total, norm_gain):
    return pl.pallas_call(
        sums_kernel,
        out_shape=jax.ShapeDtypeStruct((2, 128), f32),
        in_specs=[VMEM] * 3,
        out_specs=VMEM,
        name="last_sums",
    )(loss, total, norm_gain.reshape(1, 128))


def finish_kernel(D, total_ref, hidden_ref, gain_ref, inv_ref, out_ref):
    total = total_ref[0].astype(f32)
    for z in range(1, total_ref.shape[0]):
        total = total + total_ref[z].astype(f32)
    inner = to_column(read_tile(total[LIVE:128], 1)[0])
    total = total[0:LIVE]
    inv = inv_ref[...]
    activation = hidden_ref[0:LIVE, :].astype(f32)
    grad = inv * (total * gain_ref[...]) - activation * (inv * inv * (inner / D))
    out_ref[0:LIVE, :] = grad.astype(bf16)
    out_ref[LIVE:128, :] = jnp.zeros((128 - LIVE, 128), bf16)


def finish(D, total, hidden, norm_gain, inv_rms):
    return pl.pallas_call(
        functools.partial(finish_kernel, D),
        out_shape=jax.ShapeDtypeStruct((128, 128), bf16),
        in_specs=[VMEM] * 4,
        out_specs=VMEM,
        name="finish",
    )(total, hidden, norm_gain.reshape(1, 128), inv_rms)


def body(hidden, norm_gain, head_weight, targets, span_starts, live_rows):
    Z, Y, X = (lax.axis_size(a) for a in "zyx")
    Zh = Z // 2
    V, D = head_weight.shape
    vocab = V * 2 * Z * Y * X
    c, z, y, x = (lax.axis_index(a) for a in "czyx")
    spot = (z * Y + y) * X + x
    first, second = (c * (Z * Y * X) + spot) * V, ((1 - c) * (Z * Y * X) + spot) * V
    place = jnp.stack([y, x, first, second]).astype(jnp.int32)

    live_other = shift(live_rows, "c", 1)
    weight_other = shift(head_weight, "c", 1)

    block, meta = prepare(Z, vocab, hidden, norm_gain, targets, span_starts, live_rows)
    block = lax.all_to_all(block, "z", 0, 0)
    meta = meta + jnp.pad(live_other[None].astype(bf16), ((4, 11), (0, 0)))
    block, weight_other, meta = lax.optimization_barrier((block, weight_other, meta))

    a_block = jnp.concatenate(
        [block[:Zh, :LIVE].reshape(-1, 128), block[:, LIVE:].reshape(-1, 128)]
    )
    b_block = jnp.concatenate([block[Zh:, :LIVE].reshape(-1, 128), meta])
    a_blocks = [a_block] + [shift(a_block, "y", k) for k in range(1, R)]
    b_blocks = [b_block] + [shift(b_block, "x", k) for k in range(1, R)]
    a_all = ring_gather(jnp.concatenate([a[: Zh * LIVE] for a in a_blocks]), "x")
    b_all = ring_gather(jnp.concatenate([b[: Zh * LIVE] for b in b_blocks]), "y")
    labels, live, factor, live_total, gain = read_meta(
        Zh * LIVE, head_weight, Z, b_blocks, a_blocks
    )
    a_all, b_all, labels, live, factor, gain = lax.optimization_barrier(
        (a_all, b_all, labels, live, factor, gain)
    )

    weights = (head_weight, weight_other)
    normed, inv_rms, logits, share = forward(place, Zh, *weights, gain, a_all, b_all)
    every = lax.all_to_all(share, ("z", "y", "x"), 0, 0)
    g, normed, side, loss, gain_far, a_low, a_high, b_low, b_high = soft_rows(
        place, Zh, *weights, every, logits, normed, labels, live, factor
    )

    a_low, a_high = shift(a_low, "x", 1), shift(a_high, "x", -1)
    b_low, b_high = shift(b_low, "y", 1), shift(b_high, "y", -1)
    near = near_rows(place, Zh, *weights, side, g, normed)
    near, a_low, a_high, b_low, b_high, g, normed = lax.optimization_barrier(
        (near, a_low, a_high, b_low, b_high, g, normed)
    )
    theirs = shift(normed, "c", 1)
    a0, a1, a3, b0, b1, b3, gain_near = near
    a_up, a_down, gain = relay(a3, a1, a_low, a_high, gain_far, gain_near)
    b_up, b_down = relay(b1, b3, b_low, b_high)
    a_in = shift(a_up, "x", 1), shift(a_down, "x", -1)
    b_in = shift(b_up, "y", 1), shift(b_down, "y", -1)
    gain_in = shift(gain, "x", 2)
    weight_grad = outer(g, normed, theirs, D)
    a_in, b_in, weight_grad = lax.optimization_barrier((a_in, b_in, weight_grad))
    outs = turn_rows(place, Zh, side, gain, gain_in, (a0, *a_in), (b0, *b_in))
    a_sums = [outs[0]] + [shift(outs[k], "y", k) for k in range(1, R)]
    b_sums = [outs[R]] + [shift(outs[R + k], "x", -k) for k in range(1, R)]
    total = gather_rows(Zh, outs[2 * R], outs[2 * R + 1], a_sums, b_sums)
    total = lax.all_to_all(total, "z", 0, 0)
    sums = last_sums(loss, total, norm_gain)
    came = shift(sums, "c", 1)
    hidden_grad = finish(D, total, hidden, norm_gain, inv_rms)
    came, hidden_grad = lax.optimization_barrier((came, hidden_grad))
    gain_grad, mean_loss = last(sums, came, live_total)
    gain_grad, mean_loss = gain_grad.reshape(128), mean_loss.reshape(())
    return (hidden_grad, gain_grad, weight_grad, mean_loss)


def solution(mesh):
    S, T, X = mesh.devices.shape
    split = Mesh(mesh.devices.reshape(S, T // R, R, X), ("c", "z", "y", "x"))
    rows, features, entries = ("c", "x"), ("z", "y"), ("c", "z", "y", "x")
    return jax.shard_map(
        body,
        mesh=split,
        in_specs=(P(rows, features), P(features), P(entries, None), P(rows), P(rows), P(rows)),
        out_specs=(P(rows, features), P(features), P(entries, None), P()),
        check_vma=False,
    )
```

```python
import functools
import jax
import jax.numpy as jnp
from jax import lax
from jax.experimental import pallas as pl
from jax.experimental.pallas import tpu as pltpu
from jax.sharding import Mesh, PartitionSpec as P

NSENT = 100
LIVE = 112
loss_scale = 8192.0
epsilon = 1e-06
f32, bf16 = jnp.float32, jnp.bfloat16
VMEM = pl.BlockSpec(memory_space=pltpu.VMEM)
SMEM = pl.BlockSpec(memory_space=pltpu.SMEM)
HBM = pl.BlockSpec(memory_space=pltpu.HBM)
R = 4
ORDER = (0, 1, 3, 2)
SCOPED = 16 << 20


def shift(x, axis, k):
    n = lax.axis_size(axis)
    return lax.ppermute(x, axis, [(i, (i + k) % n) for i in range(n)])


def around(x, axis, k):
    n = lax.axis_size(axis)
    pairs = [(c * n + i, c * n + (i + (k, -k)[c]) % n) for c in range(2) for i in range(n)]
    return lax.ppermute(x, ("c", axis), pairs)


def ring_gather(block, axis):
    one = around(block, axis, 1)
    return block, one, around(block, axis, -1), around(one, axis, 1)


PARTS = ((0, 0, 4), (1, 0, 4), (3, 0, 4), (2, 0, 4))


def spot_of(j):
    return jnp.where(j < 2, j, 5 - j)


def same():
    return lax.broadcasted_iota(jnp.int32, (LIVE, 128), 0) == lax.broadcasted_iota(
        jnp.int32, (LIVE, 128), 1
    )


def to_row(column):
    return jnp.sum(jnp.where(same(), column, 0.0), axis=0, keepdims=True)


def to_column(row):
    return jnp.sum(jnp.where(same(), row, 0.0), axis=1, keepdims=True)


def place_of(place_ref, p):
    return lax.rem(place_ref[1] - place_ref[4] * ORDER[p] + R, R)


def forward_kernel(Zh, place_ref, w0_ref, w1_ref, gain_ref, *refs):
    a_refs, b_refs = refs[:R], refs[R : 2 * R]
    n_ref, inv_ref, l_ref, share_ref, w_ref, total_ref, w_sems = refs[2 * R :]
    Z = 2 * Zh
    V = w0_ref.shape[0]
    copies = [
        pltpu.make_async_copy(w, w_ref.at[i], w_sems.at[i]) for i, w in enumerate((w0_ref, w1_ref))
    ]
    for copy in copies:
        copy.start()

    def load(ref, i, z):
        at = pl.multiple_of((i * Zh + z) * LIVE, 16)
        return ref[pl.ds(at, LIVE), :].astype(f32)

    def squares(ref, i):
        def add(z, total):
            block = load(ref, i, z)
            return total + block * block

        return lax.fori_loop(0, Zh, add, jnp.zeros((LIVE, 128), f32), unroll=True)

    total_ref[...] = jnp.zeros_like(total_ref)
    for ref, (j, first, last) in zip(a_refs, PARTS):
        add = lambda i, total, ref=ref: total + squares(ref, i)
        p = ORDER.index(j)
        total_ref[p] = lax.fori_loop(0, last - first, add, total_ref[p])
    for ref, (_, first, last) in zip(b_refs, PARTS):

        def add(i, _, ref=ref, first=first):
            p = spot_of(first + i)
            total_ref[p] = total_ref[p] + squares(ref, i)
            return 0

        lax.fori_loop(0, last - first, add, 0)
    for p in range(R):
        mean_square = jnp.sum(total_ref[p], axis=1, keepdims=True) / (Z * R * 128)
        inv = lax.rsqrt(mean_square + epsilon)
        if p == 0:
            inv_ref[...] = inv
        total_ref[p] = jnp.broadcast_to(inv, (LIVE, 128))

    def scale(ref, i, k, p, half):
        inv = total_ref[p]
        y = lax.rem(place_ref[0] - place_ref[4] * k + R, R)
        rows = pl.ds(pl.multiple_of(p * LIVE, 16), LIVE)

        def one(z, _):
            t = half * Zh + z
            column = pl.multiple_of((t * R + y) * 128, 128)
            n_ref[rows, pl.ds(column, 128)] = (
                load(ref, i, z) * inv * gain_ref[pl.ds(k * Z + t, 1), :]
            ).astype(bf16)
            return 0

        lax.fori_loop(0, Zh, one, 0, unroll=True)

    for ref, (j, first, last) in zip(a_refs, PARTS):

        def one(i, _, ref=ref, j=j, first=first):
            scale(ref, i, first + i, ORDER.index(j), 0)
            return 0

        lax.fori_loop(0, last - first, one, 0)
    for ref, (k, first, last) in zip(b_refs, PARTS):

        def one(i, _, ref=ref, k=k, first=first):
            scale(ref, i, k, spot_of(first + i), 1)
            return 0

        lax.fori_loop(0, last - first, one, 0)

    def logits_of(q, _):
        pltpu.make_async_copy(w0_ref, w_ref.at[q], w_sems.at[q]).wait()
        l_ref[:, pl.ds(pl.multiple_of(q * V, V), V)] = lax.dot_general(
            n_ref[:, 0 : w_ref.shape[2]], w_ref[q], (((1,), (1,)), ((), ())), preferred_element_type=f32
        )
        return 0

    lax.fori_loop(0, 2, logits_of, 0)
    place = lax.broadcasted_iota(jnp.int32, (R, 128), 0)
    share = jnp.zeros((R, 128), f32)
    for p in range(R):
        logits = l_ref[p * LIVE : (p + 1) * LIVE, :]
        top = jnp.max(logits, axis=1, keepdims=True)
        here = top + jnp.log(jnp.sum(jnp.exp(logits - top), axis=1, keepdims=True))
        share = jnp.where(place == place_of(place_ref, p), to_row(here), share)
    share_ref[...] = jnp.broadcast_to(share[None], share_ref.shape)


def forward(place, Zh, w0, w1, gain, a, b):
    V, D = w0.shape
    rows = R * LIVE
    return pl.pallas_call(
        functools.partial(forward_kernel, Zh),
        out_shape=(
            jax.ShapeDtypeStruct((rows, D + V), bf16),
            jax.ShapeDtypeStruct((LIVE, 1), f32),
            jax.ShapeDtypeStruct((rows, 2 * V), f32),
            jax.ShapeDtypeStruct((2 * Zh * R * R, R, 128), f32),
        ),
        in_specs=[SMEM, HBM, HBM] + [VMEM] * (1 + 2 * R),
        out_specs=(VMEM,) * 4,
        scratch_shapes=[
            pltpu.VMEM((2, V, D), bf16),
            pltpu.VMEM((R, LIVE, 128), f32),
            pltpu.SemaphoreType.DMA((2,)),
        ],
        compiler_params=pltpu.CompilerParams(vmem_limit_bytes=28 << 20),
        cost_estimate=pl.CostEstimate(
            flops=4 * rows * V * D, bytes_accessed=4 * V * D, transcendentals=2 * rows * V
        ),
        name="forward",
    )(place, w0, w1, gain, *a, *b)


def split_tile(rows):
    place = lax.broadcasted_iota(jnp.int32, (16, 128), 0)
    tile = jnp.zeros((16, 128), f32)
    for i, row in enumerate(rows):
        for n in range(3):
            piece = row.astype(bf16).astype(f32)
            tile = jnp.where(place == 3 * i + n, piece, tile)
            row = row - piece
    return tile.astype(bf16)


def read_tile(tile, n):
    tile = tile.astype(f32)
    return [tile[3 * i : 3 * i + 1] + tile[3 * i + 1 : 3 * i + 2] + tile[3 * i + 2 : 3 * i + 3] for i in range(n)]


def soft_kernel(Zh, place_ref, w0_ref, w1_ref, every_ref, l_ref, n_ref, label_ref, live_ref, factor_ref, *refs):
    g_ref, ng_ref, side_ref, loss_ref, gain_ref, a_low, a_high, b_low, b_high = refs[:9]
    wa_ref, wb_ref, sems = refs[9:]
    V = w0_ref.shape[0]
    far = lax.rem(place_ref[0] + 2, R)
    copies = []
    for i, w in enumerate((w0_ref, w1_ref)):
        rows = pl.ds(i * V, V)
        copies.append(
            [pltpu.make_async_copy(w.at[:, pl.ds(0, Zh * R * 128)], wa_ref.at[rows], sems.at[0, i])]
        )
        for z in range(Zh):
            column = pl.multiple_of(((Zh + z) * R + far) * 128, 128)
            copies[-1].append(
                pltpu.make_async_copy(
                    w.at[:, pl.ds(column, 128)],
                    wb_ref.at[rows, pl.ds(z * 128, 128)],
                    sems.at[1 + z, i],
                )
            )
    for pair in copies:
        for copy in pair:
            copy.start()
    every = every_ref[...]
    best = jnp.max(every, axis=0)
    log_total = best + jnp.log(jnp.sum(jnp.exp(every - best[None]), axis=0))
    place = lax.broadcasted_iota(jnp.int32, (R, 128), 0)
    lane = lax.broadcasted_iota(jnp.int32, (1, 2 * V), 1)
    entry = jnp.where(lane < V, place_ref[2] + lane, place_ref[3] + lane - V).astype(f32)

    def block(p, sums):
        inner, target, loss = sums
        rows = pl.ds(pl.multiple_of(p * LIVE, 16), LIVE)
        distance = jnp.where(p < 2, p, 5 - p)
        here = lax.rem(place_ref[1] - place_ref[4] * distance + R, R)
        total = jnp.sum(jnp.where(place == here, log_total, 0.0), axis=0, keepdims=True)
        pick_row = lambda ref: jnp.sum(jnp.where(place == p, ref[...], 0.0), axis=0, keepdims=True)
        live = pick_row(live_ref)
        logits = l_ref[rows, :]
        match = to_column(pick_row(label_ref)) == entry
        grad = jnp.exp(logits - to_column(total)) - jnp.where(match, 1.0, 0.0)
        grad = grad * to_column(pick_row(factor_ref))
        g_ref[rows, :] = grad.astype(bf16)
        ng_ref[rows, pl.ds(w0_ref.shape[1], V)] = grad[:, V:].astype(bf16)
        line = to_row(jnp.sum(grad * logits, axis=1, keepdims=True))
        inner = jnp.where(place == p, line, inner)
        own = jnp.sum(jnp.where(match, logits, 0.0), axis=1, keepdims=True) * to_column(live)
        target = target + jnp.sum(own, axis=0, keepdims=True)
        loss = loss + jnp.sum(live * total, axis=1, keepdims=True)
        return inner, target, loss

    zero = jnp.zeros((1, 1), f32)
    inner, target, loss = lax.fori_loop(0, R, block, (jnp.zeros((R, 128), f32), zero, zero))
    for p in range(R):
        side_ref[p] = split_tile([inner[p : p + 1], jnp.broadcast_to(target, (1, 128))])
    loss_ref[...] = jnp.broadcast_to(loss, (1, 128))
    for pair in copies:
        for copy in pair:
            copy.wait()
    half = Zh // 2
    gain_ref[...] = jnp.zeros_like(gain_ref)
    part = jnp.dot(g_ref[(R - 1) * LIVE :, :], wa_ref[...], preferred_element_type=f32)
    gain = part * n_ref[(R - 1) * LIVE :, 0 : Zh * R * 128].astype(f32)
    gain = jnp.sum(gain, axis=0, keepdims=True)
    for t in range(Zh * R):
        at = t % (half * R) * LIVE
        gain_ref[t : t + 1, :] = gain[:, t * 128 : (t + 1) * 128]
        (a_low if t < half * R else a_high)[at : at + LIVE, :] = part[
            :, t * 128 : (t + 1) * 128
        ].astype(bf16)
    part = jnp.dot(g_ref[...], wb_ref[...], preferred_element_type=f32)
    for z in range(Zh):
        at = z % half * R * LIVE
        t = (Zh + z) * R + far
        block = part[:, z * 128 : (z + 1) * 128]
        (b_low if z < half else b_high)[at : at + R * LIVE, :] = block.astype(bf16)
        gain = block * n_ref[:, pl.ds(pl.multiple_of(t * 128, 128), 128)].astype(f32)
        gain_ref[pl.ds(t, 1), :] = jnp.sum(gain, axis=0, keepdims=True)
    a_low[Zh // 2 * R * LIVE :, :] = side_ref[R - 1]


def soft_rows(place, Zh, w0, w1, every, logits, normed, labels, live, factor):
    V = w0.shape[0]
    rows = logits.shape[0]
    half = Zh // 2 * R * LIVE
    shapes = [((rows, 2 * V), bf16), (normed.shape, bf16), ((R, 16, 128), bf16), ((1, 128), f32)]
    shapes += [((2 * Zh * R, 128), f32)]
    shapes += [((half + 16, 128), bf16)] + [((half, 128), bf16)] * 3
    return pl.pallas_call(
        functools.partial(soft_kernel, Zh),
        out_shape=tuple(jax.ShapeDtypeStruct(*shape) for shape in shapes),
        in_specs=[SMEM, HBM, HBM] + [VMEM] * 6,
        out_specs=(VMEM,) * len(shapes),
        scratch_shapes=[
            pltpu.VMEM((2 * V, Zh * R * 128), bf16),
            pltpu.VMEM((2 * V, Zh * 128), bf16),
            pltpu.SemaphoreType.DMA((1 + Zh, 2)),
        ],
        input_output_aliases={5: 1},
        compiler_params=pltpu.CompilerParams(vmem_limit_bytes=20 << 20),
        name="soft_rows",
    )(place, w0, w1, every, logits, normed, labels, live, factor)


def near_kernel(Zh, place_ref, w0_ref, w1_ref, side_ref, g_ref, n_ref, *refs):
    a_refs, b_refs, (gain_ref, wa_ref, wb_ref, sems) = refs[:3], refs[3:6], refs[6:]
    V = w0_ref.shape[0]
    wide = Zh * R * 128
    towards = [lax.rem(place_ref[0] + place_ref[4] * k + R, R) for k in (0, 1, 3)]
    first, second = [], []
    for i, w in enumerate((w0_ref, w1_ref)):
        rows = pl.ds(i * V, V)
        first.append(pltpu.make_async_copy(w.at[:, pl.ds(0, wide)], wa_ref.at[rows], sems.at[0, i]))
        for n in range(3 * Zh):
            column = pl.multiple_of(((Zh + n // 3) * R + towards[n % 3]) * 128, 128)
            second.append(
                pltpu.make_async_copy(
                    w.at[:, pl.ds(column, 128)],
                    wb_ref.at[rows, pl.ds(n * 128, 128)],
                    sems.at[1 + n, i],
                )
            )
    for copy in first + second:
        copy.start()
    gain_ref[...] = jnp.zeros_like(gain_ref)
    for copy in first:
        copy.wait()
    part = jnp.dot(g_ref[0 : 3 * LIVE, :], wa_ref[...], preferred_element_type=f32)
    gain = part * n_ref[0 : 3 * LIVE, 0:wide].astype(f32)
    gain = jnp.sum(gain, axis=0, keepdims=True)
    for t in range(Zh * R):
        lanes = slice(t * 128, (t + 1) * 128)
        gain_ref[t : t + 1, :] = gain[:, lanes]
        for p, ref in enumerate(a_refs):
            ref[t * LIVE : (t + 1) * LIVE, :] = part[p * LIVE : (p + 1) * LIVE, lanes].astype(bf16)
    for p, ref in enumerate(a_refs[1:]):
        ref[Zh * R * LIVE :, :] = side_ref[p + 1]
    for copy in second:
        copy.wait()
    part = jnp.dot(g_ref[...], wb_ref[...], preferred_element_type=f32)
    for n in range(3 * Zh):
        z = n // 3
        t = (Zh + z) * R + towards[n % 3]
        block = part[:, n * 128 : (n + 1) * 128]
        b_refs[n % 3][z * R * LIVE : (z + 1) * R * LIVE, :] = block.astype(bf16)
        gain = block * n_ref[:, pl.ds(pl.multiple_of(t * 128, 128), 128)].astype(f32)
        gain_ref[pl.ds(t, 1), :] = jnp.sum(gain, axis=0, keepdims=True)


def near_rows(place, Zh, w0, w1, side, g, normed):
    V = w0.shape[0]
    rows, block = g.shape[0], Zh * R * LIVE
    shapes = [(block, 128), (block + 16, 128), (block + 16, 128)] + [(block, 128)] * 3
    return pl.pallas_call(
        functools.partial(near_kernel, Zh),
        out_shape=(
            *(jax.ShapeDtypeStruct(shape, bf16) for shape in shapes),
            jax.ShapeDtypeStruct((2 * Zh * R, 128), f32),
        ),
        in_specs=[SMEM, HBM, HBM, VMEM, VMEM, VMEM],
        out_specs=(VMEM,) * 7,
        scratch_shapes=[
            pltpu.VMEM((2 * V, Zh * R * 128), bf16),
            pltpu.VMEM((2 * V, 3 * Zh * 128), bf16),
            pltpu.SemaphoreType.DMA((1 + 3 * Zh, 2)),
        ],
        compiler_params=pltpu.CompilerParams(vmem_limit_bytes=24 << 20),
        name="near_rows",
    )(place, w0, w1, side, g, normed)


def two(value):
    high = value.astype(bf16)
    return high, (value - high.astype(f32)).astype(bf16)


def relay_kernel(up, down, low, high, *refs):
    half, block = high.shape[0], 2 * high.shape[0]
    up_out, down_out = refs[-2:] if len(refs) == 2 else refs[2:4]
    add = lambda a, b: (a.astype(f32) + b.astype(f32)).astype(bf16)
    up_out[0:half, :] = add(up[0:half, :], low[0:half, :])
    up_out[half:block, :] = up[half:block, :]
    down_out[0:half, :] = down[0:half, :]
    down_out[half:block, :] = add(down[half:block, :], high[...])
    if len(refs) > 2:
        mine, came = read_tile(up[block:, :], 2), read_tile(low[half:, :], 2)
        up_out[block : block + 16, :] = split_tile([a + b for a, b in zip(mine, came)])
        down_out[block : block + 16, :] = down[block:, :]
        gain = refs[0][...] + refs[1][...]
        refs[4][...] = gain
        lines = gain.shape[0]
        for i, piece in enumerate(two(gain)):
            for out in (up_out, down_out):
                at = block + 16 + i * lines
                out[at : at + lines, :] = piece


def relay(up, down, low, high, *gains):
    lines = gains[0].shape[0] if gains else 0
    shape = jax.ShapeDtypeStruct((up.shape[0] + 2 * lines, 128), bf16)
    shapes = (shape, shape) + ((jax.ShapeDtypeStruct((lines, 128), f32),) if gains else ())
    return pl.pallas_call(
        relay_kernel,
        out_shape=shapes,
        in_specs=[VMEM] * (4 + len(gains)),
        out_specs=(VMEM,) * len(shapes),
        compiler_params=pltpu.CompilerParams(vmem_limit_bytes=SCOPED),
        name="relay",
    )(up, down, low, high, *gains)


def turn_kernel(Zh, y_ref, side_ref, mine, far, a0, a1, a2, b0, b1, b2, *outs):
    block, part = Zh * R * LIVE, Zh * LIVE

    def one(z, _):
        to = pl.ds(pl.multiple_of(z * LIVE, 16), LIVE)
        for k in range(R):
            row = pl.multiple_of((z * R + lax.rem(y_ref[0] + y_ref[4] * k + R, R)) * LIVE, 16)
            rows = pl.ds(row, LIVE)
            total = a0[rows, :].astype(f32) + a1[rows, :].astype(f32) + a2[rows, :].astype(f32)
            outs[k][to, :] = total.astype(outs[k].dtype)
        for j in range(R):
            rows = pl.ds(pl.multiple_of((z * R + ORDER.index(j)) * LIVE, 16), LIVE)
            total = b0[rows, :].astype(f32) + b1[rows, :].astype(f32) + b2[rows, :].astype(f32)
            outs[R + j][to, :] = total.astype(outs[R + j].dtype)
        return 0

    lax.fori_loop(0, Zh, one, 0)
    tiles = [read_tile(t, 2) for t in (side_ref[0], a1[block : block + 16, :], a2[block : block + 16, :])]
    tile = split_tile([sum(rows) for rows in zip(*tiles)])
    outs[2 * R][...] = tile
    lines, gain_ref = mine.shape[0], outs[2 * R + 2]
    gain = mine[...] + far[...]
    for ref in (a1, a2):
        for i in range(2):
            at = block + 16 + i * lines
            gain = gain + ref[at : at + lines, :].astype(f32)
    gain_ref[...] = gain
    Z = 2 * Zh
    place = lax.broadcasted_iota(jnp.int32, (Z, 128), 0)
    for k in range(R):
        gain = jnp.zeros((Z, 128), f32)
        for z in range(Z):
            line = gain_ref[pl.ds(z * R + lax.rem(y_ref[0] + y_ref[4] * k + R, R), 1), :]
            gain = jnp.where(place == z, line, gain)
        if k == 0:
            outs[2 * R + 1][...] = gain
        else:
            outs[k][part : part + 16, :] = tile
            outs[k][part + 16 : part + 32, :] = jnp.concatenate(
                [piece.astype(f32) for piece in two(gain)]
            ).astype(bf16)


def turn_rows(y, Zh, side, mine, far, a, b):
    part = Zh * LIVE
    shapes = [((part, 128), f32)] + [((part + 32, 128), bf16)] * (R - 1)
    shapes += [((part, 128), f32)] + [((part, 128), bf16)] * (R - 1) + [((16, 128), bf16)]
    shapes += [((2 * Zh, 128), f32)]
    return pl.pallas_call(
        functools.partial(turn_kernel, Zh),
        out_shape=tuple(jax.ShapeDtypeStruct(*shape) for shape in shapes),
        in_specs=[SMEM] + [VMEM] * 9,
        out_specs=(VMEM,) * (2 * R + 2),
        scratch_shapes=[pltpu.VMEM(mine.shape, f32)],
        compiler_params=pltpu.CompilerParams(vmem_limit_bytes=SCOPED),
        name="turn_rows",
    )(y, side, mine, far, *a, *b)


def gather_kernel(Zh, side_ref, gain_ref, *refs):
    a, b, out = refs[:R], refs[R : 2 * R], refs[2 * R]
    at, Z = Zh * LIVE, 2 * Zh
    tiles = [read_tile(side_ref[...], 2)] + [read_tile(ref[at : at + 16, :], 2) for ref in a[1:]]
    lines = [sum(rows) for rows in zip(*tiles)]
    gain = gain_ref[...]
    for ref in a[1:]:
        pieces = ref[at + 16 : at + 32, :].astype(f32)
        gain = gain + pieces[0:Z] + pieces[Z : 2 * Z]
    for z in range(Z):
        out[z, LIVE:128, :] = split_tile(lines + [gain[z : z + 1]])
    for half, refs in enumerate((a, b)):

        def one(z, _):
            rows = pl.ds(pl.multiple_of(z * LIVE, 16), LIVE)
            total = refs[0][rows, :]
            for ref in refs[1:]:
                total = total + ref[rows, :].astype(f32)
            out[half * Zh + z, 0:LIVE, :] = total.astype(bf16)
            return 0

        lax.fori_loop(0, Zh, one, 0)


def gather_rows(Zh, side, gain, a, b):
    return pl.pallas_call(
        functools.partial(gather_kernel, Zh),
        out_shape=jax.ShapeDtypeStruct((2 * Zh, 128, 128), bf16),
        in_specs=[VMEM] * (2 * R + 2),
        out_specs=VMEM,
        compiler_params=pltpu.CompilerParams(vmem_limit_bytes=SCOPED),
        name="gather_rows",
    )(side, gain, *a, *b)


def prepare_kernel(vocab, hidden_ref, gain_ref, target_ref, start_ref, live_ref, out_ref, meta_ref):
    gain = gain_ref[...]
    high = gain.astype(bf16).astype(f32)
    middle = (gain - high).astype(bf16).astype(f32)
    low = gain - high - middle
    row = lax.broadcasted_iota(jnp.int32, (16, 128), 0)
    tile = jnp.where(row == 0, high, jnp.where(row == 1, middle, jnp.where(row == 2, low, 0.0)))
    for z in range(out_ref.shape[0]):
        out_ref[z, 0:LIVE, :] = hidden_ref[0:LIVE, :]
        out_ref[z, LIVE:128, :] = tile.astype(bf16)
    starts = start_ref[...]
    upto = lax.broadcasted_iota(jnp.int32, (128, 128), 0) <= lax.broadcasted_iota(
        jnp.int32, (128, 128), 1
    )
    flags = jnp.broadcast_to(starts.astype(f32), (16, 128)).astype(bf16)
    order = jnp.dot(flags, upto.astype(f32).astype(bf16), preferred_element_type=f32)
    order = order[0:1].astype(jnp.int32) - 1
    sentinel = vocab - 1 - jnp.clip(order, 0, NSENT - 1)
    label = jnp.where(starts > 0, sentinel, target_ref[...])
    pieces = (label >> 16, (label >> 8) & 255, label & 255, live_ref[...])
    tile = jnp.zeros((16, 128), f32)
    for i, piece in enumerate(pieces):
        tile = jnp.where(row == i, piece.astype(f32), tile)
    meta_ref[...] = tile.astype(bf16)


def prepare(Z, vocab, hidden, norm_gain, targets, span_starts, live_rows):
    line = lambda a: a.reshape(1, 128)
    return pl.pallas_call(
        functools.partial(prepare_kernel, vocab),
        out_shape=(
            jax.ShapeDtypeStruct((Z, 128, 128), bf16),
            jax.ShapeDtypeStruct((16, 128), bf16),
        ),
        in_specs=[VMEM] * 5,
        out_specs=(VMEM, VMEM),
        name="prepare",
    )(hidden, line(norm_gain), line(targets), line(span_starts), line(live_rows))


def meta_kernel(at, w_ref, *refs):
    tiles, a_refs = refs[:R], refs[R : 2 * R]
    label_ref, live_ref, factor_ref, total_ref, gain_ref = refs[2 * R :]
    Z = gain_ref.shape[0] // R
    for k, ref in enumerate(a_refs):
        pieces = ref[at:, :].astype(f32)
        for z in range(Z):
            three = [pieces[3 * z + i : 3 * z + i + 1] for i in range(3)]
            gain_ref[k * Z + z : k * Z + z + 1, :] = three[0] + three[1] + three[2]
    place = lax.broadcasted_iota(jnp.int32, (R, 128), 0)
    labels, live, total = jnp.zeros((R, 128), f32), jnp.zeros((R, 128), f32), jnp.zeros((1, 1), f32)
    for p, j in enumerate(ORDER):
        tile = tiles[j][at : at + 16, :].astype(f32)
        label = tile[0:1] * 65536 + tile[1:2] * 256 + tile[2:3]
        labels = jnp.where(place == p, label, labels)
        live = jnp.where(place == p, tile[3:4], live)
        total = total + jnp.sum(tile[3:4] + tile[4:5], axis=1, keepdims=True)
    label_ref[...] = labels
    live_ref[...] = live
    factor_ref[...] = live * (loss_scale / total)
    total_ref[...] = jnp.broadcast_to(total, (1, 128))


def read_meta(at, weight, Z, blocks, a_blocks):
    line = jax.ShapeDtypeStruct((R, 128), f32)
    return pl.pallas_call(
        functools.partial(meta_kernel, at),
        out_shape=(
            line,
            line,
            line,
            jax.ShapeDtypeStruct((1, 128), f32),
            jax.ShapeDtypeStruct((R * Z, 128), f32),
        ),
        in_specs=[VMEM] * (1 + 2 * R),
        out_specs=(VMEM,) * 5,
        compiler_params=pltpu.CompilerParams(vmem_limit_bytes=SCOPED),
        name="read_meta",
    )(weight, *blocks, *a_blocks)


def outer_kernel(g_ref, h_ref, n_ref, m_ref, out_ref, g_turned, h_turned):
    V = h_ref.shape[1]

    @pl.when(pl.program_id(0) == 0)
    def _():
        g_turned[...] = g_ref[:, 0:V].astype(f32).T.astype(bf16)
        h_turned[...] = h_ref[...].astype(f32).T.astype(bf16)

    total = jnp.dot(g_turned[...], n_ref[...], preferred_element_type=f32)
    total = total + jnp.dot(h_turned[...], m_ref[...], preferred_element_type=f32)
    out_ref[...] = total.astype(bf16)


def outer(g, ours, theirs, D):
    rows, V = g.shape[0], g.shape[1] // 2
    part = pl.BlockSpec((rows, V), lambda i: (0, i))
    return pl.pallas_call(
        outer_kernel,
        grid=(D // V,),
        out_shape=jax.ShapeDtypeStruct((V, D), bf16),
        in_specs=[
            pl.BlockSpec(g.shape, lambda i: (0, 0)),
            pl.BlockSpec((rows, V), lambda i: (0, D // V)),
            part,
            part,
        ],
        out_specs=pl.BlockSpec((V, V), lambda i: (0, i)),
        scratch_shapes=[pltpu.VMEM((V, rows), bf16)] * 2,
        compiler_params=pltpu.CompilerParams(vmem_limit_bytes=SCOPED),
        cost_estimate=pl.CostEstimate(
            flops=4 * rows * V * D, bytes_accessed=8 * V * D, transcendentals=0
        ),
        name="outer",
    )(g, theirs, ours, theirs)


def last_kernel(sums_ref, came_ref, total_ref, gain_ref, loss_ref):
    sums = sums_ref[...] + came_ref[...]
    gain_ref[...] = sums[0:1]
    loss_ref[...] = sums[1:2, 0:1] / total_ref[:, 0:1]


def last(sums, came, total):
    return pl.pallas_call(
        last_kernel,
        out_shape=(jax.ShapeDtypeStruct((1, 128), f32), jax.ShapeDtypeStruct((1, 1), f32)),
        in_specs=[VMEM] * 3,
        out_specs=(VMEM, VMEM),
        name="last",
    )(sums, came, total)


def sums_kernel(loss_ref, total_ref, gain_ref, sums_ref):
    tile = total_ref[0, LIVE:128, :].astype(f32)
    for z in range(1, total_ref.shape[0]):
        tile = tile + total_ref[z, LIVE:128, :].astype(f32)
    _, target, gain = read_tile(tile, 3)
    sums_ref[0:1, :] = gain / gain_ref[...]
    sums_ref[1:2, :] = loss_ref[...] - target


def last_sums(loss, total, norm_gain):
    return pl.pallas_call(
        sums_kernel,
        out_shape=jax.ShapeDtypeStruct((2, 128), f32),
        in_specs=[VMEM] * 3,
        out_specs=VMEM,
        name="last_sums",
    )(loss, total, norm_gain.reshape(1, 128))


def finish_kernel(D, total_ref, hidden_ref, gain_ref, inv_ref, out_ref):
    total = total_ref[0].astype(f32)
    for z in range(1, total_ref.shape[0]):
        total = total + total_ref[z].astype(f32)
    inner = to_column(read_tile(total[LIVE:128], 1)[0])
    total = total[0:LIVE]
    inv = inv_ref[...]
    activation = hidden_ref[0:LIVE, :].astype(f32)
    grad = inv * (total * gain_ref[...]) - activation * (inv * inv * (inner / D))
    out_ref[0:LIVE, :] = grad.astype(bf16)
    out_ref[LIVE:128, :] = jnp.zeros((128 - LIVE, 128), bf16)


def finish(D, total, hidden, norm_gain, inv_rms):
    return pl.pallas_call(
        functools.partial(finish_kernel, D),
        out_shape=jax.ShapeDtypeStruct((128, 128), bf16),
        in_specs=[VMEM] * 4,
        out_specs=VMEM,
        name="finish",
    )(total, hidden, norm_gain.reshape(1, 128), inv_rms)


def body(hidden, norm_gain, head_weight, targets, span_starts, live_rows):
    Z, Y, X = (lax.axis_size(a) for a in "zyx")
    Zh = Z // 2
    V, D = head_weight.shape
    vocab = V * 2 * Z * Y * X
    c, z, y, x = (lax.axis_index(a) for a in "czyx")
    spot = (z * Y + y) * X + x
    first, second = (c * (Z * Y * X) + spot) * V, ((1 - c) * (Z * Y * X) + spot) * V
    place = jnp.stack([y, x, first, second, 1 - 2 * c]).astype(jnp.int32)

    live_other = shift(live_rows, "c", 1)
    weight_other = shift(head_weight, "c", 1)

    block, meta = prepare(Z, vocab, hidden, norm_gain, targets, span_starts, live_rows)
    block = lax.all_to_all(block, "z", 0, 0)
    meta = meta + jnp.pad(live_other[None].astype(bf16), ((4, 11), (0, 0)))
    block, weight_other, meta = lax.optimization_barrier((block, weight_other, meta))

    pieces = block[:, LIVE : LIVE + 3].reshape(3 * Z, 128)
    a_block = jnp.concatenate(
        [block[:Zh, :LIVE].reshape(-1, 128), jnp.pad(pieces, ((0, -3 * Z % 16), (0, 0)))]
    )
    b_block = jnp.concatenate([block[Zh:, :LIVE].reshape(-1, 128), meta])
    a_blocks = [a_block] + [around(a_block, "y", k) for k in range(1, R)]
    b_blocks = [b_block] + [around(b_block, "x", k) for k in range(1, R)]
    a_all = ring_gather(jnp.concatenate([a[: Zh * LIVE] for a in a_blocks]), "x")
    b_all = ring_gather(jnp.concatenate([b[: Zh * LIVE] for b in b_blocks]), "y")
    labels, live, factor, live_total, gain = read_meta(
        Zh * LIVE, head_weight, Z, b_blocks, a_blocks
    )
    a_all, b_all, labels, live, factor, gain = lax.optimization_barrier(
        (a_all, b_all, labels, live, factor, gain)
    )

    weights = (head_weight, weight_other)
    normed, inv_rms, logits, share = forward(place, Zh, *weights, gain, a_all, b_all)
    every = lax.all_to_all(share, ("z", "y", "x"), 0, 0)
    g, normed, side, loss, gain_far, a_low, a_high, b_low, b_high = soft_rows(
        place, Zh, *weights, every, logits, normed, labels, live, factor
    )

    a_low, a_high = around(a_low, "x", 1), around(a_high, "x", -1)
    b_low, b_high = around(b_low, "y", 1), around(b_high, "y", -1)
    near = near_rows(place, Zh, *weights, side, g, normed)
    near, a_low, a_high, b_low, b_high, g, normed = lax.optimization_barrier(
        (near, a_low, a_high, b_low, b_high, g, normed)
    )
    theirs = shift(normed, "c", 1)
    a0, a1, a3, b0, b1, b3, gain_near = near
    a_up, a_down, gain = relay(a3, a1, a_low, a_high, gain_far, gain_near)
    b_up, b_down = relay(b1, b3, b_low, b_high)
    a_in = around(a_up, "x", 1), around(a_down, "x", -1)
    b_in = around(b_up, "y", 1), around(b_down, "y", -1)
    gain_in = around(gain, "x", 2)
    weight_grad = outer(g, normed, theirs, D)
    a_in, b_in, weight_grad = lax.optimization_barrier((a_in, b_in, weight_grad))
    outs = turn_rows(place, Zh, side, gain, gain_in, (a0, *a_in), (b0, *b_in))
    a_sums = [outs[0]] + [around(outs[k], "y", k) for k in range(1, R)]
    b_sums = [outs[R]] + [around(outs[R + k], "x", -k) for k in range(1, R)]
    total = gather_rows(Zh, outs[2 * R], outs[2 * R + 1], a_sums, b_sums)
    total = lax.all_to_all(total, "z", 0, 0)
    sums = last_sums(loss, total, norm_gain)
    came = shift(sums, "c", 1)
    hidden_grad = finish(D, total, hidden, norm_gain, inv_rms)
    came, hidden_grad = lax.optimization_barrier((came, hidden_grad))
    gain_grad, mean_loss = last(sums, came, live_total)
    gain_grad, mean_loss = gain_grad.reshape(128), mean_loss.reshape(())
    return (hidden_grad, gain_grad, weight_grad, mean_loss)


def solution(mesh):
    S, T, X = mesh.devices.shape
    split = Mesh(mesh.devices.reshape(S, T // R, R, X), ("c", "z", "y", "x"))
    rows, features, entries = ("c", "x"), ("z", "y"), ("c", "z", "y", "x")
    return jax.shard_map(
        body,
        mesh=split,
        in_specs=(P(rows, features), P(features), P(entries, None), P(rows), P(rows), P(rows)),
        out_specs=(P(rows, features), P(features), P(entries, None), P()),
        check_vma=False,
    )
```

```python
import functools
import jax
import jax.numpy as jnp
from jax import lax
from jax.experimental import pallas as pl
from jax.experimental.pallas import tpu as pltpu
from jax.sharding import Mesh, PartitionSpec as P

NSENT = 100
LIVE = 112
loss_scale = 8192.0
epsilon = 1e-06
f32, bf16 = jnp.float32, jnp.bfloat16
VMEM = pl.BlockSpec(memory_space=pltpu.VMEM)
SMEM = pl.BlockSpec(memory_space=pltpu.SMEM)
HBM = pl.BlockSpec(memory_space=pltpu.HBM)
R = 4
ORDER = (0, 1, 3, 2)
SCOPED = 16 << 20


def shift(x, axis, k):
    n = lax.axis_size(axis)
    return lax.ppermute(x, axis, [(i, (i + k) % n) for i in range(n)])


def around(x, axis, k):
    n = lax.axis_size(axis)
    pairs = [(c * n + i, c * n + (i + (k, -k)[c]) % n) for c in range(2) for i in range(n)]
    return lax.ppermute(x, ("c", axis), pairs)


def ring_gather(block, axis):
    one = around(block, axis, 1)
    return block, one, around(block, axis, -1), around(one, axis, 1)


PARTS = ((0, 0, 4), (1, 0, 4), (3, 0, 4), (2, 0, 4))


def spot_of(j):
    return jnp.where(j < 2, j, 5 - j)


def same():
    return lax.broadcasted_iota(jnp.int32, (LIVE, 128), 0) == lax.broadcasted_iota(
        jnp.int32, (LIVE, 128), 1
    )


def to_row(column):
    return jnp.sum(jnp.where(same(), column, 0.0), axis=0, keepdims=True)


def to_column(row):
    return jnp.sum(jnp.where(same(), row, 0.0), axis=1, keepdims=True)


def place_of(place_ref, p):
    return lax.rem(place_ref[1] - place_ref[4] * ORDER[p] + R, R)


def forward_kernel(Zh, place_ref, w0_ref, w1_ref, gain_ref, *refs):
    a_refs, b_refs = refs[:R], refs[R : 2 * R]
    n_ref, inv_ref, l_ref, share_ref, w_ref, total_ref, w_sems = refs[2 * R :]
    Z = 2 * Zh
    V = w0_ref.shape[0]
    copies = [
        pltpu.make_async_copy(w, w_ref.at[i], w_sems.at[i]) for i, w in enumerate((w0_ref, w1_ref))
    ]
    for copy in copies:
        copy.start()

    def load(ref, i, z):
        at = pl.multiple_of((i * Zh + z) * LIVE, 16)
        return ref[pl.ds(at, LIVE), :].astype(f32)

    def squares(ref, i):
        def add(z, total):
            block = load(ref, i, z)
            return total + block * block

        return lax.fori_loop(0, Zh, add, jnp.zeros((LIVE, 128), f32), unroll=True)

    total_ref[...] = jnp.zeros_like(total_ref)
    for ref, (j, first, last) in zip(a_refs, PARTS):
        add = lambda i, total, ref=ref: total + squares(ref, i)
        p = ORDER.index(j)
        total_ref[p] = lax.fori_loop(0, last - first, add, total_ref[p])
    for ref, (_, first, last) in zip(b_refs, PARTS):

        def add(i, _, ref=ref, first=first):
            p = spot_of(first + i)
            total_ref[p] = total_ref[p] + squares(ref, i)
            return 0

        lax.fori_loop(0, last - first, add, 0)
    for p in range(R):
        mean_square = jnp.sum(total_ref[p], axis=1, keepdims=True) / (Z * R * 128)
        inv = lax.rsqrt(mean_square + epsilon)
        if p == 0:
            inv_ref[...] = inv
        total_ref[p] = jnp.broadcast_to(inv, (LIVE, 128))

    def scale(ref, i, k, p, half):
        inv = total_ref[p]
        y = lax.rem(place_ref[0] - place_ref[4] * k + R, R)
        rows = pl.ds(pl.multiple_of(p * LIVE, 16), LIVE)

        def one(z, _):
            t = half * Zh + z
            column = pl.multiple_of((t * R + y) * 128, 128)
            n_ref[rows, pl.ds(column, 128)] = (
                load(ref, i, z) * inv * gain_ref[pl.ds(k * Z + t, 1), :]
            ).astype(bf16)
            return 0

        lax.fori_loop(0, Zh, one, 0, unroll=True)

    for ref, (j, first, last) in zip(a_refs, PARTS):

        def one(i, _, ref=ref, j=j, first=first):
            scale(ref, i, first + i, ORDER.index(j), 0)
            return 0

        lax.fori_loop(0, last - first, one, 0)
    for ref, (k, first, last) in zip(b_refs, PARTS):

        def one(i, _, ref=ref, k=k, first=first):
            scale(ref, i, k, spot_of(first + i), 1)
            return 0

        lax.fori_loop(0, last - first, one, 0)

    def logits_of(q, _):
        pltpu.make_async_copy(w0_ref, w_ref.at[q], w_sems.at[q]).wait()
        l_ref[:, pl.ds(pl.multiple_of(q * V, V), V)] = lax.dot_general(
            n_ref[:, 0 : w_ref.shape[2]], w_ref[q], (((1,), (1,)), ((), ())), preferred_element_type=f32
        )
        return 0

    lax.fori_loop(0, 2, logits_of, 0)
    place = lax.broadcasted_iota(jnp.int32, (R, 128), 0)
    share = jnp.zeros((R, 128), f32)
    for p in range(R):
        logits = l_ref[p * LIVE : (p + 1) * LIVE, :]
        top = jnp.max(logits, axis=1, keepdims=True)
        here = top + jnp.log(jnp.sum(jnp.exp(logits - top), axis=1, keepdims=True))
        share = jnp.where(place == place_of(place_ref, p), to_row(here), share)
    share_ref[...] = jnp.broadcast_to(share[None], share_ref.shape)


def forward(place, Zh, w0, w1, gain, a, b):
    V, D = w0.shape
    rows = R * LIVE
    return pl.pallas_call(
        functools.partial(forward_kernel, Zh),
        out_shape=(
            jax.ShapeDtypeStruct((rows, D + V), bf16),
            jax.ShapeDtypeStruct((LIVE, 1), f32),
            jax.ShapeDtypeStruct((rows, 2 * V), f32),
            jax.ShapeDtypeStruct((2 * Zh * R * R, R, 128), f32),
        ),
        in_specs=[SMEM, HBM, HBM] + [VMEM] * (1 + 2 * R),
        out_specs=(VMEM,) * 4,
        scratch_shapes=[
            pltpu.VMEM((2, V, D), bf16),
            pltpu.VMEM((R, LIVE, 128), f32),
            pltpu.SemaphoreType.DMA((2,)),
        ],
        compiler_params=pltpu.CompilerParams(vmem_limit_bytes=28 << 20),
        cost_estimate=pl.CostEstimate(
            flops=4 * rows * V * D, bytes_accessed=4 * V * D, transcendentals=2 * rows * V
        ),
        name="forward",
    )(place, w0, w1, gain, *a, *b)


def split_tile(rows):
    place = lax.broadcasted_iota(jnp.int32, (16, 128), 0)
    tile = jnp.zeros((16, 128), f32)
    for i, row in enumerate(rows):
        for n in range(3):
            piece = row.astype(bf16).astype(f32)
            tile = jnp.where(place == 3 * i + n, piece, tile)
            row = row - piece
    return tile.astype(bf16)


def read_tile(tile, n):
    tile = tile.astype(f32)
    return [tile[3 * i : 3 * i + 1] + tile[3 * i + 1 : 3 * i + 2] + tile[3 * i + 2 : 3 * i + 3] for i in range(n)]


def soft_kernel(Zh, place_ref, w0_ref, w1_ref, every_ref, l_ref, n_ref, label_ref, live_ref, factor_ref, *refs):
    g_ref, ng_ref, side_ref, loss_ref, gain_ref, a_far, b_far, wa_ref, wb_ref, sems = refs
    V = w0_ref.shape[0]
    far = lax.rem(place_ref[0] + 2, R)
    copies = []
    for i, w in enumerate((w0_ref, w1_ref)):
        rows = pl.ds(i * V, V)
        copies.append(
            [pltpu.make_async_copy(w.at[:, pl.ds(0, Zh * R * 128)], wa_ref.at[rows], sems.at[0, i])]
        )
        for z in range(Zh):
            column = pl.multiple_of(((Zh + z) * R + far) * 128, 128)
            copies[-1].append(
                pltpu.make_async_copy(
                    w.at[:, pl.ds(column, 128)],
                    wb_ref.at[rows, pl.ds(z * 128, 128)],
                    sems.at[1 + z, i],
                )
            )
    for pair in copies:
        for copy in pair:
            copy.start()
    every = every_ref[...]
    best = jnp.max(every, axis=0)
    log_total = best + jnp.log(jnp.sum(jnp.exp(every - best[None]), axis=0))
    place = lax.broadcasted_iota(jnp.int32, (R, 128), 0)
    lane = lax.broadcasted_iota(jnp.int32, (1, 2 * V), 1)
    entry = jnp.where(lane < V, place_ref[2] + lane, place_ref[3] + lane - V).astype(f32)

    def block(p, sums):
        inner, target, loss = sums
        rows = pl.ds(pl.multiple_of(p * LIVE, 16), LIVE)
        distance = jnp.where(p < 2, p, 5 - p)
        here = lax.rem(place_ref[1] - place_ref[4] * distance + R, R)
        total = jnp.sum(jnp.where(place == here, log_total, 0.0), axis=0, keepdims=True)
        pick_row = lambda ref: jnp.sum(jnp.where(place == p, ref[...], 0.0), axis=0, keepdims=True)
        live = pick_row(live_ref)
        logits = l_ref[rows, :]
        match = to_column(pick_row(label_ref)) == entry
        grad = jnp.exp(logits - to_column(total)) - jnp.where(match, 1.0, 0.0)
        grad = grad * to_column(pick_row(factor_ref))
        g_ref[rows, :] = grad.astype(bf16)
        ng_ref[rows, pl.ds(w0_ref.shape[1], V)] = grad[:, V:].astype(bf16)
        line = to_row(jnp.sum(grad * logits, axis=1, keepdims=True))
        inner = jnp.where(place == p, line, inner)
        own = jnp.sum(jnp.where(match, logits, 0.0), axis=1, keepdims=True) * to_column(live)
        target = target + jnp.sum(own, axis=0, keepdims=True)
        loss = loss + jnp.sum(live * total, axis=1, keepdims=True)
        return inner, target, loss

    zero = jnp.zeros((1, 1), f32)
    inner, target, loss = lax.fori_loop(0, R, block, (jnp.zeros((R, 128), f32), zero, zero))
    for p in range(R):
        side_ref[p] = split_tile([inner[p : p + 1], jnp.broadcast_to(target, (1, 128))])
    loss_ref[...] = jnp.broadcast_to(loss, (1, 128))
    for pair in copies:
        for copy in pair:
            copy.wait()
    gain_ref[...] = jnp.zeros_like(gain_ref)
    part = jnp.dot(g_ref[(R - 1) * LIVE :, :], wa_ref[...], preferred_element_type=f32)
    gain = part * n_ref[(R - 1) * LIVE :, 0 : Zh * R * 128].astype(f32)
    gain = jnp.sum(gain, axis=0, keepdims=True)
    for t in range(Zh * R):
        gain_ref[t : t + 1, :] = gain[:, t * 128 : (t + 1) * 128]
        a_far[t * LIVE : (t + 1) * LIVE, :] = part[:, t * 128 : (t + 1) * 128].astype(bf16)
    part = jnp.dot(g_ref[...], wb_ref[...], preferred_element_type=f32)
    for z in range(Zh):
        at = z * R * LIVE
        t = (Zh + z) * R + far
        block = part[:, z * 128 : (z + 1) * 128]
        b_far[at : at + R * LIVE, :] = block.astype(bf16)
        gain = block * n_ref[:, pl.ds(pl.multiple_of(t * 128, 128), 128)].astype(f32)
        gain_ref[pl.ds(t, 1), :] = jnp.sum(gain, axis=0, keepdims=True)
    a_far[Zh * R * LIVE :, :] = side_ref[R - 1]


def soft_rows(place, Zh, w0, w1, every, logits, normed, labels, live, factor):
    V = w0.shape[0]
    rows = logits.shape[0]
    block = Zh * R * LIVE
    shapes = [((rows, 2 * V), bf16), (normed.shape, bf16), ((R, 16, 128), bf16), ((1, 128), f32)]
    shapes += [((2 * Zh * R, 128), f32)]
    shapes += [((block + 16, 128), bf16), ((block, 128), bf16)]
    return pl.pallas_call(
        functools.partial(soft_kernel, Zh),
        out_shape=tuple(jax.ShapeDtypeStruct(*shape) for shape in shapes),
        in_specs=[SMEM, HBM, HBM] + [VMEM] * 6,
        out_specs=(VMEM,) * len(shapes),
        scratch_shapes=[
            pltpu.VMEM((2 * V, Zh * R * 128), bf16),
            pltpu.VMEM((2 * V, Zh * 128), bf16),
            pltpu.SemaphoreType.DMA((1 + Zh, 2)),
        ],
        input_output_aliases={5: 1},
        compiler_params=pltpu.CompilerParams(vmem_limit_bytes=20 << 20),
        name="soft_rows",
    )(place, w0, w1, every, logits, normed, labels, live, factor)


def near_kernel(Zh, place_ref, w0_ref, w1_ref, side_ref, g_ref, n_ref, *refs):
    a_refs, b_refs, (gain_ref, wa_ref, wb_ref, sems) = refs[:3], refs[3:6], refs[6:]
    V = w0_ref.shape[0]
    wide = Zh * R * 128
    towards = [lax.rem(place_ref[0] + place_ref[4] * k + R, R) for k in (0, 1, 3)]
    first, second = [], []
    for i, w in enumerate((w0_ref, w1_ref)):
        rows = pl.ds(i * V, V)
        first.append(pltpu.make_async_copy(w.at[:, pl.ds(0, wide)], wa_ref.at[rows], sems.at[0, i]))
        for n in range(3 * Zh):
            column = pl.multiple_of(((Zh + n // 3) * R + towards[n % 3]) * 128, 128)
            second.append(
                pltpu.make_async_copy(
                    w.at[:, pl.ds(column, 128)],
                    wb_ref.at[rows, pl.ds(n * 128, 128)],
                    sems.at[1 + n, i],
                )
            )
    for copy in first + second:
        copy.start()
    gain_ref[...] = jnp.zeros_like(gain_ref)
    for copy in first:
        copy.wait()
    part = jnp.dot(g_ref[0 : 3 * LIVE, :], wa_ref[...], preferred_element_type=f32)
    gain = part * n_ref[0 : 3 * LIVE, 0:wide].astype(f32)
    gain = jnp.sum(gain, axis=0, keepdims=True)
    for t in range(Zh * R):
        lanes = slice(t * 128, (t + 1) * 128)
        gain_ref[t : t + 1, :] = gain[:, lanes]
        for p, ref in enumerate(a_refs):
            ref[t * LIVE : (t + 1) * LIVE, :] = part[p * LIVE : (p + 1) * LIVE, lanes].astype(bf16)
    for p, ref in enumerate(a_refs[1:]):
        ref[Zh * R * LIVE :, :] = side_ref[p + 1]
    for copy in second:
        copy.wait()
    part = jnp.dot(g_ref[...], wb_ref[...], preferred_element_type=f32)
    for n in range(3 * Zh):
        z = n // 3
        t = (Zh + z) * R + towards[n % 3]
        block = part[:, n * 128 : (n + 1) * 128]
        b_refs[n % 3][z * R * LIVE : (z + 1) * R * LIVE, :] = block.astype(bf16)
        gain = block * n_ref[:, pl.ds(pl.multiple_of(t * 128, 128), 128)].astype(f32)
        gain_ref[pl.ds(t, 1), :] = jnp.sum(gain, axis=0, keepdims=True)


def near_rows(place, Zh, w0, w1, side, g, normed):
    V = w0.shape[0]
    rows, block = g.shape[0], Zh * R * LIVE
    shapes = [(block, 128), (block + 16, 128), (block + 16, 128)] + [(block, 128)] * 3
    return pl.pallas_call(
        functools.partial(near_kernel, Zh),
        out_shape=(
            *(jax.ShapeDtypeStruct(shape, bf16) for shape in shapes),
            jax.ShapeDtypeStruct((2 * Zh * R, 128), f32),
        ),
        in_specs=[SMEM, HBM, HBM, VMEM, VMEM, VMEM],
        out_specs=(VMEM,) * 7,
        scratch_shapes=[
            pltpu.VMEM((2 * V, Zh * R * 128), bf16),
            pltpu.VMEM((2 * V, 3 * Zh * 128), bf16),
            pltpu.SemaphoreType.DMA((1 + 3 * Zh, 2)),
        ],
        compiler_params=pltpu.CompilerParams(vmem_limit_bytes=24 << 20),
        name="near_rows",
    )(place, w0, w1, side, g, normed)


def two(value):
    high = value.astype(bf16)
    return high, (value - high.astype(f32)).astype(bf16)


def relay_kernel(a_up, a_down, a_far, gain_0, gain_1, b_up, b_far, a_out, down_out, b_out, gain_out):
    block = b_up.shape[0]
    add = lambda a, b: (a[0:block, :].astype(f32) + b[0:block, :].astype(f32)).astype(bf16)
    a_out[0:block, :] = add(a_up, a_far)
    b_out[...] = add(b_up, b_far)
    mine, came = (read_tile(ref[block:, :], 2) for ref in (a_up, a_far))
    a_out[block : block + 16, :] = split_tile([a + b for a, b in zip(mine, came)])
    down_out[0 : block + 16, :] = a_down[...]
    gain = gain_0[...] + gain_1[...]
    gain_out[...] = gain
    lines = gain.shape[0]
    for i, piece in enumerate(two(gain)):
        at = block + 16 + i * lines
        a_out[at : at + lines, :] = piece
        down_out[at : at + lines, :] = piece


def relay(a_up, a_down, a_far, gain_0, gain_1, b_up, b_far):
    lines = gain_0.shape[0]
    long = (a_up.shape[0] + 2 * lines, 128)
    shapes = [(long, bf16), (long, bf16), (b_up.shape, bf16), (gain_0.shape, f32)]
    return pl.pallas_call(
        relay_kernel,
        out_shape=tuple(jax.ShapeDtypeStruct(*shape) for shape in shapes),
        in_specs=[VMEM] * 7,
        out_specs=(VMEM,) * 4,
        compiler_params=pltpu.CompilerParams(vmem_limit_bytes=SCOPED),
        name="relay",
    )(a_up, a_down, a_far, gain_0, gain_1, b_up, b_far)


def turn_kernel(Zh, y_ref, side_ref, mine, far, a0, a1, a2, b0, b1, b2, *outs):
    block, part = Zh * R * LIVE, Zh * LIVE

    def one(z, _):
        to = pl.ds(pl.multiple_of(z * LIVE, 16), LIVE)
        for k in range(R):
            row = pl.multiple_of((z * R + lax.rem(y_ref[0] + y_ref[4] * k + R, R)) * LIVE, 16)
            rows = pl.ds(row, LIVE)
            total = a0[rows, :].astype(f32) + a1[rows, :].astype(f32) + a2[rows, :].astype(f32)
            outs[k][to, :] = total.astype(outs[k].dtype)
        for j in range(R):
            rows = pl.ds(pl.multiple_of((z * R + ORDER.index(j)) * LIVE, 16), LIVE)
            total = b0[rows, :].astype(f32) + b1[rows, :].astype(f32) + b2[rows, :].astype(f32)
            outs[R + j][to, :] = total.astype(outs[R + j].dtype)
        return 0

    lax.fori_loop(0, Zh, one, 0)
    tiles = [read_tile(t, 2) for t in (side_ref[0], a1[block : block + 16, :], a2[block : block + 16, :])]
    tile = split_tile([sum(rows) for rows in zip(*tiles)])
    outs[2 * R][...] = tile
    lines, gain_ref = mine.shape[0], outs[2 * R + 2]
    gain = mine[...] + far[...]
    for ref in (a1, a2):
        for i in range(2):
            at = block + 16 + i * lines
            gain = gain + ref[at : at + lines, :].astype(f32)
    gain_ref[...] = gain
    Z = 2 * Zh
    place = lax.broadcasted_iota(jnp.int32, (Z, 128), 0)
    for k in range(R):
        gain = jnp.zeros((Z, 128), f32)
        for z in range(Z):
            line = gain_ref[pl.ds(z * R + lax.rem(y_ref[0] + y_ref[4] * k + R, R), 1), :]
            gain = jnp.where(place == z, line, gain)
        if k == 0:
            outs[2 * R + 1][...] = gain
        else:
            outs[k][part : part + 16, :] = tile
            outs[k][part + 16 : part + 32, :] = jnp.concatenate(
                [piece.astype(f32) for piece in two(gain)]
            ).astype(bf16)


def turn_rows(y, Zh, side, mine, far, a, b):
    part = Zh * LIVE
    shapes = [((part, 128), f32)] + [((part + 32, 128), bf16)] * (R - 1)
    shapes += [((part, 128), f32)] + [((part, 128), bf16)] * (R - 1) + [((16, 128), bf16)]
    shapes += [((2 * Zh, 128), f32)]
    return pl.pallas_call(
        functools.partial(turn_kernel, Zh),
        out_shape=tuple(jax.ShapeDtypeStruct(*shape) for shape in shapes),
        in_specs=[SMEM] + [VMEM] * 9,
        out_specs=(VMEM,) * (2 * R + 2),
        scratch_shapes=[pltpu.VMEM(mine.shape, f32)],
        compiler_params=pltpu.CompilerParams(vmem_limit_bytes=SCOPED),
        name="turn_rows",
    )(y, side, mine, far, *a, *b)


def gather_kernel(Zh, side_ref, gain_ref, *refs):
    a, b, out = refs[:R], refs[R : 2 * R], refs[2 * R]
    at, Z = Zh * LIVE, 2 * Zh
    tiles = [read_tile(side_ref[...], 2)] + [read_tile(ref[at : at + 16, :], 2) for ref in a[1:]]
    lines = [sum(rows) for rows in zip(*tiles)]
    gain = gain_ref[...]
    for ref in a[1:]:
        pieces = ref[at + 16 : at + 32, :].astype(f32)
        gain = gain + pieces[0:Z] + pieces[Z : 2 * Z]
    for z in range(Z):
        out[z, LIVE:128, :] = split_tile(lines + [gain[z : z + 1]])
    for half, refs in enumerate((a, b)):

        def one(z, _):
            rows = pl.ds(pl.multiple_of(z * LIVE, 16), LIVE)
            total = refs[0][rows, :]
            for ref in refs[1:]:
                total = total + ref[rows, :].astype(f32)
            out[half * Zh + z, 0:LIVE, :] = total.astype(bf16)
            return 0

        lax.fori_loop(0, Zh, one, 0)


def gather_rows(Zh, side, gain, a, b):
    return pl.pallas_call(
        functools.partial(gather_kernel, Zh),
        out_shape=jax.ShapeDtypeStruct((2 * Zh, 128, 128), bf16),
        in_specs=[VMEM] * (2 * R + 2),
        out_specs=VMEM,
        compiler_params=pltpu.CompilerParams(vmem_limit_bytes=SCOPED),
        name="gather_rows",
    )(side, gain, *a, *b)


def prepare_kernel(vocab, hidden_ref, gain_ref, target_ref, start_ref, live_ref, out_ref, meta_ref):
    gain = gain_ref[...]
    high = gain.astype(bf16).astype(f32)
    middle = (gain - high).astype(bf16).astype(f32)
    low = gain - high - middle
    row = lax.broadcasted_iota(jnp.int32, (16, 128), 0)
    tile = jnp.where(row == 0, high, jnp.where(row == 1, middle, jnp.where(row == 2, low, 0.0)))
    for z in range(out_ref.shape[0]):
        out_ref[z, 0:LIVE, :] = hidden_ref[0:LIVE, :]
        out_ref[z, LIVE:128, :] = tile.astype(bf16)
    starts = start_ref[...]
    upto = lax.broadcasted_iota(jnp.int32, (128, 128), 0) <= lax.broadcasted_iota(
        jnp.int32, (128, 128), 1
    )
    flags = jnp.broadcast_to(starts.astype(f32), (16, 128)).astype(bf16)
    order = jnp.dot(flags, upto.astype(f32).astype(bf16), preferred_element_type=f32)
    order = order[0:1].astype(jnp.int32) - 1
    sentinel = vocab - 1 - jnp.clip(order, 0, NSENT - 1)
    label = jnp.where(starts > 0, sentinel, target_ref[...])
    pieces = (label >> 16, (label >> 8) & 255, label & 255, live_ref[...])
    tile = jnp.zeros((16, 128), f32)
    for i, piece in enumerate(pieces):
        tile = jnp.where(row == i, piece.astype(f32), tile)
    meta_ref[...] = tile.astype(bf16)


def prepare(Z, vocab, hidden, norm_gain, targets, span_starts, live_rows):
    line = lambda a: a.reshape(1, 128)
    return pl.pallas_call(
        functools.partial(prepare_kernel, vocab),
        out_shape=(
            jax.ShapeDtypeStruct((Z, 128, 128), bf16),
            jax.ShapeDtypeStruct((16, 128), bf16),
        ),
        in_specs=[VMEM] * 5,
        out_specs=(VMEM, VMEM),
        name="prepare",
    )(hidden, line(norm_gain), line(targets), line(span_starts), line(live_rows))


def meta_kernel(at, w_ref, *refs):
    tiles, a_refs = refs[:R], refs[R : 2 * R]
    label_ref, live_ref, factor_ref, total_ref, gain_ref = refs[2 * R :]
    Z = gain_ref.shape[0] // R
    for k, ref in enumerate(a_refs):
        pieces = ref[at:, :].astype(f32)
        for z in range(Z):
            three = [pieces[3 * z + i : 3 * z + i + 1] for i in range(3)]
            gain_ref[k * Z + z : k * Z + z + 1, :] = three[0] + three[1] + three[2]
    place = lax.broadcasted_iota(jnp.int32, (R, 128), 0)
    labels, live, total = jnp.zeros((R, 128), f32), jnp.zeros((R, 128), f32), jnp.zeros((1, 1), f32)
    for p, j in enumerate(ORDER):
        tile = tiles[j][at : at + 16, :].astype(f32)
        label = tile[0:1] * 65536 + tile[1:2] * 256 + tile[2:3]
        labels = jnp.where(place == p, label, labels)
        live = jnp.where(place == p, tile[3:4], live)
        total = total + jnp.sum(tile[3:4] + tile[4:5], axis=1, keepdims=True)
    label_ref[...] = labels
    live_ref[...] = live
    factor_ref[...] = live * (loss_scale / total)
    total_ref[...] = jnp.broadcast_to(total, (1, 128))


def read_meta(at, weight, Z, blocks, a_blocks):
    line = jax.ShapeDtypeStruct((R, 128), f32)
    return pl.pallas_call(
        functools.partial(meta_kernel, at),
        out_shape=(
            line,
            line,
            line,
            jax.ShapeDtypeStruct((1, 128), f32),
            jax.ShapeDtypeStruct((R * Z, 128), f32),
        ),
        in_specs=[VMEM] * (1 + 2 * R),
        out_specs=(VMEM,) * 5,
        compiler_params=pltpu.CompilerParams(vmem_limit_bytes=SCOPED),
        name="read_meta",
    )(weight, *blocks, *a_blocks)


def outer_kernel(g_ref, h_ref, n_ref, m_ref, out_ref, g_turned, h_turned):
    V = h_ref.shape[1]

    @pl.when(pl.program_id(0) == 0)
    def _():
        g_turned[...] = g_ref[:, 0:V].astype(f32).T.astype(bf16)
        h_turned[...] = h_ref[...].astype(f32).T.astype(bf16)

    total = jnp.dot(g_turned[...], n_ref[...], preferred_element_type=f32)
    total = total + jnp.dot(h_turned[...], m_ref[...], preferred_element_type=f32)
    out_ref[...] = total.astype(bf16)


def outer(g, ours, theirs, D):
    rows, V = g.shape[0], g.shape[1] // 2
    part = pl.BlockSpec((rows, V), lambda i: (0, i))
    return pl.pallas_call(
        outer_kernel,
        grid=(D // V,),
        out_shape=jax.ShapeDtypeStruct((V, D), bf16),
        in_specs=[
            pl.BlockSpec(g.shape, lambda i: (0, 0)),
            pl.BlockSpec((rows, V), lambda i: (0, D // V)),
            part,
            part,
        ],
        out_specs=pl.BlockSpec((V, V), lambda i: (0, i)),
        scratch_shapes=[pltpu.VMEM((V, rows), bf16)] * 2,
        compiler_params=pltpu.CompilerParams(vmem_limit_bytes=SCOPED),
        cost_estimate=pl.CostEstimate(
            flops=4 * rows * V * D, bytes_accessed=8 * V * D, transcendentals=0
        ),
        name="outer",
    )(g, theirs, ours, theirs)


def last_kernel(sums_ref, came_ref, total_ref, gain_ref, loss_ref):
    sums = sums_ref[...] + came_ref[...]
    gain_ref[...] = sums[0:1]
    loss_ref[...] = sums[1:2, 0:1] / total_ref[:, 0:1]


def last(sums, came, total):
    return pl.pallas_call(
        last_kernel,
        out_shape=(jax.ShapeDtypeStruct((1, 128), f32), jax.ShapeDtypeStruct((1, 1), f32)),
        in_specs=[VMEM] * 3,
        out_specs=(VMEM, VMEM),
        name="last",
    )(sums, came, total)


def sums_kernel(loss_ref, total_ref, gain_ref, sums_ref):
    tile = total_ref[0, LIVE:128, :].astype(f32)
    for z in range(1, total_ref.shape[0]):
        tile = tile + total_ref[z, LIVE:128, :].astype(f32)
    _, target, gain = read_tile(tile, 3)
    sums_ref[0:1, :] = gain / gain_ref[...]
    sums_ref[1:2, :] = loss_ref[...] - target


def last_sums(loss, total, norm_gain):
    return pl.pallas_call(
        sums_kernel,
        out_shape=jax.ShapeDtypeStruct((2, 128), f32),
        in_specs=[VMEM] * 3,
        out_specs=VMEM,
        name="last_sums",
    )(loss, total, norm_gain.reshape(1, 128))


def finish_kernel(D, total_ref, hidden_ref, gain_ref, inv_ref, out_ref):
    total = total_ref[0].astype(f32)
    for z in range(1, total_ref.shape[0]):
        total = total + total_ref[z].astype(f32)
    inner = to_column(read_tile(total[LIVE:128], 1)[0])
    total = total[0:LIVE]
    inv = inv_ref[...]
    activation = hidden_ref[0:LIVE, :].astype(f32)
    grad = inv * (total * gain_ref[...]) - activation * (inv * inv * (inner / D))
    out_ref[0:LIVE, :] = grad.astype(bf16)
    out_ref[LIVE:128, :] = jnp.zeros((128 - LIVE, 128), bf16)


def finish(D, total, hidden, norm_gain, inv_rms):
    return pl.pallas_call(
        functools.partial(finish_kernel, D),
        out_shape=jax.ShapeDtypeStruct((128, 128), bf16),
        in_specs=[VMEM] * 4,
        out_specs=VMEM,
        name="finish",
    )(total, hidden, norm_gain.reshape(1, 128), inv_rms)


def body(hidden, norm_gain, head_weight, targets, span_starts, live_rows):
    Z, Y, X = (lax.axis_size(a) for a in "zyx")
    Zh = Z // 2
    V, D = head_weight.shape
    vocab = V * 2 * Z * Y * X
    c, z, y, x = (lax.axis_index(a) for a in "czyx")
    spot = (z * Y + y) * X + x
    first, second = (c * (Z * Y * X) + spot) * V, ((1 - c) * (Z * Y * X) + spot) * V
    place = jnp.stack([y, x, first, second, 1 - 2 * c]).astype(jnp.int32)

    live_other = shift(live_rows, "c", 1)
    weight_other = shift(head_weight, "c", 1)

    block, meta = prepare(Z, vocab, hidden, norm_gain, targets, span_starts, live_rows)
    block = lax.all_to_all(block, "z", 0, 0)
    meta = meta + jnp.pad(live_other[None].astype(bf16), ((4, 11), (0, 0)))
    block, weight_other, meta = lax.optimization_barrier((block, weight_other, meta))

    pieces = block[:, LIVE : LIVE + 3].reshape(3 * Z, 128)
    a_block = jnp.concatenate(
        [block[:Zh, :LIVE].reshape(-1, 128), jnp.pad(pieces, ((0, -3 * Z % 16), (0, 0)))]
    )
    b_block = jnp.concatenate([block[Zh:, :LIVE].reshape(-1, 128), meta])
    a_blocks = [a_block] + [around(a_block, "y", k) for k in range(1, R)]
    b_blocks = [b_block] + [around(b_block, "x", k) for k in range(1, R)]
    a_all = ring_gather(jnp.concatenate([a[: Zh * LIVE] for a in a_blocks]), "x")
    b_all = ring_gather(jnp.concatenate([b[: Zh * LIVE] for b in b_blocks]), "y")
    labels, live, factor, live_total, gain = read_meta(
        Zh * LIVE, head_weight, Z, b_blocks, a_blocks
    )
    a_all, b_all, labels, live, factor, gain = lax.optimization_barrier(
        (a_all, b_all, labels, live, factor, gain)
    )

    weights = (head_weight, weight_other)
    normed, inv_rms, logits, share = forward(place, Zh, *weights, gain, a_all, b_all)
    every = lax.all_to_all(share, ("z", "y", "x"), 0, 0)
    g, normed, side, loss, gain_far, a_far, b_far = soft_rows(
        place, Zh, *weights, every, logits, normed, labels, live, factor
    )

    a_far, b_far = around(a_far, "x", 1), around(b_far, "y", 1)
    near = near_rows(place, Zh, *weights, side, g, normed)
    near, a_far, b_far, g, normed = lax.optimization_barrier((near, a_far, b_far, g, normed))
    theirs = shift(normed, "c", 1)
    a0, a1, a3, b0, b1, b3, gain_near = near
    a_up, a_down, b_up, gain = relay(a3, a1, a_far, gain_far, gain_near, b1, b_far)
    a_in = around(a_up, "x", 1), around(a_down, "x", -1)
    b_in = around(b_up, "y", 1), around(b3, "y", -1)
    gain_in = around(gain, "x", 2)
    weight_grad = outer(g, normed, theirs, D)
    a_in, b_in, weight_grad = lax.optimization_barrier((a_in, b_in, weight_grad))
    outs = turn_rows(place, Zh, side, gain, gain_in, (a0, *a_in), (b0, *b_in))
    a_sums = [outs[0]] + [around(outs[k], "y", k) for k in range(1, R)]
    b_sums = [outs[R]] + [around(outs[R + k], "x", -k) for k in range(1, R)]
    total = gather_rows(Zh, outs[2 * R], outs[2 * R + 1], a_sums, b_sums)
    total = lax.all_to_all(total, "z", 0, 0)
    sums = last_sums(loss, total, norm_gain)
    came = shift(sums, "c", 1)
    hidden_grad = finish(D, total, hidden, norm_gain, inv_rms)
    came, hidden_grad = lax.optimization_barrier((came, hidden_grad))
    gain_grad, mean_loss = last(sums, came, live_total)
    gain_grad, mean_loss = gain_grad.reshape(128), mean_loss.reshape(())
    return (hidden_grad, gain_grad, weight_grad, mean_loss)


def solution(mesh):
    S, T, X = mesh.devices.shape
    split = Mesh(mesh.devices.reshape(S, T // R, R, X), ("c", "z", "y", "x"))
    rows, features, entries = ("c", "x"), ("z", "y"), ("c", "z", "y", "x")
    return jax.shard_map(
        body,
        mesh=split,
        in_specs=(P(rows, features), P(features), P(entries, None), P(rows), P(rows), P(rows)),
        out_specs=(P(rows, features), P(features), P(entries, None), P()),
        check_vma=False,
    )
```
